256 devices in a mesh: cuts: 8 (over z_hi, core), seq: 32 (over z_lo, x, y).
Axes of the slice: x: 4, y: 4, z: 8 (z_hi: 4, z_lo: 2; z = z_hi * 2 + z_lo), core: 2. Of those that a mesh axis runs over, the one named last changes fastest.
Arguments:
- query_feat: bfloat16 [8, 512, 4096], P('cuts', None, 'seq'), may hold values from -6 to 6
- key_feat: bfloat16 [8, 512, 4096], P('cuts', None, 'seq'), may hold values from -6 to 6
- value_feat: bfloat16 [8, 512, 4096], P('cuts', None, 'seq'), may hold values from -6 to 6
- upstream: bfloat16 [8, 4096, 8192], P('cuts', 'seq'), may hold values from -1.5 to 1.5
- out_weight: bfloat16 [512, 8192], P('seq'), may hold values from -0.25 to 0.25
- residues: float32 [512, 16], P('seq'), may hold values from -0.06 to 0.06
- decay_rates: float32 [512, 16], P('seq'), may hold values from 0.00048828125 to 0.05
Outputs:
- query_grad: bfloat16 [8, 512, 4096], P('cuts', None, 'seq')
- key_grad: bfloat16 [8, 512, 4096], P('cuts', None, 'seq')
- value_grad: bfloat16 [8, 512, 4096], P('cuts', None, 'seq')
- weight_grad: float32 [512, 8192], P('seq')
- residue_grad: float32 [512, 16], P('seq')
- rate_grad: float32 [512, 16], P('seq')
The draws below stay inside these ranges and needn't reach their ends.
All inputs are finite; a program needn't handle non-finite values.
Results may differ from the reference program's by a relative error of at most 0.005.
Values may be sent and summed in bfloat16 or wider, within the bound.
A program may use at most 128 MiB of HBM per device.

```python
import math
import jax
import jax.numpy as jnp
from jax import lax

D = 8192
CH = 512
MODES = 16
SEQ_LEN = 4096
SEQS = 8


def block_scale(rng, shape, shards, low, high):
    level = 1.0
    for axis_at, blocks in shards:
        heights = jax.random.uniform(jax.random.fold_in(jax.random.fold_in(rng, 6), axis_at), (blocks,), jnp.float32, low / len(shards), high / len(shards))
        level = level * jnp.repeat(jnp.exp(heights), shape[axis_at] // blocks).reshape((-1,) + (1,) * (len(shape) - 1 - axis_at))
    return level


def normal_values(stream_key, dims, width, bound, cuts=(), held_as=jnp.bfloat16):
    loudness = block_scale(stream_key, dims, cuts, -0.22, 0.18) if cuts else 1.0
    values = jax.random.normal(stream_key, dims, jnp.float32) * width * loudness
    return jnp.minimum(jnp.maximum(values, -bound), bound).astype(held_as)


def setup_inputs(seed: int = 0) -> dict:
    splits = jax.random.split(jax.random.key(seed), 8)
    query_feat = normal_values(splits[0], (SEQS, CH, SEQ_LEN), 1.0, 6.0, ((0, 8), (2, 32)))
    key_feat = normal_values(splits[1], (SEQS, CH, SEQ_LEN), 1.0, 6.0, ((0, 8), (2, 32)))
    value_feat = normal_values(splits[2], (SEQS, CH, SEQ_LEN), 1.0, 6.0, ((0, 8), (2, 32)))
    upstream = normal_values(splits[3], (SEQS, SEQ_LEN, D), 0.25, 1.5, ((0, 8), (1, 32)))
    out_weight = normal_values(splits[4], (CH, D), CH ** -0.5, 0.25, ((0, 32),))
    residues = normal_values(splits[5], (CH, MODES), 0.01, 0.06, ((0, 32),), jnp.float32)
    decay_rates = jnp.clip(jnp.exp(math.log(0.05) - 4.6288867 * jax.random.uniform(splits[6], (CH, MODES), jnp.float32) ** block_scale(splits[6], (CH, MODES), ((0, 32),), -0.2, 0.2)), 0.00048828125, 0.05)
    return {"query_feat": query_feat, "key_feat": key_feat, "value_feat": value_feat, "upstream": upstream, "out_weight": out_weight, "residues": residues, "decay_rates": decay_rates}


def reference(query_feat, key_feat, value_feat, upstream, out_weight, residues, decay_rates):
    length = query_feat.shape[2]
    padded = 2 * length
    positions = jnp.arange(length).astype(jnp.float32)
    fading = jnp.exp(-decay_rates[:, :, None] * positions)
    impulse = jnp.einsum('cm,cml->cl', residues, fading, precision=lax.Precision.HIGHEST)
    spec_filter = jnp.fft.rfft(impulse, n=padded)

    def one_sequence(carry, inputs):
        filter_acc, weight_acc = carry
        query_seq, key_seq, value_seq, upstream_seq = inputs
        query_f = query_seq.astype(jnp.float32)
        key_f = key_seq.astype(jnp.float32)
        value_f = value_seq.astype(jnp.float32)
        product = key_f * value_f
        spec_prod = jnp.fft.rfft(product, n=padded)
        smooth = jnp.fft.irfft(spec_filter * spec_prod, n=padded)[:, :length]
        conv_out = (query_f * smooth).astype(jnp.bfloat16)
        back_proj = jnp.dot(out_weight, upstream_seq.T, preferred_element_type=jnp.float32).astype(jnp.bfloat16)
        back_f = back_proj.astype(jnp.float32)
        inner_grad = back_f * query_f
        query_grad = (back_f * smooth).astype(jnp.bfloat16)
        spec_inner = jnp.fft.rfft(inner_grad, n=padded)
        prod_grad = jnp.fft.irfft(jnp.conj(spec_filter) * spec_inner, n=padded)[:, :length]
        key_grad = (prod_grad * value_f).astype(jnp.bfloat16)
        value_grad = (prod_grad * key_f).astype(jnp.bfloat16)
        filter_acc = filter_acc + jnp.fft.irfft(jnp.conj(spec_prod) * spec_inner, n=padded)[:, :length]
        weight_acc = weight_acc + jnp.dot(conv_out, upstream_seq, preferred_element_type=jnp.float32)
        return (filter_acc, weight_acc), (query_grad, key_grad, value_grad)

    start_acc = (jnp.zeros((query_feat.shape[1], length), jnp.float32), jnp.zeros(out_weight.shape, jnp.float32))
    (filter_acc, weight_acc), (query_grad, key_grad, value_grad) = lax.scan(
        one_sequence, start_acc, (query_feat, key_feat, value_feat, upstream))
    residue_grad = jnp.einsum('cl,cml->cm', filter_acc, fading, precision=lax.Precision.HIGHEST)
    rate_grad = -decay_rates * residues * jnp.einsum('cl,cml->cm', filter_acc * positions, fading, precision=lax.Precision.HIGHEST)
    return query_grad, key_grad, value_grad, weight_acc, residue_grad, rate_grad
```

```python
import jax
import jax.numpy as jnp
from jax import lax
from jax.experimental import pallas as pl
from jax.experimental.pallas import tpu as pltpu
from jax.sharding import PartitionSpec as P

MESH = pl.DeviceIdType.MESH
F32 = jnp.float32
BF16 = jnp.bfloat16
NX, NY, NZ, NH = 4, 4, 2, 4
CH, LEN, WIDTH, HALF = 512, 128, 8192, 4096
MODES, SUB, NSUB = 16, 16, 8
QUART = HALF // NH

GATHER = (
    (("x", "y", "z"), 0, 1280),
    (("y", "x", "z"), 1280, 1280),
    (("z", "x", "y"), 2560, 768),
    (("z", "y", "x"), 3328, 768),
)
REDUCE = (
    (("z", "x", "y"), 0, 1280),
    (("z", "y", "x"), 1280, 1280),
    (("x", "y", "z"), 2560, 768),
    (("y", "x", "z"), 3328, 768),
)
N_SEMS = 160


def reduce_buffers():
    shapes = []
    for order, _, cols in REDUCE:
        size = {"z": NZ, "x": NX, "y": NY}
        for dim in order:
            size[dim] = 1
            slab = (size["z"], size["x"], size["y"], 16, cols)
            shapes.append([slab] * (1 if dim == "z" else 3))
    return shapes


def kernel(
    q_ref, k_ref, v_ref, up_ref, w_ref, res_ref, dec_ref,
    qg_ref, kg_ref, vg_ref, wg_ref, resg_ref, rateg_ref,
    wbuf, terms, upb, bp_own, bp_sib, bp_in, pblk, par, upad, gbuf, hpad, hrev,
    e1, e1d, re2, re3, ls, lds, st, std, lgs, lgds, yb, smooth,
    sty, stg, gty, gtg, conv_own, conv_sib, fgt, fgy, fgs, fgg, fgz, fsib, fgall,
    quart_in, fin, fin_sib, *rest,
):
    n_red = sum(len(b) for b in reduce_buffers())
    red_refs = list(rest[:n_red])
    send_sem, recv_sem, local_sem = rest[n_red:]
    cuts, seq = lax.axis_index("cuts"), lax.axis_index("seq")
    core, zh = cuts % 2, cuts // 2
    zl, x, y = seq // 16, (seq // 4) % 4, seq % 4
    z = zh * 2 + zl

    def dev(z_, x_, y_, c_):
        return {"cuts": (z_ // 2) * 2 + c_, "seq": (z_ % 2) * 16 + x_ * 4 + y_}

    xs = [(x + d) % 4 for d in range(4)]
    ys = [(y + d) % 4 for d in range(4)]
    sib = dev(z, x, y, 1 - core)
    zpair = zh * 2 + (1 - zl)
    ymates = [dev(z, x, ys[d], core) for d in (1, 2, 3)]
    gmates = []
    for dz in (0, 1):
        for dx in range(4):
            if dz or dx:
                zz = zpair if dz else z
                gmates.append((zz % 2, xs[dx], dev(zz, xs[dx], y, core)))
    hmates = [((zh + d) % 4, dev(((zh + d) % 4) * 2 + zl, x, y, core)) for d in (1, 2, 3)]
    z_plus, z_minus = (z + 1) % 8, (z + 7) % 8
    near = {
        "x": (dev(z, xs[1], y, core), dev(z, xs[3], y, core)),
        "y": (dev(z, x, ys[1], core), dev(z, x, ys[3], core)),
        "z": (dev(z_plus, x, y, core), dev(z_minus, x, y, core)),
    }
    zfar = z_minus + z_plus - zpair
    partners = [sib] + ymates + [g[2] for g in gmates] + [h[1] for h in hmates] + [dev(zfar, x, y, core)]

    copies = []

    def send(src, dst, to):
        i = len(copies)
        c = pltpu.make_async_remote_copy(
            src_ref=src, dst_ref=dst, send_sem=send_sem.at[i], recv_sem=recv_sem.at[i],
            device_id=to, device_id_type=MESH,
        )
        c.start()
        copies.append(c)
        return c

    mine = pl.ds(pl.multiple_of(core * HALF, HALF), HALF)
    theirs = pl.ds(pl.multiple_of((1 - core) * HALF, HALF), HALF)
    lc_w = pltpu.make_async_copy(w_ref.at[:, mine], wbuf.at[zl, x, y], local_sem.at[0])
    lc_w.start()
    lc_up = pltpu.make_async_copy(up_ref.at[0, :, mine], upb.at[pl.ds(0, LEN)], local_sem.at[1])
    lc_up.start()

    barrier = pltpu.get_barrier_semaphore()
    for d in partners:
        pl.semaphore_signal(barrier, inc=1, device_id=d, device_id_type=MESH)
    pblk[zl, x, y] = jnp.zeros((16, 128), F32)
    pblk[zl, x, y, :, 0:16] = res_ref[...]
    pblk[zl, x, y, :, 16:32] = dec_ref[...]
    pl.semaphore_wait(barrier, len(partners))

    coord = {"z": zl, "x": x, "y": y}
    around = {"x": xs, "y": ys}
    full = {"z": pl.ds(0, NZ), "x": pl.ds(0, NX), "y": pl.ds(0, NY)}

    def gather(order, col, cols):
        held = {d: pl.ds(coord[d], 1) for d in "zxy"}
        half = cols // 2

        def at(first, count, **other):
            s = {**held, **other}
            return wbuf.at[s["z"], s["x"], s["y"], :, pl.ds(first, count)]

        for dim in order:
            plus, minus = near[dim]
            if dim == "z":
                r0, r1 = at(col, half), at(col + half, half)
                a, b = send(r0, r0, plus), send(r1, r1, minus)
                yield
                a.wait_recv()
                b.wait_recv()
            else:
                r = at(col, cols)
                a, b = send(r, r, plus), send(r, r, minus)
                yield
                a.wait_recv()
                r0 = at(col, half, **{dim: pl.ds(around[dim][3], 1)})
                c = send(r0, r0, plus)
                b.wait_recv()
                r1 = at(col + half, half, **{dim: pl.ds(around[dim][1], 1)})
                d = send(r1, r1, minus)
                yield
                c.wait_recv()
                d.wait_recv()
            held[dim] = full[dim]

    def add_into(dst, srcs):
        na, nb, nc = dst.shape[:3]

        def body(i, carry):
            ia, ib, ic = i // (nb * nc), (i // nc) % nb, i % nc
            total = dst[ia, ib, ic].astype(F32)
            for s in srcs:
                total = total + s[ia, ib, ic].astype(F32)
            dst[ia, ib, ic] = total.astype(BF16)
            return carry

        lax.fori_loop(0, na * nb * nc, body, 0)

    def reduce(order, col, cols, bufs):
        left = dict(full)
        half = cols // 2

        def at(first, count, **other):
            s = {**left, **other}
            return terms.at[s["z"], s["x"], s["y"], :, pl.ds(first, count)]

        def part(ref, first, count):
            return ref.at[:, :, :, :, pl.ds(first, count)]

        for dim, buf in zip(order, bufs):
            plus, minus = near[dim]
            if dim == "z":
                (land,) = buf
                out = pl.ds(1 - zl, 1)
                a = send(at(col, half, z=out), part(land, 0, half), plus)
                b = send(at(col + half, half, z=out), part(land, half, half), minus)
                left["z"] = pl.ds(zl, 1)
                yield
                a.wait_recv()
                b.wait_recv()
                add_into(at(col, cols), [land])
            else:
                far_in, from_minus, from_plus = buf
                pos = around[dim]
                far = pl.ds(pos[2], 1)
                a = send(at(col, half, **{dim: far}), part(far_in, 0, half), plus)
                b = send(at(col + half, half, **{dim: far}), part(far_in, half, half), minus)
                yield
                a.wait_recv()
                to_plus = {dim: pl.ds(pos[1], 1)}
                add_into(at(col, half, **to_plus), [part(far_in, 0, half)])
                c = send(at(col, cols, **to_plus), from_minus, plus)
                b.wait_recv()
                to_minus = {dim: pl.ds(pos[3], 1)}
                add_into(at(col + half, half, **to_minus), [part(far_in, half, half)])
                d = send(at(col, cols, **to_minus), from_plus, minus)
                left[dim] = pl.ds(coord[dim], 1)
                yield
                c.wait_recv()
                d.wait_recv()
                add_into(at(col, cols), [from_minus, from_plus])

    def step(gens):
        for g in gens:
            next(g, None)

    def lanes(body):
        def run(i, carry):
            body(pl.ds(pl.multiple_of(i * 128, 128), 128))
            return carry

        lax.fori_loop(0, CH // 128, run, 0)

    par_y = [send(pblk.at[zl, x, y], pblk.at[zl, x, y], d) for d in ymates]
    up_sib = send(up_ref.at[0, :, theirs], upb.at[pl.ds(LEN, LEN)], sib)
    lc_w.wait()
    gathers = [gather(*g) for g in GATHER]
    step(gathers)

    upad[:, 0:SUB, :] = jnp.zeros((NSUB, SUB, CH), F32)
    upad[:, SUB : 2 * SUB, :] = (k_ref[0].astype(F32) * v_ref[0].astype(F32)).T.reshape(NSUB, SUB, CH)

    for c in par_y:
        c.wait_recv()
    par_g = [send(pblk.at[zl, x], pblk.at[zl, x], g[2]) for g in gmates]
    step(gathers)
    for c in par_g:
        c.wait_recv()
    par[...] = pblk[...].reshape(CH, 128).T[0:32]

    def tables(ln):
        r, rate = par[0:16, ln], par[16:32, ln]
        row = lax.broadcasted_iota(jnp.int32, (16, 128), 0).astype(F32)
        for i in range(SUB + 1):
            e = jnp.exp(-rate * float(i))
            e1[16 * i : 16 * i + 16, ln] = e
            e1d[16 * i : 16 * i + 16, ln] = e * float(i)
        h = jnp.zeros((16, 128), F32)
        hr = jnp.zeros((16, 128), F32)
        for m in range(MODES):
            rm, dm = r[m : m + 1], rate[m : m + 1]
            fwd = rm * jnp.exp(-dm * row)
            re2[16 * m : 16 * m + 16, ln] = fwd
            re3[16 * m : 16 * m + 16, ln] = rm * jnp.exp(-dm * (16.0 - row))
            h = h + fwd
            hr = hr + rm * jnp.exp(-dm * (15.0 - row))
        hpad[0:16, ln] = jnp.zeros((16, 128), F32)
        hpad[16:32, ln] = h
        hrev[0:16, ln] = hr
        hrev[16:32, ln] = jnp.zeros((16, 128), F32)

    lanes(tables)

    def product_states(ln):
        for s0 in range(0, NSUB, 4):
            a = [jnp.zeros((16, 128), F32) for _ in range(4)]
            b = [jnp.zeros((16, 128), F32) for _ in range(4)]
            for i in range(SUB):
                lo = 16 * (SUB - i)
                e, ed = e1[lo : lo + 16, ln], e1d[lo : lo + 16, ln]
                for j in range(4):
                    u = upad[s0 + j, SUB + i : SUB + i + 1, ln]
                    a[j] = a[j] + e * u
                    b[j] = b[j] + ed * u
            for j in range(4):
                ls[16 * (s0 + j) : 16 * (s0 + j) + 16, ln] = a[j]
                lds[16 * (s0 + j) : 16 * (s0 + j) + 16, ln] = b[j]

    lanes(product_states)

    def forward(ln, s, ds_, keep):
        decay = e1[16 * SUB : 16 * SUB + 16, ln]
        for i in range(NSUB):
            if keep:
                st[16 * i : 16 * i + 16, ln] = s
                std[16 * i : 16 * i + 16, ln] = ds_
            ds_ = decay * (ds_ + float(SUB) * s) + lds[16 * i : 16 * i + 16, ln]
            s = decay * s + ls[16 * i : 16 * i + 16, ln]
        return s, ds_

    def whole_states(ln):
        s, ds_ = forward(ln, jnp.zeros((16, 128), F32), jnp.zeros((16, 128), F32), False)
        sty[y, 0:16, ln] = s
        sty[y, 16:32, ln] = ds_

    lanes(whole_states)
    sts_y = [send(sty.at[y], sty.at[y], d) for d in ymates]
    step(gathers)

    def local_smooth(ln):
        for s0 in range(0, NSUB, 4):
            acc = [jnp.zeros((16, 128), F32) for _ in range(4)]
            for i in range(SUB):
                t = hpad[16 - i : 32 - i, ln]
                for j in range(4):
                    acc[j] = acc[j] + t * upad[s0 + j, SUB + i : SUB + i + 1, ln]
            for j in range(4):
                yb[16 * (s0 + j) : 16 * (s0 + j) + 16, ln] = acc[j]

    lanes(local_smooth)
    for c in sts_y:
        c.wait_recv()
    g_own = zl * 4 + x

    def chain_forward(rate, count, length, read, here):
        decay = jnp.exp(-rate * float(length))
        zero = jnp.zeros((16, 128), F32)
        s, ds_, cs, cds = zero, zero, zero, zero
        for i in range(count):
            cs = jnp.where(here == i, s, cs)
            cds = jnp.where(here == i, ds_, cds)
            add, addd = read(i)
            ds_ = decay * (ds_ + float(length) * s) + addd
            s = decay * s + add
        return s, ds_, cs, cds

    def group_states(ln):
        s, ds_, _, _ = chain_forward(par[16:32, ln], NY, LEN, lambda i: (sty[i, 0:16, ln], sty[i, 16:32, ln]), y)
        stg[g_own, 0:16, ln] = s
        stg[g_own, 16:32, ln] = ds_

    lanes(group_states)
    sts_g = [send(stg.at[g_own], stg.at[g_own], g[2]) for g in gmates]
    step(gathers)
    for c in sts_g:
        c.wait_recv()

    yf = y.astype(F32) * float(LEN)

    def start_states(ln):
        rate = par[16:32, ln]
        _, _, cs, cds = chain_forward(rate, NY, LEN, lambda i: (sty[i, 0:16, ln], sty[i, 16:32, ln]), y)
        _, _, gs, gds = chain_forward(
            rate, NZ * NX, NY * LEN, lambda i: (stg[i, 0:16, ln], stg[i, 16:32, ln]), g_own
        )
        move = jnp.exp(-rate * yf)
        forward(ln, cs + move * gs, cds + move * (gds + yf * gs), True)

    lanes(start_states)

    def far_smooth(ln):
        for s0 in range(0, NSUB, 4):
            acc = [yb[16 * (s0 + j) : 16 * (s0 + j) + 16, ln] for j in range(4)]
            for m in range(MODES):
                t = re2[16 * m : 16 * m + 16, ln]
                for j in range(4):
                    at = 16 * (s0 + j) + m
                    acc[j] = acc[j] + t * st[at : at + 1, ln]
            for j in range(4):
                yb[16 * (s0 + j) : 16 * (s0 + j) + 16, ln] = acc[j]

    lanes(far_smooth)
    smooth[...] = yb[...].T
    conv_own[...] = (q_ref[0].astype(F32) * smooth[...]).astype(BF16)
    conv_sib_copy = send(conv_own, conv_sib, sib)
    step(gathers)
    lc_up.wait()
    up_sib.wait_recv()
    conv_sib_copy.wait_recv()

    both = jnp.concatenate([conv_own[...], conv_sib[...]], axis=1)
    reduces = []
    at_buf = 0
    for (order, col, cols), shapes in zip(REDUCE, [reduce_buffers()[3 * i : 3 * i + 3] for i in range(len(REDUCE))]):
        bufs = []
        for group in shapes:
            bufs.append(red_refs[at_buf : at_buf + len(group)])
            at_buf += len(group)

        def tile(i, carry, col=col):
            c = pl.ds(pl.multiple_of(col + i * 256, 256), 256)
            t = jnp.dot(both, upb[:, c], preferred_element_type=F32)
            terms[:, :, :, :, c] = t.astype(BF16).reshape(NZ, NX, NY, 16, 256)
            return carry

        lax.fori_loop(0, cols // 256, tile, 0)
        g = reduce(order, col, cols, bufs)
        next(g, None)
        reduces.append(g)

    for _ in range(4):
        step(gathers)

    bp_own[...] = jnp.zeros((CH, LEN), F32)
    bp_sib[...] = jnp.zeros((CH, LEN), F32)

    def proj(i, carry):
        c = pl.ds(pl.multiple_of(i * 512, 512), 512)
        t = lax.dot_general(
            wbuf[:, :, :, :, c].reshape(CH, 512), upb[:, c], (((1,), (1,)), ((), ())), preferred_element_type=F32
        )
        bp_own[...] += t[:, 0:LEN]
        bp_sib[...] += t[:, LEN:]
        return carry

    lax.fori_loop(0, HALF // 512, proj, 0)
    bp_copy = send(bp_sib, bp_in, sib)
    step(reduces)
    bp_copy.wait_recv()
    back = (bp_own[...] + bp_in[...]).astype(BF16).astype(F32)
    qg_ref[0] = (back * smooth[...]).astype(BF16)
    gbuf[...] = (back * q_ref[0].astype(F32)).T

    def grad_states(ln):
        for s0 in range(0, NSUB, 4):
            a = [jnp.zeros((16, 128), F32) for _ in range(4)]
            b = [jnp.zeros((16, 128), F32) for _ in range(4)]
            for i in range(SUB):
                e, ed = e1[16 * i : 16 * i + 16, ln], e1d[16 * i : 16 * i + 16, ln]
                for j in range(4):
                    at = 16 * (s0 + j) + i
                    g = gbuf[at : at + 1, ln]
                    a[j] = a[j] + e * g
                    b[j] = b[j] + ed * g
            for j in range(4):
                lgs[16 * (s0 + j) : 16 * (s0 + j) + 16, ln] = a[j]
                lgds[16 * (s0 + j) : 16 * (s0 + j) + 16, ln] = b[j]

    lanes(grad_states)

    def whole_grad(ln):
        decay = e1[16 * SUB : 16 * SUB + 16, ln]
        b = jnp.zeros((16, 128), F32)
        for i in reversed(range(NSUB)):
            b = decay * b + lgs[16 * i : 16 * i + 16, ln]
        gty[y, :, ln] = b

    lanes(whole_grad)
    gts_y = [send(gty.at[y], gty.at[y], d) for d in ymates]
    step(reduces)

    fgall[32:128, :] = jnp.zeros((96, CH), F32)

    def filter_grads(ln):
        a = jnp.zeros((16, 128), F32)
        b = jnp.zeros((16, 128), F32)
        for i in range(NSUB):
            at = slice(16 * i, 16 * i + 16)
            lg, s = lgs[at, ln], st[at, ln]
            a = a + lg * s
            b = b + lgds[at, ln] * s + lg * std[at, ln]
        for j in range(SUB):
            acc = jnp.zeros((16, 128), F32)
            for i in range(NSUB):
                acc = acc + gbuf[16 * i : 16 * i + 16, ln] * upad[i, 16 - j : 32 - j, ln]
            f = jnp.sum(acc, axis=0, keepdims=True)
            a = a + f * e1[16 * j : 16 * j + 16, ln]
            b = b + f * e1d[16 * j : 16 * j + 16, ln]
        fgall[0:16, ln] = a
        fgall[16:32, ln] = -par[16:32, ln] * par[0:16, ln] * b

    lanes(filter_grads)
    fgt[...] = fgall[...].T.reshape(NZ, NX, NY, 16, 128)
    fg_y = [
        send(fgt.at[:, :, ys[d]], fgy.at[y], ymates[d - 1]) for d in (1, 2, 3)
    ]

    def local_grad(ln):
        for s0 in range(0, NSUB, 4):
            acc = [jnp.zeros((16, 128), F32) for _ in range(4)]
            for i in range(SUB):
                t = hrev[15 - i : 31 - i, ln]
                for j in range(4):
                    at = 16 * (s0 + j) + i
                    acc[j] = acc[j] + t * gbuf[at : at + 1, ln]
            for j in range(4):
                yb[16 * (s0 + j) : 16 * (s0 + j) + 16, ln] = acc[j]

    lanes(local_grad)
    for c in gts_y:
        c.wait_recv()

    def chain_back(rate, count, length, read, here):
        decay = jnp.exp(-rate * float(length))
        b = jnp.zeros((16, 128), F32)
        cb = b
        for i in reversed(range(count)):
            cb = jnp.where(here == i, b, cb)
            b = decay * b + read(i)
        return b, cb

    def group_grad(ln):
        b, _ = chain_back(par[16:32, ln], NY, LEN, lambda i: gty[i, :, ln], y)
        gtg[g_own, :, ln] = b

    lanes(group_grad)
    gts_g = [send(gtg.at[g_own], gtg.at[g_own], g[2]) for g in gmates]
    step(reduces)
    for c in fg_y:
        c.wait_recv()
    fgy[y] = fgt[:, :, y]
    fgs[...] = fgy[0] + fgy[1] + fgy[2] + fgy[3]
    fg_g = [send(fgs.at[g[0], g[1]], fgg.at[g_own], g[2]) for g in gmates]
    for c in gts_g:
        c.wait_recv()

    y_left = (3.0 - y.astype(F32)) * float(LEN)

    def end_states(ln):
        rate = par[16:32, ln]
        _, cb = chain_back(rate, NY, LEN, lambda i: gty[i, :, ln], y)
        _, gb = chain_back(rate, NZ * NX, NY * LEN, lambda i: gtg[i, :, ln], g_own)
        b = cb + jnp.exp(-rate * y_left) * gb
        decay = e1[16 * SUB : 16 * SUB + 16, ln]
        for i in reversed(range(NSUB)):
            st[16 * i : 16 * i + 16, ln] = b
            b = decay * b + lgs[16 * i : 16 * i + 16, ln]

    lanes(end_states)

    def far_grad(ln):
        for s0 in range(0, NSUB, 4):
            acc = [yb[16 * (s0 + j) : 16 * (s0 + j) + 16, ln] for j in range(4)]
            for m in range(MODES):
                t = re3[16 * m : 16 * m + 16, ln]
                for j in range(4):
                    at = 16 * (s0 + j) + m
                    acc[j] = acc[j] + t * st[at : at + 1, ln]
            for j in range(4):
                yb[16 * (s0 + j) : 16 * (s0 + j) + 16, ln] = acc[j]

    lanes(far_grad)
    prod_grad = yb[...].T
    kg_ref[0] = (prod_grad * v_ref[0].astype(F32)).astype(BF16)
    vg_ref[0] = (prod_grad * k_ref[0].astype(F32)).astype(BF16)

    for c in fg_g:
        c.wait_recv()
    fgg[g_own] = fgs[zl, x]
    tot = fgg[0]
    for i in range(1, NZ * NX):
        tot = tot + fgg[i]
    fgz[zh] = tot
    fg_z = [send(fgz.at[zh], fgz.at[zh], h[1]) for h in hmates]
    step(reduces)
    for c in fg_z:
        c.wait_recv()
    fsib[0] = (fgz[0] + fgz[1]) + (fgz[2] + fgz[3])
    fg_s = send(fsib.at[0], fsib.at[1], sib)

    for _ in range(4):
        step(reduces)

    def quarter(h):
        return pl.ds(pl.multiple_of(h * QUART, QUART), QUART)

    q_sends = [
        send(terms.at[zl, x, y, :, quarter(h[0])], quart_in.at[i], h[1]) for i, h in enumerate(hmates)
    ]
    fg_s.wait_recv()
    fsum = fsib[0] + fsib[1]
    resg_ref[...] = fsum[:, 0:16]
    rateg_ref[...] = fsum[:, 16:32]
    for c in q_sends:
        c.wait_recv()
    total = terms[zl, x, y, :, quarter(zh)].astype(F32)
    for i in range(NH - 1):
        total = total + quart_in[i].astype(F32)
    fin[zh] = total
    f_sends = [send(fin.at[zh], fin.at[zh], h[1]) for h in hmates]
    for c in f_sends:
        c.wait_recv()
    f_sib = send(fin, fin_sib, sib)
    for h in range(NH):
        at = pl.multiple_of(core * HALF + h * QUART, QUART)
        wg_ref[:, pl.ds(at, QUART)] = fin[h]
    f_sib.wait_recv()
    for h in range(NH):
        at = pl.multiple_of((1 - core) * HALF + h * QUART, QUART)
        wg_ref[:, pl.ds(at, QUART)] = fin_sib[h]
    for c in copies:
        c.wait_send()


def on_device(query_feat, key_feat, value_feat, upstream, out_weight, residues, decay_rates):
    vm = pl.BlockSpec(memory_space=pltpu.VMEM)
    hbm = pl.BlockSpec(memory_space=pl.ANY)
    slab = (NZ, NX, NY, 16)
    scratch = [
        pltpu.VMEM(slab + (HALF,), BF16),
        pltpu.VMEM(slab + (HALF,), BF16),
        pltpu.VMEM((2 * LEN, HALF), BF16),
        pltpu.VMEM((CH, LEN), F32),
        pltpu.VMEM((CH, LEN), F32),
        pltpu.VMEM((CH, LEN), F32),
        pltpu.VMEM(slab + (128,), F32),
        pltpu.VMEM((32, CH), F32),
        pltpu.VMEM((NSUB, 2 * SUB, CH), F32),
        pltpu.VMEM((LEN, CH), F32),
        pltpu.VMEM((32, CH), F32),
        pltpu.VMEM((32, CH), F32),
        pltpu.VMEM((272, CH), F32),
        pltpu.VMEM((272, CH), F32),
        pltpu.VMEM((256, CH), F32),
        pltpu.VMEM((256, CH), F32),
        pltpu.VMEM((LEN, CH), F32),
        pltpu.VMEM((LEN, CH), F32),
        pltpu.VMEM((LEN, CH), F32),
        pltpu.VMEM((LEN, CH), F32),
        pltpu.VMEM((LEN, CH), F32),
        pltpu.VMEM((LEN, CH), F32),
        pltpu.VMEM((LEN, CH), F32),
        pltpu.VMEM((CH, LEN), F32),
        pltpu.VMEM((NY, 32, CH), F32),
        pltpu.VMEM((NZ * NX, 32, CH), F32),
        pltpu.VMEM((NY, 16, CH), F32),
        pltpu.VMEM((NZ * NX, 16, CH), F32),
        pltpu.VMEM((CH, LEN), BF16),
        pltpu.VMEM((CH, LEN), BF16),
        pltpu.VMEM(slab + (128,), F32),
        pltpu.VMEM((NY, NZ, NX, 16, 128), F32),
        pltpu.VMEM((NZ, NX, 16, 128), F32),
        pltpu.VMEM((NZ * NX, 16, 128), F32),
        pltpu.VMEM((NH, 16, 128), F32),
        pltpu.VMEM((2, 16, 128), F32),
        pltpu.VMEM((128, CH), F32),
        pltpu.VMEM((NH - 1, 16, QUART), BF16),
        pltpu.VMEM((NH, 16, QUART), F32),
        pltpu.VMEM((NH, 16, QUART), F32),
    ]
    for group in reduce_buffers():
        scratch += [pltpu.VMEM(s, BF16) for s in group]
    scratch += [
        pltpu.SemaphoreType.DMA((N_SEMS,)),
        pltpu.SemaphoreType.DMA((N_SEMS,)),
        pltpu.SemaphoreType.DMA((2,)),
    ]
    return pl.pallas_call(
        kernel,
        out_shape=(
            jax.ShapeDtypeStruct(query_feat.shape, BF16),
            jax.ShapeDtypeStruct(key_feat.shape, BF16),
            jax.ShapeDtypeStruct(value_feat.shape, BF16),
            jax.ShapeDtypeStruct(out_weight.shape, F32),
            jax.ShapeDtypeStruct(residues.shape, F32),
            jax.ShapeDtypeStruct(decay_rates.shape, F32),
        ),
        in_specs=[vm, vm, vm, hbm, hbm, vm, vm],
        out_specs=(vm,) * 6,
        scratch_shapes=scratch,
        compiler_params=pltpu.CompilerParams(
            collective_id=0, has_side_effects=True, vmem_limit_bytes=56 * 1024 * 1024
        ),
    )(query_feat, key_feat, value_feat, upstream, out_weight, residues, decay_rates)


def solution(mesh):
    return jax.shard_map(
        on_device,
        mesh=mesh,
        in_specs=(
            P("cuts", None, "seq"),
            P("cuts", None, "seq"),
            P("cuts", None, "seq"),
            P("cuts", "seq", None),
            P("seq", None),
            P("seq", None),
            P("seq", None),
        ),
        out_specs=(
            P("cuts", None, "seq"),
            P("cuts", None, "seq"),
            P("cuts", None, "seq"),
            P("seq", None),
            P("seq", None),
            P("seq", None),
        ),
        check_vma=False,
    )
```

```python
import jax
import jax.numpy as jnp
from jax import lax
from jax.experimental import pallas as pl
from jax.experimental.pallas import tpu as pltpu
from jax.sharding import PartitionSpec as P

MESH = pl.DeviceIdType.MESH
F32 = jnp.float32
BF16 = jnp.bfloat16
NX, NY, NZ, NH = 4, 4, 2, 4
NSEQ = NX * NY * NZ
CH, LEN, WIDTH, HALF = 512, 128, 8192, 4096
MODES, SUB, NSUB = 16, 16, 8
GROUPS, PER = 4, 8

GATHER = (
    (("x", "y", "z"), 0, 1536),
    (("y", "x", "z"), 1536, 1536),
    (("z", "x", "y"), 3072, 512),
    (("z", "y", "x"), 3584, 512),
)
REDUCE = (
    (("z", "x", "y"), 0, 1024),
    (("x", "y", "z"), 1024, 1024),
    (("z", "y", "x"), 2048, 1024),
    (("y", "x", "z"), 3072, 1024),
)
N_SEMS = 160


def reduce_buffers():
    shapes = []
    for order, _, cols in REDUCE:
        size = {"z": NZ, "x": NX, "y": NY}
        for dim in order:
            size[dim] = 1
            shapes.append((1 if dim == "z" else 3, size["z"], size["x"], size["y"], 16, cols))
    return shapes


def kernel(
    q_ref, k_ref, v_ref, up_ref, w_ref, res_ref, dec_ref,
    qg_ref, kg_ref, vg_ref, wg_ref, resg_ref, rateg_ref,
    wbuf, terms, upb, bp_own, bp_sib, bp_in, qkv, ptile, par,
    e1, e1d, re2, re3, hpad, hrev, a2a, upad, gbuf,
    ls, lds, st, std, lgs, lgds, heads, yb, conv_own, conv_sib, fgz, fgs, tail_in, fin, fin_sib, *rest,
):
    n_red = len(reduce_buffers())
    red_refs = list(rest[:n_red])
    send_sem, recv_sem, local_sem = rest[n_red:]
    cuts, seq = lax.axis_index("cuts"), lax.axis_index("seq")
    core, zh = cuts % 2, cuts // 2
    zl, x, y = seq // 16, (seq // 4) % 4, seq % 4
    z = zh * 2 + zl

    def dev(z_, x_, y_, c_):
        return {"cuts": (z_ // 2) * 2 + c_, "seq": (z_ % 2) * 16 + x_ * 4 + y_}

    xs = [(x + d) % 4 for d in range(4)]
    ys = [(y + d) % 4 for d in range(4)]
    sib = dev(z, x, y, 1 - core)
    zpair = zh * 2 + (1 - zl)
    hmates = [dev(((zh + d) % 4) * 2 + zl, x, y, core) for d in (1, 2, 3)]
    z_plus, z_minus = (z + 1) % 8, (z + 7) % 8
    mates = {
        "x": [dev(z, xs[d], y, core) for d in (1, 2, 3)],
        "y": [dev(z, x, ys[d], core) for d in (1, 2, 3)],
    }
    near_z = (dev(z_plus, x, y, core), dev(z_minus, x, y, core))
    zfar = z_minus + z_plus - zpair
    others = [{"cuts": cuts, "seq": (seq + d) % NSEQ} for d in range(1, NSEQ)]
    partners = [sib] + others + hmates + [dev(zfar, x, y, core)]

    copies, used = [], [0]

    def new_sem():
        used[0] += 1
        return used[0] - 1

    def send(src, dst, to):
        i = new_sem()
        c = pltpu.make_async_remote_copy(
            src_ref=src, dst_ref=dst, send_sem=send_sem.at[i], recv_sem=recv_sem.at[i],
            device_id=to, device_id_type=MESH,
        )
        c.start()
        copies.append(c)
        return c

    mine = pl.ds(pl.multiple_of(core * HALF, HALF), HALF)
    theirs = pl.ds(pl.multiple_of((1 - core) * HALF, HALF), HALF)
    locals_ = [
        pltpu.make_async_copy(src, dst, local_sem.at[i])
        for i, (src, dst) in enumerate(
            (
                (k_ref.at[0], qkv.at[1]),
                (v_ref.at[0], qkv.at[2]),
                (w_ref.at[:, mine], wbuf.at[zl, x, y]),
                (q_ref.at[0], qkv.at[0]),
                (up_ref.at[0, :, mine], upb.at[pl.ds(0, LEN)]),
            )
        )
    ]
    for c in locals_:
        c.start()
    barrier = pltpu.get_barrier_semaphore()
    for d in partners:
        pl.semaphore_signal(barrier, inc=1, device_id=d, device_id_type=MESH)

    locals_[0].wait()
    locals_[1].wait()
    u_out, u_in, s_out, s_in = a2a.at[0], a2a.at[1], a2a.at[2], a2a.at[3]
    g_out, g_in, p_out, p_in = a2a.at[4], a2a.at[5], a2a.at[6], a2a.at[7]
    u_out[...] = (qkv[1].astype(F32) * qkv[2].astype(F32)).reshape(NSEQ, 16, LEN)
    fgs[...] = jnp.zeros((2, 128, 128), F32)
    pl.semaphore_wait(barrier, len(partners))

    def round_copy(src, dst, sem, n):
        return pltpu.make_async_remote_copy(
            src_ref=src.at[n], dst_ref=dst.at[seq], send_sem=send_sem.at[sem], recv_sem=recv_sem.at[sem],
            device_id={"cuts": cuts, "seq": n}, device_id_type=MESH,
        )

    def round_wait(buf, sem_ref, sem):
        part = buf.at[pl.ds(0, NSEQ - 1)]
        pltpu.make_async_copy(part, part, sem_ref.at[sem]).wait()

    def scatter(src, dst):
        sem = new_sem()
        for d in range(1, NSEQ):
            round_copy(src, dst, sem, (seq + d) % NSEQ).start()
        dst[seq] = src[seq]
        return sem

    u_sem = scatter(u_out, u_in)

    coord = {"z": zl, "x": x, "y": y}
    around = {"x": xs, "y": ys}
    full = {"z": pl.ds(0, NZ), "x": pl.ds(0, NX), "y": pl.ds(0, NY)}

    def gather(order, col, cols):
        held = {d: pl.ds(coord[d], 1) for d in "zxy"}
        half = cols // 2

        def at(first, count):
            return wbuf.at[held["z"], held["x"], held["y"], :, pl.ds(first, count)]

        for dim in order:
            if dim == "z":
                r0, r1 = at(col, half), at(col + half, half)
                sent = [send(r0, r0, near_z[0]), send(r1, r1, near_z[1])]
            else:
                r = at(col, cols)
                sent = [send(r, r, m) for m in mates[dim]]
            yield
            for c in sent:
                c.wait_recv()
            held[dim] = full[dim]

    def add_into(dst, srcs):
        na, nb, nc = dst.shape[:3]

        def body(i, carry):
            ia, ib, ic = i // (nb * nc), (i // nc) % nb, i % nc
            total = dst[ia, ib, ic].astype(F32)
            for s in srcs:
                total = total + s[ia, ib, ic].astype(F32)
            dst[ia, ib, ic] = total.astype(BF16)
            return carry

        lax.fori_loop(0, na * nb * nc, body, 0)

    def reduce(order, col, cols, bufs):
        left = dict(full)
        half = cols // 2

        def at(first, count, **other):
            s = {**left, **other}
            return terms.at[s["z"], s["x"], s["y"], :, pl.ds(first, count)]

        for dim, land in zip(order, bufs):
            if dim == "z":
                out = pl.ds(1 - zl, 1)
                sent = [
                    send(at(col + i * half, half, z=out), land.at[0, :, :, :, :, pl.ds(i * half, half)], near_z[i])
                    for i in (0, 1)
                ]
            else:
                sent = [
                    send(at(col, cols, **{dim: pl.ds(around[dim][d], 1)}), land.at[d - 1], mates[dim][d - 1])
                    for d in (1, 2, 3)
                ]
            left[dim] = pl.ds(coord[dim], 1)
            yield
            for c in sent:
                c.wait_recv()
            add_into(at(col, cols), [land.at[i] for i in range(land.shape[0])])
        at_cols = pl.ds(col, cols)
        own = terms.at[zl, x, y, :, at_cols]
        sent = [send(own, tail_in.at[i, :, at_cols], m) for i, m in enumerate(hmates)]
        yield
        for c in sent:
            c.wait_recv()
        total = own[...].astype(F32)
        for i in range(NH - 1):
            total = total + tail_in[i, :, at_cols].astype(F32)
        fin[:, at_cols] = total
        c = send(fin.at[:, at_cols], fin_sib.at[:, at_cols], sib)
        wg_ref[:, pl.ds(pl.multiple_of(core * HALF + col, 128), cols)] = total
        yield
        c.wait_recv()
        wg_ref[:, pl.ds(pl.multiple_of((1 - core) * HALF + col, 128), cols)] = fin_sib[:, at_cols]

    def step(gens):
        for g in gens:
            next(g, None)

    def lanes(body):
        def run(i, carry):
            body(i, pl.ds(pl.multiple_of(i * 128, 128), 128))
            return carry

        lax.fori_loop(0, GROUPS, run, 0)

    up_sib = send(up_ref.at[0, :, theirs], upb.at[pl.ds(LEN, LEN)], sib)
    locals_[2].wait()
    gathers = [gather(*g) for g in GATHER]
    step(gathers)

    ptile[...] = jnp.zeros((128, 128), F32)
    for j in range(PER):
        ptile[16 * j : 16 * j + 16, 0:16] = res_ref[...]
        ptile[16 * j : 16 * j + 16, 16:32] = dec_ref[...]
    par[...] = ptile[...].T[0:32]
    resid, rate = par[0:16], par[16:32]
    row = lax.broadcasted_iota(jnp.int32, (16, 128), 0).astype(F32)
    lane = lax.broadcasted_iota(jnp.int32, (16, 128), 1)
    zero = jnp.zeros((16, 128), F32)

    def rows16(i):
        return slice(16 * i, 16 * i + 16)

    for i in range(SUB + 1):
        e = jnp.exp(-rate * float(i))
        e1[rows16(i)] = e
        e1d[rows16(i)] = e * float(i)
    h, hr = zero, zero
    for m in range(MODES):
        rm, dm = resid[m : m + 1], rate[m : m + 1]
        fwd = rm * jnp.exp(-dm * row)
        re2[rows16(m)] = fwd
        re3[rows16(m)] = rm * jnp.exp(-dm * (16.0 - row))
        h = h + fwd
        hr = hr + rm * jnp.exp(-dm * (15.0 - row))
    hpad[0:16] = zero
    hpad[16:32] = h
    hrev[0:16] = hr
    hrev[16:32] = zero
    upad[:, 0:SUB, :] = jnp.zeros((NSUB, SUB, CH), F32)
    sub_decay = e1[rows16(SUB)]

    def hop(d):
        return jnp.exp(-rate * float(LEN * d))

    moved = (lane // 16).astype(F32) * float(LEN)
    moved_back = ((PER - 1) - lane // 16).astype(F32) * float(LEN)

    def spread(t, last):
        t = jnp.where((lane >= 112) if last else (lane < 16), t, 0.0)
        for d in (16, 32, 64):
            t = t + pltpu.roll(t, d, 1)
        return t

    round_wait(u_in, recv_sem, u_sem)

    def product_states(g, ln):
        upad[:, SUB : 2 * SUB, ln] = u_in[pl.ds(g * PER, PER)].reshape(128, LEN).T.reshape(NSUB, SUB, 128)
        for s0 in range(0, NSUB, 4):
            a = [zero for _ in range(4)]
            b = [zero for _ in range(4)]
            for i in range(SUB):
                e, ed = e1[rows16(SUB - i)], e1d[rows16(SUB - i)]
                for j in range(4):
                    u = upad[s0 + j, SUB + i : SUB + i + 1, ln]
                    a[j] = a[j] + e * u
                    b[j] = b[j] + ed * u
            for j in range(4):
                ls[rows16(s0 + j), ln] = a[j]
                lds[rows16(s0 + j), ln] = b[j]
        s, ds_ = zero, zero
        for i in range(NSUB):
            ds_ = sub_decay * (ds_ + float(SUB) * s) + lds[rows16(i), ln]
            s = sub_decay * s + ls[rows16(i), ln]
        heads[0:16, ln] = s
        heads[16:32, ln] = ds_

    lanes(product_states)

    cs, cds = zero, zero
    for g in range(GROUPS):
        ln = slice(128 * g, 128 * g + 128)
        s, ds_ = heads[0:16, ln], heads[16:32, ln]
        for d in (1, 2, 4):
            keep = lane >= 16 * d
            sh = jnp.where(keep, pltpu.roll(s, 16 * d, 1), 0.0)
            shd = jnp.where(keep, pltpu.roll(ds_, 16 * d, 1), 0.0)
            q = hop(d)
            ds_ = ds_ + q * (shd + float(LEN * d) * sh)
            s = s + q * sh
        first = lane >= 16
        q = jnp.exp(-rate * moved)
        heads[0:16, ln] = jnp.where(first, pltpu.roll(s, 16, 1), 0.0) + q * cs
        heads[16:32, ln] = jnp.where(first, pltpu.roll(ds_, 16, 1), 0.0) + q * (cds + moved * cs)
        q = hop(PER)
        cds = spread(ds_, True) + q * (cds + float(LEN * PER) * cs)
        cs = spread(s, True) + q * cs

    s_sem = new_sem()
    own_group = seq // PER

    def give(src, dst, sem, g):
        for j in range(PER):
            n = g * PER + (j + seq) % PER

            @pl.when(n != seq)
            def _():
                round_copy(src, dst, sem, n).start()

    def smooth_group(i, carry):
        g = (i + own_group) % GROUPS
        ln = pl.ds(pl.multiple_of(g * 128, 128), 128)
        s, ds_ = heads[0:16, ln], heads[16:32, ln]
        for j in range(NSUB):
            st[rows16(j), ln] = s
            std[rows16(j), ln] = ds_
            ds_ = sub_decay * (ds_ + float(SUB) * s) + lds[rows16(j), ln]
            s = sub_decay * s + ls[rows16(j), ln]
        for s0 in range(0, NSUB, 4):
            acc = [zero for _ in range(4)]
            for k in range(SUB):
                t, t2 = hpad[16 - k : 32 - k], re2[rows16(k)]
                for j in range(4):
                    at = 16 * (s0 + j) + k
                    acc[j] = acc[j] + t * upad[s0 + j, SUB + k : SUB + k + 1, ln] + t2 * st[at : at + 1, ln]
            for j in range(4):
                yb[rows16(s0 + j)] = acc[j]
        s_out[pl.ds(g * PER, PER)] = yb[...].T.reshape(PER, 16, LEN)
        give(s_out, s_in, s_sem, g)
        return carry

    lax.fori_loop(0, GROUPS, smooth_group, 0)
    s_in[seq] = s_out[seq]
    step(gathers)
    locals_[3].wait()
    locals_[4].wait()
    up_sib.wait_recv()
    round_wait(s_in, recv_sem, s_sem)
    smooth = s_in[...].reshape(CH, LEN)
    conv_own[...] = (qkv[0].astype(F32) * smooth).astype(BF16)
    conv_sib_copy = send(conv_own, conv_sib, sib)
    step(gathers)
    conv_sib_copy.wait_recv()

    both = jnp.concatenate([conv_own[...], conv_sib[...]], axis=1)
    reduces = []
    for n, (order, col, cols) in enumerate(REDUCE):

        def tile(i, carry, col=col):
            c = pl.ds(pl.multiple_of(col + i * 256, 256), 256)
            t = jnp.dot(both, upb[:, c], preferred_element_type=F32)
            terms[:, :, :, :, c] = t.astype(BF16).reshape(NZ, NX, NY, 16, 256)
            return carry

        lax.fori_loop(0, cols // 256, tile, 0)
        g = reduce(order, col, cols, red_refs[3 * n : 3 * n + 3])
        next(g, None)
        reduces.append(g)

    step(gathers)

    bp_own[...] = jnp.zeros((CH, LEN), F32)
    bp_sib[...] = jnp.zeros((CH, LEN), F32)

    def proj(i, carry):
        c = pl.ds(pl.multiple_of(i * 512, 512), 512)
        t = lax.dot_general(
            wbuf[:, :, :, :, c].reshape(CH, 512), upb[:, c], (((1,), (1,)), ((), ())), preferred_element_type=F32
        )
        bp_own[...] += t[:, 0:LEN]
        bp_sib[...] += t[:, LEN:]
        return carry

    lax.fori_loop(0, HALF // 512, proj, 0)
    bp_copy = send(bp_sib, bp_in, sib)
    bp_copy.wait_recv()
    back = (bp_own[...] + bp_in[...]).astype(BF16).astype(F32)
    g_out[...] = (back * qkv[0].astype(F32)).reshape(NSEQ, 16, LEN)
    g_sem = scatter(g_out, g_in)
    qg_ref[0] = (back * s_in[...].reshape(CH, LEN)).astype(BF16)
    step(reduces)
    round_wait(g_in, recv_sem, g_sem)

    def grad_states(g, ln):
        gbuf[:, ln] = g_in[pl.ds(g * PER, PER)].reshape(128, LEN).T
        for s0 in range(0, NSUB, 4):
            a = [zero for _ in range(4)]
            b = [zero for _ in range(4)]
            for i in range(SUB):
                e, ed = e1[rows16(i)], e1d[rows16(i)]
                for j in range(4):
                    at = 16 * (s0 + j) + i
                    v = gbuf[at : at + 1, ln]
                    a[j] = a[j] + e * v
                    b[j] = b[j] + ed * v
            for j in range(4):
                lgs[rows16(s0 + j), ln] = a[j]
                lgds[rows16(s0 + j), ln] = b[j]
        b = zero
        for i in reversed(range(NSUB)):
            b = sub_decay * b + lgs[rows16(i), ln]
        heads[0:16, ln] = b

    lanes(grad_states)
    cb = zero
    for g in reversed(range(GROUPS)):
        ln = slice(128 * g, 128 * g + 128)
        b = heads[0:16, ln]
        for d in (1, 2, 4):
            b = b + hop(d) * jnp.where(lane < 128 - 16 * d, pltpu.roll(b, 128 - 16 * d, 1), 0.0)
        heads[0:16, ln] = jnp.where(lane < 112, pltpu.roll(b, 112, 1), 0.0) + jnp.exp(-rate * moved_back) * cb
        cb = spread(b, False) + hop(PER) * cb

    p_sem = new_sem()

    def grad_group(i, carry):
        g = (i + own_group) % GROUPS
        ln = pl.ds(pl.multiple_of(g * 128, 128), 128)
        b = heads[0:16, ln]
        for j in reversed(range(NSUB)):
            ls[rows16(j), ln] = b
            b = sub_decay * b + lgs[rows16(j), ln]
        for s0 in range(0, NSUB, 4):
            acc = [zero for _ in range(4)]
            for k in range(SUB):
                t, t2 = hrev[15 - k : 31 - k], re3[rows16(k)]
                for j in range(4):
                    at = 16 * (s0 + j) + k
                    acc[j] = acc[j] + t * gbuf[at : at + 1, ln] + t2 * ls[at : at + 1, ln]
            for j in range(4):
                yb[rows16(s0 + j)] = acc[j]
        p_out[pl.ds(g * PER, PER)] = yb[...].T.reshape(PER, 16, LEN)
        give(p_out, p_in, p_sem, g)
        return carry

    lax.fori_loop(0, GROUPS, grad_group, 0)
    p_in[seq] = p_out[seq]
    step(reduces)

    def filter_grads(g, ln):
        a, b = zero, zero
        for i in range(NSUB):
            lg, s = lgs[rows16(i), ln], st[rows16(i), ln]
            a = a + lg * s
            b = b + lgds[rows16(i), ln] * s + lg * std[rows16(i), ln]
        for j in range(SUB):
            acc = zero
            for i in range(NSUB):
                acc = acc + gbuf[rows16(i), ln] * upad[i, SUB - j : 2 * SUB - j, ln]
            f = jnp.sum(acc, axis=0, keepdims=True)
            a = a + f * e1[rows16(j)]
            b = b + f * e1d[rows16(j)]
        fgs[0, 0:16] += a
        fgs[0, 16:32] += b

    lanes(filter_grads)
    a, b = fgs[0, 0:16], fgs[0, 16:32]
    for d in (16, 32, 64):
        a = a + pltpu.roll(a, d, 1)
        b = b + pltpu.roll(b, d, 1)
    fgz[zh, 0:16] = a
    fgz[zh, 16:32] = -rate * resid * b
    fg_z = [send(fgz.at[zh], fgz.at[zh], m) for m in hmates]
    step(reduces)
    for c in fg_z:
        c.wait_recv()
    fgs[0, 0:32] = (fgz[0] + fgz[1]) + (fgz[2] + fgz[3])
    fg_s = send(fgs.at[0, pl.ds(0, 32)], fgs.at[1, pl.ds(0, 32)], sib)

    round_wait(p_in, recv_sem, p_sem)
    prod_grad = p_in[...].reshape(CH, LEN)
    kg_ref[0] = (prod_grad * qkv[2].astype(F32)).astype(BF16)
    vg_ref[0] = (prod_grad * qkv[1].astype(F32)).astype(BF16)
    fg_s.wait_recv()
    both_fg = (fgs[0] + fgs[1]).T
    resg_ref[...] = both_fg[0:16, 0:16]
    rateg_ref[...] = both_fg[0:16, 16:32]

    for _ in range(3):
        step(reduces)
    for c in copies:
        c.wait_send()
    for sem in (u_sem, s_sem, g_sem, p_sem):
        round_wait(u_out, send_sem, sem)


def hand_on(*refs):
    n = len(refs) // 2
    sems = refs[-1]
    moves = [pltpu.make_async_copy(refs[i], refs[n + i], sems.at[i]) for i in range(n)]
    for m in moves:
        m.start()
    for m in moves:
        m.wait()


def on_device(query_feat, key_feat, value_feat, upstream, out_weight, residues, decay_rates):
    vm = pl.BlockSpec(memory_space=pltpu.VMEM)
    hbm = pl.BlockSpec(memory_space=pl.ANY)
    slab = (NZ, NX, NY, 16)
    scratch = [
        pltpu.VMEM(slab + (HALF,), BF16),
        pltpu.VMEM(slab + (HALF,), BF16),
        pltpu.VMEM((2 * LEN, HALF), BF16),
        pltpu.VMEM((CH, LEN), F32),
        pltpu.VMEM((CH, LEN), F32),
        pltpu.VMEM((CH, LEN), F32),
        pltpu.VMEM((3, CH, LEN), BF16),
        pltpu.VMEM((128, 128), F32),
        pltpu.VMEM((32, 128), F32),
        pltpu.VMEM((272, 128), F32),
        pltpu.VMEM((272, 128), F32),
        pltpu.VMEM((256, 128), F32),
        pltpu.VMEM((256, 128), F32),
        pltpu.VMEM((32, 128), F32),
        pltpu.VMEM((32, 128), F32),
        pltpu.VMEM((8, NSEQ, 16, LEN), F32),
        pltpu.VMEM((NSUB, 2 * SUB, CH), F32),
        pltpu.VMEM((LEN, CH), F32),
        pltpu.VMEM((LEN, CH), F32),
        pltpu.VMEM((LEN, CH), F32),
        pltpu.VMEM((LEN, CH), F32),
        pltpu.VMEM((LEN, CH), F32),
        pltpu.VMEM((LEN, CH), F32),
        pltpu.VMEM((LEN, CH), F32),
        pltpu.VMEM((32, CH), F32),
        pltpu.VMEM((LEN, 128), F32),
        pltpu.VMEM((CH, LEN), BF16),
        pltpu.VMEM((CH, LEN), BF16),
        pltpu.VMEM((NH, 32, 128), F32),
        pltpu.VMEM((2, 128, 128), F32),
        pltpu.VMEM((NH - 1, 16, HALF), BF16),
        pltpu.VMEM((16, HALF), F32),
        pltpu.VMEM((16, HALF), F32),
    ]
    scratch += [pltpu.VMEM(s, BF16) for s in reduce_buffers()]
    scratch += [
        pltpu.SemaphoreType.DMA((N_SEMS,)),
        pltpu.SemaphoreType.DMA((N_SEMS,)),
        pltpu.SemaphoreType.DMA((5,)),
    ]
    out_shape = (
        jax.ShapeDtypeStruct(query_feat.shape, BF16),
        jax.ShapeDtypeStruct(key_feat.shape, BF16),
        jax.ShapeDtypeStruct(value_feat.shape, BF16),
        jax.ShapeDtypeStruct(out_weight.shape, F32),
        jax.ShapeDtypeStruct(residues.shape, F32),
        jax.ShapeDtypeStruct(decay_rates.shape, F32),
    )
    results = pl.pallas_call(
        kernel,
        out_shape=out_shape,
        in_specs=[hbm, hbm, hbm, hbm, hbm, vm, vm],
        out_specs=(vm,) * 6,
        scratch_shapes=scratch,
        compiler_params=pltpu.CompilerParams(
            collective_id=0, has_side_effects=True, vmem_limit_bytes=56 * 1024 * 1024
        ),
    )(query_feat, key_feat, value_feat, upstream, out_weight, residues, decay_rates)
    return pl.pallas_call(
        hand_on,
        out_shape=out_shape,
        in_specs=[hbm] * 6,
        out_specs=(hbm,) * 6,
        scratch_shapes=[pltpu.SemaphoreType.DMA((6,))],
    )(*results)


def solution(mesh):
    return jax.shard_map(
        on_device,
        mesh=mesh,
        in_specs=(
            P("cuts", None, "seq"),
            P("cuts", None, "seq"),
            P("cuts", None, "seq"),
            P("cuts", "seq", None),
            P("seq", None),
            P("seq", None),
            P("seq", None),
        ),
        out_specs=(
            P("cuts", None, "seq"),
            P("cuts", None, "seq"),
            P("cuts", None, "seq"),
            P("seq", None),
            P("seq", None),
            P("seq", None),
        ),
        check_vma=False,
    )
```

```python
import jax
import jax.numpy as jnp
from jax import lax
from jax.experimental import pallas as pl
from jax.experimental.pallas import tpu as pltpu
from jax.sharding import PartitionSpec as P

MESH = pl.DeviceIdType.MESH
F32 = jnp.float32
BF16 = jnp.bfloat16
NX, NY, NZ, NH = 4, 4, 2, 4
NSEQ = NX * NY * NZ
CH, LEN, WIDTH, HALF = 512, 128, 8192, 4096
MODES, SUB, NSUB = 16, 16, 8
GROUPS, PER = 4, 8

GATHER = (
    ("xyz", 0, 512),
    ("yxz", 512, 512),
    ("zxY", 1024, 512),
    ("zyX", 1536, 512),
    ("xyz", 2048, 512),
    ("yxz", 2560, 512),
    ("zxY", 3072, 512),
    ("zyX", 3584, 512),
)
REDUCE = (
    ("zXy", 0, 512),
    ("Xyz", 512, 512),
    ("zYx", 1024, 512),
    ("Yxz", 1536, 512),
    ("zXy", 2048, 512),
    ("Xyz", 2560, 512),
    ("zYx", 3072, 512),
    ("Yxz", 3584, 512),
)
ORDER = (
    "G2", "G3", "G6", "G7", "m", "G0", "G1", "G4", "G5", "G2", "G3", "G6", "G7", "m", "m", "R0", "R1", "G0", "G1", "R2", "R3", "R4", "R5", "R6", "G4", "G5", "R7", "G2", "G3", "R0", "G6", "G7", "M0", "R1",
    "R3", "R5", "R7", "M1", "M2", "M3", "R0", "M6", "M7", "R2", "R3", "R1", "R4", "R7", "R5", "R2", "R6", "R0", "R1", "M4", "R4", "R3", "R5", "R2", "M5", "g", "R7", "R1", "R6", "R3", "R4", "g", "R0", "R5",
    "R7", "R2", "R6", "R4", "R1", "R3", "R1", "R6", "R3", "g", "g", "R0", "R5", "R7", "R2", "R0", "R5", "R7", "R4", "R2", "g", "R6", "R4", "R6", "g", "g",
)


def reduce_buffers():
    shapes = []
    for order, _, cols in REDUCE:
        size = {"z": NZ, "x": NX, "y": NY}
        for dim in order.lower():
            size[dim] = 1
            shapes.append((1 if dim == "z" else 3, size["z"], size["x"], size["y"], 16, cols))
    return shapes


def n_semaphores():
    steps = sum(len(o) + sum(d.isupper() for d in o) for o, _, _ in GATHER + REDUCE)
    return steps + 2 * len(REDUCE) + 9


def kernel(
    q_ref, k_ref, v_ref, up_ref, w_ref, res_ref, dec_ref,
    qg_ref, kg_ref, vg_ref, wg_ref, resg_ref, rateg_ref,
    wbuf, terms, upb, bp_own, bp_sib, bp_in, qkv, ptile, par,
    e1, e1d, re2, re3, hpad, hrev, a2a, upad, gbuf,
    ls, lds, st, std, lgs, lgds, heads, yb, conv_own, conv_sib, fgz, fgs, tail_in, fin, fin_sib, grads_out, modes_in, modes_out, *rest,
):
    n_red = len(reduce_buffers())
    red_refs = list(rest[:n_red])
    send_sem, recv_sem, local_sem = rest[n_red:]
    cuts, seq = lax.axis_index("cuts"), lax.axis_index("seq")
    core, zh = cuts % 2, cuts // 2
    zl, x, y = seq // 16, (seq // 4) % 4, seq % 4
    z = zh * 2 + zl

    def dev(z_, x_, y_, c_):
        return {"cuts": (z_ // 2) * 2 + c_, "seq": (z_ % 2) * 16 + x_ * 4 + y_}

    xs = [(x + d) % 4 for d in range(4)]
    ys = [(y + d) % 4 for d in range(4)]
    sib = dev(z, x, y, 1 - core)
    zpair = zh * 2 + (1 - zl)
    hmates = [dev(((zh + d) % 4) * 2 + zl, x, y, core) for d in (1, 2, 3)]
    z_plus, z_minus = (z + 1) % 8, (z + 7) % 8
    mates = {
        "x": [dev(z, xs[d], y, core) for d in (1, 2, 3)],
        "y": [dev(z, x, ys[d], core) for d in (1, 2, 3)],
    }
    near_z = (dev(z_plus, x, y, core), dev(z_minus, x, y, core))
    zfar = z_minus + z_plus - zpair
    others = [{"cuts": cuts, "seq": (seq + d) % NSEQ} for d in range(1, NSEQ)]
    partners = [sib] + others + hmates + [dev(zfar, x, y, core)]

    copies, used = [], [0]

    def new_sem():
        used[0] += 1
        return used[0] - 1

    class Group:
        def __init__(self, moves, whole):
            self.sem, self.whole = new_sem(), whole
            for src, dst, to in moves:
                pltpu.make_async_remote_copy(
                    src_ref=src, dst_ref=dst, send_sem=send_sem.at[self.sem], recv_sem=recv_sem.at[self.sem],
                    device_id=to, device_id_type=MESH,
                ).start()
            copies.append(self)

        def wait_recv(self):
            pltpu.make_async_copy(self.whole, self.whole, recv_sem.at[self.sem]).wait()

        def wait_send(self):
            pltpu.make_async_copy(self.whole, self.whole, send_sem.at[self.sem]).wait()

    def send(src, dst, to):
        return Group([(src, dst, to)], dst)

    results = []

    def put(src, dst):
        c = pltpu.make_async_copy(src, dst, local_sem.at[7 + len(results)])
        c.start()
        results.append(c)

    mine = pl.ds(pl.multiple_of(core * HALF, HALF), HALF)
    theirs = pl.ds(pl.multiple_of((1 - core) * HALF, HALF), HALF)
    locals_ = [
        pltpu.make_async_copy(src, dst, local_sem.at[i])
        for i, (src, dst) in enumerate(
            (
                (k_ref.at[0], qkv.at[1]),
                (v_ref.at[0], qkv.at[2]),
                (w_ref.at[:, mine], wbuf.at[zl, x, y]),
                (q_ref.at[0], qkv.at[0]),
                (up_ref.at[0, :, mine], upb.at[pl.ds(0, LEN)]),
                (res_ref, modes_in.at[0]),
                (dec_ref, modes_in.at[1]),
            )
        )
    ]
    for c in locals_:
        c.start()
    barrier = pltpu.get_barrier_semaphore()
    for d in partners:
        pl.semaphore_signal(barrier, inc=1, device_id=d, device_id_type=MESH)

    locals_[0].wait()
    locals_[1].wait()
    u_out, u_in, s_out, s_in = a2a.at[0], a2a.at[1], a2a.at[2], a2a.at[3]
    g_out, g_in, p_out, p_in = a2a.at[4], a2a.at[5], a2a.at[6], a2a.at[7]
    u_out[...] = (qkv[1].astype(F32) * qkv[2].astype(F32)).reshape(NSEQ, 16, LEN)
    fgs[...] = jnp.zeros((2, 128, 128), F32)
    bp_own[...] = jnp.zeros((CH, LEN), F32)
    bp_sib[...] = jnp.zeros((CH, LEN), F32)
    pl.semaphore_wait(barrier, len(partners))

    def round_copy(src, dst, sem, n):
        return pltpu.make_async_remote_copy(
            src_ref=src.at[n], dst_ref=dst.at[seq], send_sem=send_sem.at[sem], recv_sem=recv_sem.at[sem],
            device_id={"cuts": cuts, "seq": n}, device_id_type=MESH,
        )

    def round_wait(buf, sem_ref, sem):
        part = buf.at[pl.ds(0, NSEQ - 1)]
        pltpu.make_async_copy(part, part, sem_ref.at[sem]).wait()

    def scatter(src, dst, sem):
        for d in range(1, NSEQ):
            round_copy(src, dst, sem, (seq + d) % NSEQ).start()
        dst[seq] = src[seq]

    u_sem = new_sem()
    scatter(u_out, u_in, u_sem)

    coord = {"z": zl, "x": x, "y": y}
    around = {"x": xs, "y": ys}
    full = {"z": pl.ds(0, NZ), "x": pl.ds(0, NX), "y": pl.ds(0, NY)}

    def gather(order, col, cols):
        held = {d: pl.ds(coord[d], 1) for d in "zxy"}
        half = cols // 2

        def at(first, count, **other):
            s = {**held, **other}
            return wbuf.at[s["z"], s["x"], s["y"], :, pl.ds(first, count)]

        for name in order:
            dim = name.lower()
            r, r0, r1 = at(col, cols), at(col, half), at(col + half, half)
            if dim == "z":
                sent = Group([(r0, r0, near_z[0]), (r1, r1, near_z[1])], r)
            elif name == dim:
                sent = Group([(r, r, m) for m in mates[dim]], at(col, cols, **{dim: pl.ds(0, 3)}))
            else:
                plus, minus = mates[dim][0], mates[dim][2]
                sent = Group([(r, r, plus), (r, r, minus)], at(col, cols, **{dim: pl.ds(0, 2)}))
                yield
                sent.wait_recv()
                r0 = at(col, half, **{dim: pl.ds(around[dim][3], 1)})
                r1 = at(col + half, half, **{dim: pl.ds(around[dim][1], 1)})
                sent = Group([(r0, r0, plus), (r1, r1, minus)], r)
            yield
            sent.wait_recv()
            held[dim] = full[dim]

    def add_into(dst, srcs):
        na, nb, nc = dst.shape[:3]

        def body(i, carry):
            ia, ib, ic = i // (nb * nc), (i // nc) % nb, i % nc
            total = dst[ia, ib, ic].astype(F32)
            for s in srcs:
                total = total + s[ia, ib, ic].astype(F32)
            dst[ia, ib, ic] = total.astype(BF16)
            return carry

        lax.fori_loop(0, na * nb * nc, body, 0)

    def reduce(order, col, cols, bufs):
        left = dict(full)
        half = cols // 2

        def at(first, count, **other):
            s = {**left, **other}
            return terms.at[s["z"], s["x"], s["y"], :, pl.ds(first, count)]

        for name, land in zip(order, bufs):
            dim = name.lower()
            arrived = [land.at[i] for i in range(land.shape[0])]
            if dim == "z":
                out = pl.ds(1 - zl, 1)
                parts = [land.at[0, :, :, :, :, pl.ds(i * half, half)] for i in (0, 1)]
                sent = Group([(at(col + i * half, half, z=out), parts[i], near_z[i]) for i in (0, 1)], land)
            elif name == dim:
                sent = Group(
                    [
                        (at(col, cols, **{dim: pl.ds(around[dim][d], 1)}), land.at[d - 1], mates[dim][d - 1])
                        for d in (1, 2, 3)
                    ],
                    land,
                )
            else:
                plus, minus = mates[dim][0], mates[dim][2]
                to_plus, to_minus = ({dim: pl.ds(around[dim][d], 1)} for d in (1, 3))
                far = {dim: pl.ds(around[dim][2], 1)}
                in0 = land.at[2, :, :, :, :, pl.ds(0, half)]
                in1 = land.at[2, :, :, :, :, pl.ds(half, half)]
                sent = Group([(at(col, half, **far), in0, plus), (at(col + half, half, **far), in1, minus)], land.at[2])
                yield
                sent.wait_recv()
                add_into(at(col, half, **to_plus), [in0])
                add_into(at(col + half, half, **to_minus), [in1])
                sent = Group(
                    [(at(col, cols, **to_plus), land.at[0], plus), (at(col, cols, **to_minus), land.at[1], minus)],
                    land.at[pl.ds(0, 2)],
                )
                arrived = arrived[:2]
            left[dim] = pl.ds(coord[dim], 1)
            yield
            sent.wait_recv()
            add_into(at(col, cols), arrived)
        at_cols = pl.ds(col, cols)
        own = terms.at[zl, x, y, :, at_cols]
        landed = tail_in.at[:, :, at_cols]
        sent = Group([(own, tail_in.at[i, :, at_cols], m) for i, m in enumerate(hmates)], landed)
        yield
        sent.wait_recv()
        total = own[...].astype(F32)
        for i in range(NH - 1):
            total = total + tail_in[i, :, at_cols].astype(F32)
        fin[:, at_cols] = total
        c = send(fin.at[:, at_cols], fin_sib.at[:, at_cols], sib)
        put(fin.at[:, at_cols], wg_ref.at[:, pl.ds(pl.multiple_of(core * HALF + col, 128), cols)])
        yield
        c.wait_recv()
        put(fin_sib.at[:, at_cols], wg_ref.at[:, pl.ds(pl.multiple_of((1 - core) * HALF + col, 128), cols)])

    def terms_of(order, col, cols, bufs):
        width = 256 if cols % 256 == 0 else 128

        def tile(i, carry):
            c = pl.ds(pl.multiple_of(col + i * width, 128), width)
            t = jnp.dot(
                jnp.concatenate([conv_own[...], conv_sib[...]], axis=1), upb[:, c], preferred_element_type=F32
            )
            terms[:, :, :, :, c] = t.astype(BF16).reshape(NZ, NX, NY, 16, width)
            return carry

        lax.fori_loop(0, cols // width, tile, 0)
        yield from reduce(order, col, cols, bufs)

    def project(col, cols):
        width = 512 if cols % 512 == 0 else 256

        def tile(i, carry):
            c = pl.ds(pl.multiple_of(col + i * width, 128), width)
            t = lax.dot_general(
                wbuf[:, :, :, :, c].reshape(CH, width), upb[:, c], (((1,), (1,)), ((), ())), preferred_element_type=F32
            )
            bp_own[...] += t[:, 0:LEN]
            bp_sib[...] += t[:, LEN:]
            return carry

        lax.fori_loop(0, cols // width, tile, 0)

    gathers = [gather(*g) for g in GATHER]
    reduces = [terms_of(*r, red_refs[3 * n : 3 * n + 3]) for n, r in enumerate(REDUCE)]

    def lanes(body):
        def run(i, carry):
            body(i, pl.ds(pl.multiple_of(i * 128, 128), 128))
            return carry

        lax.fori_loop(0, GROUPS, run, 0)

    up_sib = send(up_ref.at[0, :, theirs], upb.at[pl.ds(LEN, LEN)], sib)
    locals_[2].wait()
    for g in gathers:
        next(g)

    locals_[5].wait()
    locals_[6].wait()
    ptile[...] = jnp.zeros((128, 128), F32)
    for j in range(PER):
        ptile[16 * j : 16 * j + 16, 0:16] = modes_in[0]
        ptile[16 * j : 16 * j + 16, 16:32] = modes_in[1]
    par[...] = ptile[...].T[0:32]
    resid, rate = par[0:16], par[16:32]
    row = lax.broadcasted_iota(jnp.int32, (16, 128), 0).astype(F32)
    lane = lax.broadcasted_iota(jnp.int32, (16, 128), 1)
    zero = jnp.zeros((16, 128), F32)

    def rows16(i):
        return slice(16 * i, 16 * i + 16)

    for i in range(SUB + 1):
        e = jnp.exp(-rate * float(i))
        e1[rows16(i)] = e
        e1d[rows16(i)] = e * float(i)
    h, hr = zero, zero
    for m in range(MODES):
        rm, dm = resid[m : m + 1], rate[m : m + 1]
        fwd = rm * jnp.exp(-dm * row)
        re2[rows16(m)] = fwd
        re3[rows16(m)] = rm * jnp.exp(-dm * (16.0 - row))
        h = h + fwd
        hr = hr + rm * jnp.exp(-dm * (15.0 - row))
    hpad[0:16] = zero
    hpad[16:32] = h
    hrev[0:16] = hr
    hrev[16:32] = zero
    upad[:, 0:SUB, :] = jnp.zeros((NSUB, SUB, CH), F32)
    sub_decay = e1[rows16(SUB)]

    def hop(d):
        return jnp.exp(-rate * float(LEN * d))

    moved = (lane // 16).astype(F32) * float(LEN)
    moved_back = ((PER - 1) - lane // 16).astype(F32) * float(LEN)

    def spread(t, last):
        t = jnp.where((lane >= 112) if last else (lane < 16), t, 0.0)
        for d in (16, 32, 64):
            t = t + pltpu.roll(t, d, 1)
        return t

    s_sem, g_sem, p_sem = new_sem(), new_sem(), new_sem()
    own_group = seq // PER

    def give(src, dst, sem, g):
        for j in range(PER):
            n = g * PER + (j + seq) % PER

            @pl.when(n != seq)
            def _():
                round_copy(src, dst, sem, n).start()

    def convolve():
        yield
        round_wait(u_in, recv_sem, u_sem)

        def product_states(g, ln):
            upad[:, SUB : 2 * SUB, ln] = u_in[pl.ds(g * PER, PER)].reshape(128, LEN).T.reshape(NSUB, SUB, 128)
            for s0 in range(0, NSUB, 4):
                a = [zero for _ in range(4)]
                b = [zero for _ in range(4)]
                for i in range(SUB):
                    e, ed = e1[rows16(SUB - i)], e1d[rows16(SUB - i)]
                    for j in range(4):
                        u = upad[s0 + j, SUB + i : SUB + i + 1, ln]
                        a[j] = a[j] + e * u
                        b[j] = b[j] + ed * u
                for j in range(4):
                    ls[rows16(s0 + j), ln] = a[j]
                    lds[rows16(s0 + j), ln] = b[j]
            s, ds_ = zero, zero
            for i in range(NSUB):
                ds_ = sub_decay * (ds_ + float(SUB) * s) + lds[rows16(i), ln]
                s = sub_decay * s + ls[rows16(i), ln]
            heads[0:16, ln] = s
            heads[16:32, ln] = ds_

        lanes(product_states)

        cs, cds = zero, zero
        for g in range(GROUPS):
            ln = slice(128 * g, 128 * g + 128)
            s, ds_ = heads[0:16, ln], heads[16:32, ln]
            for d in (1, 2, 4):
                keep = lane >= 16 * d
                sh = jnp.where(keep, pltpu.roll(s, 16 * d, 1), 0.0)
                shd = jnp.where(keep, pltpu.roll(ds_, 16 * d, 1), 0.0)
                q = hop(d)
                ds_ = ds_ + q * (shd + float(LEN * d) * sh)
                s = s + q * sh
            first = lane >= 16
            q = jnp.exp(-rate * moved)
            heads[0:16, ln] = jnp.where(first, pltpu.roll(s, 16, 1), 0.0) + q * cs
            heads[16:32, ln] = jnp.where(first, pltpu.roll(ds_, 16, 1), 0.0) + q * (cds + moved * cs)
            q = hop(PER)
            cds = spread(ds_, True) + q * (cds + float(LEN * PER) * cs)
            cs = spread(s, True) + q * cs


        def smooth_group(i, carry):
            g = (i + own_group) % GROUPS
            ln = pl.ds(pl.multiple_of(g * 128, 128), 128)
            s, ds_ = heads[0:16, ln], heads[16:32, ln]
            for j in range(NSUB):
                st[rows16(j), ln] = s
                std[rows16(j), ln] = ds_
                ds_ = sub_decay * (ds_ + float(SUB) * s) + lds[rows16(j), ln]
                s = sub_decay * s + ls[rows16(j), ln]
            for s0 in range(0, NSUB, 4):
                acc = [zero for _ in range(4)]
                for k in range(SUB):
                    t, t2 = hpad[16 - k : 32 - k], re2[rows16(k)]
                    for j in range(4):
                        at = 16 * (s0 + j) + k
                        acc[j] = acc[j] + t * upad[s0 + j, SUB + k : SUB + k + 1, ln] + t2 * st[at : at + 1, ln]
                for j in range(4):
                    yb[rows16(s0 + j)] = acc[j]
            s_out[pl.ds(g * PER, PER)] = yb[...].T.reshape(PER, 16, LEN)
            give(s_out, s_in, s_sem, g)
            return carry

        lax.fori_loop(0, GROUPS, smooth_group, 0)
        s_in[seq] = s_out[seq]
        locals_[3].wait()
        locals_[4].wait()
        up_sib.wait_recv()
        yield
        round_wait(s_in, recv_sem, s_sem)
        smooth = s_in[...].reshape(CH, LEN)
        conv_own[...] = (qkv[0].astype(F32) * smooth).astype(BF16)
        conv_sib_copy = send(conv_own, conv_sib, sib)
        yield
        conv_sib_copy.wait_recv()


    def gradients():
        bp_copy = send(bp_sib, bp_in, sib)
        yield
        bp_copy.wait_recv()
        back = (bp_own[...] + bp_in[...]).astype(BF16).astype(F32)
        g_out[...] = (back * qkv[0].astype(F32)).reshape(NSEQ, 16, LEN)
        scatter(g_out, g_in, g_sem)
        grads_out[0] = (back * s_in[...].reshape(CH, LEN)).astype(BF16)
        put(grads_out.at[0], qg_ref.at[0])
        yield
        round_wait(g_in, recv_sem, g_sem)

        def grad_states(g, ln):
            gbuf[:, ln] = g_in[pl.ds(g * PER, PER)].reshape(128, LEN).T
            for s0 in range(0, NSUB, 4):
                a = [zero for _ in range(4)]
                b = [zero for _ in range(4)]
                for i in range(SUB):
                    e, ed = e1[rows16(i)], e1d[rows16(i)]
                    for j in range(4):
                        at = 16 * (s0 + j) + i
                        v = gbuf[at : at + 1, ln]
                        a[j] = a[j] + e * v
                        b[j] = b[j] + ed * v
                for j in range(4):
                    lgs[rows16(s0 + j), ln] = a[j]
                    lgds[rows16(s0 + j), ln] = b[j]
            b = zero
            for i in reversed(range(NSUB)):
                b = sub_decay * b + lgs[rows16(i), ln]
            heads[0:16, ln] = b

        lanes(grad_states)
        cb = zero
        for g in reversed(range(GROUPS)):
            ln = slice(128 * g, 128 * g + 128)
            b = heads[0:16, ln]
            for d in (1, 2, 4):
                b = b + hop(d) * jnp.where(lane < 128 - 16 * d, pltpu.roll(b, 128 - 16 * d, 1), 0.0)
            heads[0:16, ln] = jnp.where(lane < 112, pltpu.roll(b, 112, 1), 0.0) + jnp.exp(-rate * moved_back) * cb
            cb = spread(b, False) + hop(PER) * cb


        def grad_group(i, carry):
            g = (i + own_group) % GROUPS
            ln = pl.ds(pl.multiple_of(g * 128, 128), 128)
            b = heads[0:16, ln]
            for j in reversed(range(NSUB)):
                ls[rows16(j), ln] = b
                b = sub_decay * b + lgs[rows16(j), ln]
            for s0 in range(0, NSUB, 4):
                acc = [zero for _ in range(4)]
                for k in range(SUB):
                    t, t2 = hrev[15 - k : 31 - k], re3[rows16(k)]
                    for j in range(4):
                        at = 16 * (s0 + j) + k
                        acc[j] = acc[j] + t * gbuf[at : at + 1, ln] + t2 * ls[at : at + 1, ln]
                for j in range(4):
                    yb[rows16(s0 + j)] = acc[j]
            p_out[pl.ds(g * PER, PER)] = yb[...].T.reshape(PER, 16, LEN)
            give(p_out, p_in, p_sem, g)
            return carry

        lax.fori_loop(0, GROUPS, grad_group, 0)
        p_in[seq] = p_out[seq]
        yield

        def filter_grads(g, ln):
            a, b = zero, zero
            for i in range(NSUB):
                lg, s = lgs[rows16(i), ln], st[rows16(i), ln]
                a = a + lg * s
                b = b + lgds[rows16(i), ln] * s + lg * std[rows16(i), ln]
            for j in range(SUB):
                acc = zero
                for i in range(NSUB):
                    acc = acc + gbuf[rows16(i), ln] * upad[i, SUB - j : 2 * SUB - j, ln]
                f = jnp.sum(acc, axis=0, keepdims=True)
                a = a + f * e1[rows16(j)]
                b = b + f * e1d[rows16(j)]
            fgs[0, 0:16] += a
            fgs[0, 16:32] += b

        lanes(filter_grads)
        a, b = fgs[0, 0:16], fgs[0, 16:32]
        for d in (16, 32, 64):
            a = a + pltpu.roll(a, d, 1)
            b = b + pltpu.roll(b, d, 1)
        fgz[zh, 0:16] = a
        fgz[zh, 16:32] = -rate * resid * b
        fg_z = Group([(fgz.at[zh], fgz.at[zh], m) for m in hmates], fgz.at[pl.ds(0, NH - 1)])
        yield
        fg_z.wait_recv()
        fgs[0, 0:32] = (fgz[0] + fgz[1]) + (fgz[2] + fgz[3])
        fg_s = send(fgs.at[0, pl.ds(0, 32)], fgs.at[1, pl.ds(0, 32)], sib)

        yield
        round_wait(p_in, recv_sem, p_sem)
        prod_grad = p_in[...].reshape(CH, LEN)
        grads_out[1] = (prod_grad * qkv[2].astype(F32)).astype(BF16)
        put(grads_out.at[1], kg_ref.at[0])
        grads_out[2] = (prod_grad * qkv[1].astype(F32)).astype(BF16)
        put(grads_out.at[2], vg_ref.at[0])
        yield
        fg_s.wait_recv()
        both_fg = (fgs[0] + fgs[1]).T
        modes_out[0] = both_fg[0:16, 0:16]
        modes_out[1] = both_fg[0:16, 16:32]
        put(modes_out.at[0], resg_ref)
        put(modes_out.at[1], rateg_ref)


    chains = {"m": convolve(), "g": gradients()}
    next(chains["m"])
    for what in ORDER:
        if what in chains:
            next(chains[what], None)
        elif what[0] == "M":
            for _ in gathers[int(what[1:])]:
                pass
            project(*GATHER[int(what[1:])][1:])
        else:
            next((gathers if what[0] == "G" else reduces)[int(what[1:])], None)
    for c in results:
        c.wait()
    for c in copies:
        c.wait_send()
    for sem in (u_sem, s_sem, g_sem, p_sem):
        round_wait(u_out, send_sem, sem)


def hand_on(*refs):
    n = len(refs) // 2
    for i in range(n):
        refs[n + i][...] = refs[i][...]


def on_device(query_feat, key_feat, value_feat, upstream, out_weight, residues, decay_rates):
    vm = pl.BlockSpec(memory_space=pltpu.VMEM)
    hbm = pl.BlockSpec(memory_space=pl.ANY)
    slab = (NZ, NX, NY, 16)
    scratch = [
        pltpu.VMEM(slab + (HALF,), BF16),
        pltpu.VMEM(slab + (HALF,), BF16),
        pltpu.VMEM((2 * LEN, HALF), BF16),
        pltpu.VMEM((CH, LEN), F32),
        pltpu.VMEM((CH, LEN), F32),
        pltpu.VMEM((CH, LEN), F32),
        pltpu.VMEM((3, CH, LEN), BF16),
        pltpu.VMEM((128, 128), F32),
        pltpu.VMEM((32, 128), F32),
        pltpu.VMEM((272, 128), F32),
        pltpu.VMEM((272, 128), F32),
        pltpu.VMEM((256, 128), F32),
        pltpu.VMEM((256, 128), F32),
        pltpu.VMEM((32, 128), F32),
        pltpu.VMEM((32, 128), F32),
        pltpu.VMEM((8, NSEQ, 16, LEN), F32),
        pltpu.VMEM((NSUB, 2 * SUB, CH), F32),
        pltpu.VMEM((LEN, CH), F32),
        pltpu.VMEM((LEN, CH), F32),
        pltpu.VMEM((LEN, CH), F32),
        pltpu.VMEM((LEN, CH), F32),
        pltpu.VMEM((LEN, CH), F32),
        pltpu.VMEM((LEN, CH), F32),
        pltpu.VMEM((LEN, CH), F32),
        pltpu.VMEM((32, CH), F32),
        pltpu.VMEM((LEN, 128), F32),
        pltpu.VMEM((CH, LEN), BF16),
        pltpu.VMEM((CH, LEN), BF16),
        pltpu.VMEM((NH, 32, 128), F32),
        pltpu.VMEM((2, 128, 128), F32),
        pltpu.VMEM((NH - 1, 16, HALF), BF16),
        pltpu.VMEM((16, HALF), F32),
        pltpu.VMEM((16, HALF), F32),
        pltpu.VMEM((3, CH, LEN), BF16),
        pltpu.VMEM((2, 16, MODES), F32),
        pltpu.VMEM((2, 16, MODES), F32),
    ]
    scratch += [pltpu.VMEM(s, BF16) for s in reduce_buffers()]
    scratch += [
        pltpu.SemaphoreType.DMA((n_semaphores(),)),
        pltpu.SemaphoreType.DMA((n_semaphores(),)),
        pltpu.SemaphoreType.DMA((7 + 5 + 2 * len(REDUCE),)),
    ]
    out_shape = (
        jax.ShapeDtypeStruct(query_feat.shape, BF16),
        jax.ShapeDtypeStruct(key_feat.shape, BF16),
        jax.ShapeDtypeStruct(value_feat.shape, BF16),
        jax.ShapeDtypeStruct(out_weight.shape, F32),
        jax.ShapeDtypeStruct(residues.shape, F32),
        jax.ShapeDtypeStruct(decay_rates.shape, F32),
    )
    results = pl.pallas_call(
        kernel,
        out_shape=out_shape,
        in_specs=[hbm] * 7,
        out_specs=(hbm,) * 6,
        scratch_shapes=scratch,
        compiler_params=pltpu.CompilerParams(
            collective_id=0, has_side_effects=True, vmem_limit_bytes=56 * 1024 * 1024
        ),
    )(query_feat, key_feat, value_feat, upstream, out_weight, residues, decay_rates)
    return pl.pallas_call(
        hand_on,
        out_shape=out_shape,
        in_specs=[vm] * 6,
        out_specs=(vm,) * 6,
    )(*results)


def solution(mesh):
    return jax.shard_map(
        on_device,
        mesh=mesh,
        in_specs=(
            P("cuts", None, "seq"),
            P("cuts", None, "seq"),
            P("cuts", None, "seq"),
            P("cuts", "seq", None),
            P("seq", None),
            P("seq", None),
            P("seq", None),
        ),
        out_specs=(
            P("cuts", None, "seq"),
            P("cuts", None, "seq"),
            P("cuts", None, "seq"),
            P("seq", None),
            P("seq", None),
            P("seq", None),
        ),
        check_vma=False,
    )
```

```python
import jax
import jax.numpy as jnp
from jax import lax
from jax.experimental import pallas as pl
from jax.experimental.pallas import tpu as pltpu
from jax.sharding import PartitionSpec as P

MESH = pl.DeviceIdType.MESH
F32 = jnp.float32
BF16 = jnp.bfloat16
NX, NY, NZ, NH = 4, 4, 2, 4
NSEQ = NX * NY * NZ
CH, LEN, WIDTH, HALF = 512, 128, 8192, 4096
MODES, SUB, NSUB = 16, 16, 8
GROUPS, PER = 4, 8

GATHER = (
    ("xYz", 0, 256),
    ("yXz", 256, 256),
    ("zxY", 512, 1024),
    ("zyX", 1536, 1024),
    ("xzY", 2560, 768),
    ("yzX", 3328, 768),
)
REDUCE = (
    ("zxy", 0, 512),
    ("zyx", 512, 512),
    ("zxy", 1024, 512),
    ("zyx", 1536, 512),
    ("zxy", 2048, 512),
    ("zyx", 2560, 512),
    ("Xzy", 3072, 512),
    ("Yzx", 3584, 512),
)
ORDER = (
    "G2", "G3", "G0", "G1", "m", "G5", "G4", "G1", "G2", "G0", "G3", "G5", "G1", "G4", "m", "m", "R0", "R1", "R2", "M1", "R3", "R4", "G2", "R5", "G0", "G3", "R6", "R7", "R0", "G5", "G4", "R1", "M3", "M2",
    "R2", "R7", "R6", "M4", "R3", "R0", "M5", "R1", "R4", "R7", "R2", "R5", "M0", "g", "R6", "R7", "R3", "R1", "R0", "g", "R2", "R6", "R4", "R7", "R5", "R3", "R1", "R0", "R1", "R6", "R5", "R4", "g", "g",
    "R7", "R2", "R0", "R3", "R7", "R2", "R6", "R3", "R5", "R6", "g", "R4", "R5", "g", "R4", "g",
)


def reduce_buffers():
    shapes = []
    for order, _, cols in REDUCE:
        size = {"z": NZ, "x": NX, "y": NY}
        for dim in order.lower():
            size[dim] = 1
            shapes.append((1 if dim == "z" else 3, size["z"], size["x"], size["y"], 16, cols))
    return shapes


def n_semaphores():
    steps = sum(len(o) + sum(d.isupper() for d in o) for o, _, _ in GATHER + REDUCE)
    return steps + 2 * len(REDUCE) + 9


def kernel(
    q_ref, k_ref, v_ref, up_ref, w_ref, res_ref, dec_ref,
    qg_ref, kg_ref, vg_ref, wg_ref, resg_ref, rateg_ref,
    wbuf, terms, upb, bp_own, bp_sib, bp_in, qkv, ptile, par,
    e1, e1d, re2, re3, hpad, hrev, a2a, upad, gbuf,
    ls, lds, st, std, lgs, lgds, heads, yb, conv_own, conv_sib, fgz, fgs, tail_in, fin, fin_sib, grads_out, modes_in, modes_out, *rest,
):
    n_red = len(reduce_buffers())
    red_refs = list(rest[:n_red])
    send_sem, recv_sem, local_sem = rest[n_red:]
    cuts, seq = lax.axis_index("cuts"), lax.axis_index("seq")
    core, zh = cuts % 2, cuts // 2
    zl, x, y = seq // 16, (seq // 4) % 4, seq % 4
    z = zh * 2 + zl

    def dev(z_, x_, y_, c_):
        return {"cuts": (z_ // 2) * 2 + c_, "seq": (z_ % 2) * 16 + x_ * 4 + y_}

    xs = [(x + d) % 4 for d in range(4)]
    ys = [(y + d) % 4 for d in range(4)]
    sib = dev(z, x, y, 1 - core)
    zpair = zh * 2 + (1 - zl)
    hmates = [dev(((zh + d) % 4) * 2 + zl, x, y, core) for d in (1, 2, 3)]
    z_plus, z_minus = (z + 1) % 8, (z + 7) % 8
    mates = {
        "x": [dev(z, xs[d], y, core) for d in (1, 2, 3)],
        "y": [dev(z, x, ys[d], core) for d in (1, 2, 3)],
    }
    near_z = (dev(z_plus, x, y, core), dev(z_minus, x, y, core))
    zfar = z_minus + z_plus - zpair
    others = [{"cuts": cuts, "seq": (seq + d) % NSEQ} for d in range(1, NSEQ)]
    partners = [sib] + others + hmates + [dev(zfar, x, y, core)]

    copies, used = [], [0]

    def new_sem():
        used[0] += 1
        return used[0] - 1

    class Group:
        def __init__(self, moves, whole):
            self.sem, self.whole = new_sem(), whole
            for src, dst, to in moves:
                pltpu.make_async_remote_copy(
                    src_ref=src, dst_ref=dst, send_sem=send_sem.at[self.sem], recv_sem=recv_sem.at[self.sem],
                    device_id=to, device_id_type=MESH,
                ).start()
            copies.append(self)

        def wait_recv(self):
            pltpu.make_async_copy(self.whole, self.whole, recv_sem.at[self.sem]).wait()

        def wait_send(self):
            pltpu.make_async_copy(self.whole, self.whole, send_sem.at[self.sem]).wait()

    def send(src, dst, to):
        return Group([(src, dst, to)], dst)

    results = []

    def put(src, dst):
        c = pltpu.make_async_copy(src, dst, local_sem.at[7 + len(results)])
        c.start()
        results.append(c)

    mine = pl.ds(pl.multiple_of(core * HALF, HALF), HALF)
    theirs = pl.ds(pl.multiple_of((1 - core) * HALF, HALF), HALF)
    locals_ = [
        pltpu.make_async_copy(src, dst, local_sem.at[i])
        for i, (src, dst) in enumerate(
            (
                (k_ref.at[0], qkv.at[1]),
                (v_ref.at[0], qkv.at[2]),
                (w_ref.at[:, mine], wbuf.at[zl, x, y]),
                (q_ref.at[0], qkv.at[0]),
                (up_ref.at[0, :, mine], upb.at[pl.ds(0, LEN)]),
                (res_ref, modes_in.at[0]),
                (dec_ref, modes_in.at[1]),
            )
        )
    ]
    for c in locals_:
        c.start()
    barrier = pltpu.get_barrier_semaphore()
    for d in partners:
        pl.semaphore_signal(barrier, inc=1, device_id=d, device_id_type=MESH)

    locals_[0].wait()
    locals_[1].wait()
    u_out, u_in, s_out, s_in = a2a.at[0], a2a.at[1], a2a.at[2], a2a.at[3]
    g_out, g_in, p_out, p_in = a2a.at[4], a2a.at[5], a2a.at[6], a2a.at[7]
    u_out[...] = (qkv[1].astype(F32) * qkv[2].astype(F32)).reshape(NSEQ, 16, LEN)
    fgs[...] = jnp.zeros((2, 128, 128), F32)
    bp_own[...] = jnp.zeros((CH, LEN), F32)
    bp_sib[...] = jnp.zeros((CH, LEN), F32)
    pl.semaphore_wait(barrier, len(partners))

    def round_copy(src, dst, sem, n):
        return pltpu.make_async_remote_copy(
            src_ref=src.at[n], dst_ref=dst.at[seq], send_sem=send_sem.at[sem], recv_sem=recv_sem.at[sem],
            device_id={"cuts": cuts, "seq": n}, device_id_type=MESH,
        )

    def round_wait(buf, sem_ref, sem):
        part = buf.at[pl.ds(0, NSEQ - 1)]
        pltpu.make_async_copy(part, part, sem_ref.at[sem]).wait()

    def scatter(src, dst, sem):
        for d in range(1, NSEQ):
            round_copy(src, dst, sem, (seq + d) % NSEQ).start()
        dst[seq] = src[seq]

    u_sem = new_sem()
    scatter(u_out, u_in, u_sem)

    coord = {"z": zl, "x": x, "y": y}
    around = {"x": xs, "y": ys}
    full = {"z": pl.ds(0, NZ), "x": pl.ds(0, NX), "y": pl.ds(0, NY)}

    def gather(order, col, cols):
        held = {d: pl.ds(coord[d], 1) for d in "zxy"}
        half = cols // 2

        def at(first, count, **other):
            s = {**held, **other}
            return wbuf.at[s["z"], s["x"], s["y"], :, pl.ds(first, count)]

        for name in order:
            dim = name.lower()
            r, r0, r1 = at(col, cols), at(col, half), at(col + half, half)
            if dim == "z":
                sent = Group([(r0, r0, near_z[0]), (r1, r1, near_z[1])], r)
            elif name == dim:
                sent = Group([(r, r, m) for m in mates[dim]], at(col, cols, **{dim: pl.ds(0, 3)}))
            else:
                plus, minus = mates[dim][0], mates[dim][2]
                sent = Group([(r, r, plus), (r, r, minus)], at(col, cols, **{dim: pl.ds(0, 2)}))
                yield
                sent.wait_recv()
                r0 = at(col, half, **{dim: pl.ds(around[dim][3], 1)})
                r1 = at(col + half, half, **{dim: pl.ds(around[dim][1], 1)})
                sent = Group([(r0, r0, plus), (r1, r1, minus)], r)
            yield
            sent.wait_recv()
            held[dim] = full[dim]

    def add_into(dst, srcs):
        na, nb, nc = dst.shape[:3]

        def body(i, carry):
            ia, ib, ic = i // (nb * nc), (i // nc) % nb, i % nc
            total = dst[ia, ib, ic].astype(F32)
            for s in srcs:
                total = total + s[ia, ib, ic].astype(F32)
            dst[ia, ib, ic] = total.astype(BF16)
            return carry

        lax.fori_loop(0, na * nb * nc, body, 0)

    def reduce(order, col, cols, bufs):
        left = dict(full)
        half = cols // 2

        def at(first, count, **other):
            s = {**left, **other}
            return terms.at[s["z"], s["x"], s["y"], :, pl.ds(first, count)]

        for name, land in zip(order, bufs):
            dim = name.lower()
            arrived = [land.at[i] for i in range(land.shape[0])]
            if dim == "z":
                out = pl.ds(1 - zl, 1)
                parts = [land.at[0, :, :, :, :, pl.ds(i * half, half)] for i in (0, 1)]
                sent = Group([(at(col + i * half, half, z=out), parts[i], near_z[i]) for i in (0, 1)], land)
            elif name == dim:
                sent = Group(
                    [
                        (at(col, cols, **{dim: pl.ds(around[dim][d], 1)}), land.at[d - 1], mates[dim][d - 1])
                        for d in (1, 2, 3)
                    ],
                    land,
                )
            else:
                plus, minus = mates[dim][0], mates[dim][2]
                to_plus, to_minus = ({dim: pl.ds(around[dim][d], 1)} for d in (1, 3))
                far = {dim: pl.ds(around[dim][2], 1)}
                in0 = land.at[2, :, :, :, :, pl.ds(0, half)]
                in1 = land.at[2, :, :, :, :, pl.ds(half, half)]
                sent = Group([(at(col, half, **far), in0, plus), (at(col + half, half, **far), in1, minus)], land.at[2])
                yield
                sent.wait_recv()
                add_into(at(col, half, **to_plus), [in0])
                add_into(at(col + half, half, **to_minus), [in1])
                sent = Group(
                    [(at(col, cols, **to_plus), land.at[0], plus), (at(col, cols, **to_minus), land.at[1], minus)],
                    land.at[pl.ds(0, 2)],
                )
                arrived = arrived[:2]
            left[dim] = pl.ds(coord[dim], 1)
            yield
            sent.wait_recv()
            add_into(at(col, cols), arrived)
        at_cols = pl.ds(col, cols)
        own = terms.at[zl, x, y, :, at_cols]
        landed = tail_in.at[:, :, at_cols]
        sent = Group([(own, tail_in.at[i, :, at_cols], m) for i, m in enumerate(hmates)], landed)
        yield
        sent.wait_recv()
        total = own[...].astype(F32)
        for i in range(NH - 1):
            total = total + tail_in[i, :, at_cols].astype(F32)
        fin[:, at_cols] = total
        c = send(fin.at[:, at_cols], fin_sib.at[:, at_cols], sib)
        put(fin.at[:, at_cols], wg_ref.at[:, pl.ds(pl.multiple_of(core * HALF + col, 128), cols)])
        yield
        c.wait_recv()
        put(fin_sib.at[:, at_cols], wg_ref.at[:, pl.ds(pl.multiple_of((1 - core) * HALF + col, 128), cols)])

    def terms_of(order, col, cols, bufs):
        width = 256 if cols % 256 == 0 else 128

        def tile(i, carry):
            c = pl.ds(pl.multiple_of(col + i * width, 128), width)
            t = jnp.dot(
                jnp.concatenate([conv_own[...], conv_sib[...]], axis=1), upb[:, c], preferred_element_type=F32
            )
            terms[:, :, :, :, c] = t.astype(BF16).reshape(NZ, NX, NY, 16, width)
            return carry

        lax.fori_loop(0, cols // width, tile, 0)
        yield from reduce(order, col, cols, bufs)

    def project(col, cols):
        width = 512 if cols % 512 == 0 else 256

        def tile(i, carry):
            c = pl.ds(pl.multiple_of(col + i * width, 128), width)
            t = lax.dot_general(
                wbuf[:, :, :, :, c].reshape(CH, width), upb[:, c], (((1,), (1,)), ((), ())), preferred_element_type=F32
            )
            bp_own[...] += t[:, 0:LEN]
            bp_sib[...] += t[:, LEN:]
            return carry

        lax.fori_loop(0, cols // width, tile, 0)

    gathers = [gather(*g) for g in GATHER]
    reduces = [terms_of(*r, red_refs[3 * n : 3 * n + 3]) for n, r in enumerate(REDUCE)]

    def lanes(body):
        def run(i, carry):
            body(i, pl.ds(pl.multiple_of(i * 128, 128), 128))
            return carry

        lax.fori_loop(0, GROUPS, run, 0)

    up_sib = send(up_ref.at[0, :, theirs], upb.at[pl.ds(LEN, LEN)], sib)
    locals_[2].wait()
    for g in gathers:
        next(g)

    locals_[5].wait()
    locals_[6].wait()
    ptile[...] = jnp.zeros((128, 128), F32)
    for j in range(PER):
        ptile[16 * j : 16 * j + 16, 0:16] = modes_in[0]
        ptile[16 * j : 16 * j + 16, 16:32] = modes_in[1]
    par[...] = ptile[...].T[0:32]
    resid, rate = par[0:16], par[16:32]
    row = lax.broadcasted_iota(jnp.int32, (16, 128), 0).astype(F32)
    lane = lax.broadcasted_iota(jnp.int32, (16, 128), 1)
    zero = jnp.zeros((16, 128), F32)

    def rows16(i):
        return slice(16 * i, 16 * i + 16)

    for i in range(SUB + 1):
        e = jnp.exp(-rate * float(i))
        e1[rows16(i)] = e
        e1d[rows16(i)] = e * float(i)
    h, hr = zero, zero
    for m in range(MODES):
        rm, dm = resid[m : m + 1], rate[m : m + 1]
        fwd = rm * jnp.exp(-dm * row)
        re2[rows16(m)] = fwd
        re3[rows16(m)] = rm * jnp.exp(-dm * (16.0 - row))
        h = h + fwd
        hr = hr + rm * jnp.exp(-dm * (15.0 - row))
    hpad[0:16] = zero
    hpad[16:32] = h
    hrev[0:16] = hr
    hrev[16:32] = zero
    upad[:, 0:SUB, :] = jnp.zeros((NSUB, SUB, CH), F32)
    sub_decay = e1[rows16(SUB)]

    def hop(d):
        return jnp.exp(-rate * float(LEN * d))

    moved = (lane // 16).astype(F32) * float(LEN)
    moved_back = ((PER - 1) - lane // 16).astype(F32) * float(LEN)

    def spread(t, last):
        t = jnp.where((lane >= 112) if last else (lane < 16), t, 0.0)
        for d in (16, 32, 64):
            t = t + pltpu.roll(t, d, 1)
        return t

    s_sem, g_sem, p_sem = new_sem(), new_sem(), new_sem()
    own_group = seq // PER

    def give(src, dst, sem, g):
        for j in range(PER):
            n = g * PER + (j + seq) % PER

            @pl.when(n != seq)
            def _():
                round_copy(src, dst, sem, n).start()

    def convolve():
        yield
        round_wait(u_in, recv_sem, u_sem)

        def product_states(g, ln):
            upad[:, SUB : 2 * SUB, ln] = u_in[pl.ds(g * PER, PER)].reshape(128, LEN).T.reshape(NSUB, SUB, 128)
            for s0 in range(0, NSUB, 4):
                a = [zero for _ in range(4)]
                b = [zero for _ in range(4)]
                for i in range(SUB):
                    e, ed = e1[rows16(SUB - i)], e1d[rows16(SUB - i)]
                    for j in range(4):
                        u = upad[s0 + j, SUB + i : SUB + i + 1, ln]
                        a[j] = a[j] + e * u
                        b[j] = b[j] + ed * u
                for j in range(4):
                    ls[rows16(s0 + j), ln] = a[j]
                    lds[rows16(s0 + j), ln] = b[j]
            s, ds_ = zero, zero
            for i in range(NSUB):
                ds_ = sub_decay * (ds_ + float(SUB) * s) + lds[rows16(i), ln]
                s = sub_decay * s + ls[rows16(i), ln]
            heads[0:16, ln] = s
            heads[16:32, ln] = ds_

        lanes(product_states)

        cs, cds = zero, zero
        for g in range(GROUPS):
            ln = slice(128 * g, 128 * g + 128)
            s, ds_ = heads[0:16, ln], heads[16:32, ln]
            for d in (1, 2, 4):
                keep = lane >= 16 * d
                sh = jnp.where(keep, pltpu.roll(s, 16 * d, 1), 0.0)
                shd = jnp.where(keep, pltpu.roll(ds_, 16 * d, 1), 0.0)
                q = hop(d)
                ds_ = ds_ + q * (shd + float(LEN * d) * sh)
                s = s + q * sh
            first = lane >= 16
            q = jnp.exp(-rate * moved)
            heads[0:16, ln] = jnp.where(first, pltpu.roll(s, 16, 1), 0.0) + q * cs
            heads[16:32, ln] = jnp.where(first, pltpu.roll(ds_, 16, 1), 0.0) + q * (cds + moved * cs)
            q = hop(PER)
            cds = spread(ds_, True) + q * (cds + float(LEN * PER) * cs)
            cs = spread(s, True) + q * cs


        def smooth_group(i, carry):
            g = (i + own_group) % GROUPS
            ln = pl.ds(pl.multiple_of(g * 128, 128), 128)
            s, ds_ = heads[0:16, ln], heads[16:32, ln]
            for j in range(NSUB):
                st[rows16(j), ln] = s
                std[rows16(j), ln] = ds_
                ds_ = sub_decay * (ds_ + float(SUB) * s) + lds[rows16(j), ln]
                s = sub_decay * s + ls[rows16(j), ln]
            for s0 in range(0, NSUB, 4):
                acc = [zero for _ in range(4)]
                for k in range(SUB):
                    t, t2 = hpad[16 - k : 32 - k], re2[rows16(k)]
                    for j in range(4):
                        at = 16 * (s0 + j) + k
                        acc[j] = acc[j] + t * upad[s0 + j, SUB + k : SUB + k + 1, ln] + t2 * st[at : at + 1, ln]
                for j in range(4):
                    yb[rows16(s0 + j)] = acc[j]
            s_out[pl.ds(g * PER, PER)] = yb[...].T.reshape(PER, 16, LEN)
            give(s_out, s_in, s_sem, g)
            return carry

        lax.fori_loop(0, GROUPS, smooth_group, 0)
        s_in[seq] = s_out[seq]
        locals_[3].wait()
        locals_[4].wait()
        up_sib.wait_recv()
        yield
        round_wait(s_in, recv_sem, s_sem)
        smooth = s_in[...].reshape(CH, LEN)
        conv_own[...] = (qkv[0].astype(F32) * smooth).astype(BF16)
        conv_sib_copy = send(conv_own, conv_sib, sib)
        yield
        conv_sib_copy.wait_recv()


    def gradients():
        bp_copy = send(bp_sib, bp_in, sib)
        yield
        bp_copy.wait_recv()
        back = (bp_own[...] + bp_in[...]).astype(BF16).astype(F32)
        g_out[...] = (back * qkv[0].astype(F32)).reshape(NSEQ, 16, LEN)
        scatter(g_out, g_in, g_sem)
        grads_out[0] = (back * s_in[...].reshape(CH, LEN)).astype(BF16)
        put(grads_out.at[0], qg_ref.at[0])
        yield
        round_wait(g_in, recv_sem, g_sem)

        def grad_states(g, ln):
            gbuf[:, ln] = g_in[pl.ds(g * PER, PER)].reshape(128, LEN).T
            for s0 in range(0, NSUB, 4):
                a = [zero for _ in range(4)]
                b = [zero for _ in range(4)]
                for i in range(SUB):
                    e, ed = e1[rows16(i)], e1d[rows16(i)]
                    for j in range(4):
                        at = 16 * (s0 + j) + i
                        v = gbuf[at : at + 1, ln]
                        a[j] = a[j] + e * v
                        b[j] = b[j] + ed * v
                for j in range(4):
                    lgs[rows16(s0 + j), ln] = a[j]
                    lgds[rows16(s0 + j), ln] = b[j]
            b = zero
            for i in reversed(range(NSUB)):
                b = sub_decay * b + lgs[rows16(i), ln]
            heads[0:16, ln] = b

        lanes(grad_states)
        cb = zero
        for g in reversed(range(GROUPS)):
            ln = slice(128 * g, 128 * g + 128)
            b = heads[0:16, ln]
            for d in (1, 2, 4):
                b = b + hop(d) * jnp.where(lane < 128 - 16 * d, pltpu.roll(b, 128 - 16 * d, 1), 0.0)
            heads[0:16, ln] = jnp.where(lane < 112, pltpu.roll(b, 112, 1), 0.0) + jnp.exp(-rate * moved_back) * cb
            cb = spread(b, False) + hop(PER) * cb


        def grad_group(i, carry):
            g = (i + own_group) % GROUPS
            ln = pl.ds(pl.multiple_of(g * 128, 128), 128)
            b = heads[0:16, ln]
            for j in reversed(range(NSUB)):
                ls[rows16(j), ln] = b
                b = sub_decay * b + lgs[rows16(j), ln]
            for s0 in range(0, NSUB, 4):
                acc = [zero for _ in range(4)]
                for k in range(SUB):
                    t, t2 = hrev[15 - k : 31 - k], re3[rows16(k)]
                    for j in range(4):
                        at = 16 * (s0 + j) + k
                        acc[j] = acc[j] + t * gbuf[at : at + 1, ln] + t2 * ls[at : at + 1, ln]
                for j in range(4):
                    yb[rows16(s0 + j)] = acc[j]
            p_out[pl.ds(g * PER, PER)] = yb[...].T.reshape(PER, 16, LEN)
            give(p_out, p_in, p_sem, g)
            return carry

        lax.fori_loop(0, GROUPS, grad_group, 0)
        p_in[seq] = p_out[seq]
        yield

        def filter_grads(g, ln):
            a, b = zero, zero
            for i in range(NSUB):
                lg, s = lgs[rows16(i), ln], st[rows16(i), ln]
                a = a + lg * s
                b = b + lgds[rows16(i), ln] * s + lg * std[rows16(i), ln]
            for j in range(SUB):
                acc = zero
                for i in range(NSUB):
                    acc = acc + gbuf[rows16(i), ln] * upad[i, SUB - j : 2 * SUB - j, ln]
                f = jnp.sum(acc, axis=0, keepdims=True)
                a = a + f * e1[rows16(j)]
                b = b + f * e1d[rows16(j)]
            fgs[0, 0:16] += a
            fgs[0, 16:32] += b

        lanes(filter_grads)
        a, b = fgs[0, 0:16], fgs[0, 16:32]
        for d in (16, 32, 64):
            a = a + pltpu.roll(a, d, 1)
            b = b + pltpu.roll(b, d, 1)
        fgz[zh, 0:16] = a
        fgz[zh, 16:32] = -rate * resid * b
        fg_z = Group([(fgz.at[zh], fgz.at[zh], m) for m in hmates], fgz.at[pl.ds(0, NH - 1)])
        yield
        fg_z.wait_recv()
        fgs[0, 0:32] = (fgz[0] + fgz[1]) + (fgz[2] + fgz[3])
        fg_s = send(fgs.at[0, pl.ds(0, 32)], fgs.at[1, pl.ds(0, 32)], sib)

        yield
        round_wait(p_in, recv_sem, p_sem)
        prod_grad = p_in[...].reshape(CH, LEN)
        grads_out[1] = (prod_grad * qkv[2].astype(F32)).astype(BF16)
        put(grads_out.at[1], kg_ref.at[0])
        grads_out[2] = (prod_grad * qkv[1].astype(F32)).astype(BF16)
        put(grads_out.at[2], vg_ref.at[0])
        yield
        fg_s.wait_recv()
        both_fg = (fgs[0] + fgs[1]).T
        modes_out[0] = both_fg[0:16, 0:16]
        modes_out[1] = both_fg[0:16, 16:32]
        put(modes_out.at[0], resg_ref)
        put(modes_out.at[1], rateg_ref)


    chains = {"m": convolve(), "g": gradients()}
    next(chains["m"])
    for what in ORDER:
        if what in chains:
            next(chains[what], None)
        elif what[0] == "M":
            for _ in gathers[int(what[1:])]:
                pass
            project(*GATHER[int(what[1:])][1:])
        else:
            next((gathers if what[0] == "G" else reduces)[int(what[1:])], None)
    for c in results:
        c.wait()
    for c in copies:
        c.wait_send()
    for sem in (u_sem, s_sem, g_sem, p_sem):
        round_wait(u_out, send_sem, sem)


def hand_on(*refs):
    n = len(refs) // 2
    for i in range(n):
        refs[n + i][...] = refs[i][...]


def on_device(query_feat, key_feat, value_feat, upstream, out_weight, residues, decay_rates):
    vm = pl.BlockSpec(memory_space=pltpu.VMEM)
    hbm = pl.BlockSpec(memory_space=pl.ANY)
    slab = (NZ, NX, NY, 16)
    scratch = [
        pltpu.VMEM(slab + (HALF,), BF16),
        pltpu.VMEM(slab + (HALF,), BF16),
        pltpu.VMEM((2 * LEN, HALF), BF16),
        pltpu.VMEM((CH, LEN), F32),
        pltpu.VMEM((CH, LEN), F32),
        pltpu.VMEM((CH, LEN), F32),
        pltpu.VMEM((3, CH, LEN), BF16),
        pltpu.VMEM((128, 128), F32),
        pltpu.VMEM((32, 128), F32),
        pltpu.VMEM((272, 128), F32),
        pltpu.VMEM((272, 128), F32),
        pltpu.VMEM((256, 128), F32),
        pltpu.VMEM((256, 128), F32),
        pltpu.VMEM((32, 128), F32),
        pltpu.VMEM((32, 128), F32),
        pltpu.VMEM((8, NSEQ, 16, LEN), F32),
        pltpu.VMEM((NSUB, 2 * SUB, CH), F32),
        pltpu.VMEM((LEN, CH), F32),
        pltpu.VMEM((LEN, CH), F32),
        pltpu.VMEM((LEN, CH), F32),
        pltpu.VMEM((LEN, CH), F32),
        pltpu.VMEM((LEN, CH), F32),
        pltpu.VMEM((LEN, CH), F32),
        pltpu.VMEM((LEN, CH), F32),
        pltpu.VMEM((32, CH), F32),
        pltpu.VMEM((LEN, 128), F32),
        pltpu.VMEM((CH, LEN), BF16),
        pltpu.VMEM((CH, LEN), BF16),
        pltpu.VMEM((NH, 32, 128), F32),
        pltpu.VMEM((2, 128, 128), F32),
        pltpu.VMEM((NH - 1, 16, HALF), BF16),
        pltpu.VMEM((16, HALF), F32),
        pltpu.VMEM((16, HALF), F32),
        pltpu.VMEM((3, CH, LEN), BF16),
        pltpu.VMEM((2, 16, MODES), F32),
        pltpu.VMEM((2, 16, MODES), F32),
    ]
    scratch += [pltpu.VMEM(s, BF16) for s in reduce_buffers()]
    scratch += [
        pltpu.SemaphoreType.DMA((n_semaphores(),)),
        pltpu.SemaphoreType.DMA((n_semaphores(),)),
        pltpu.SemaphoreType.DMA((7 + 5 + 2 * len(REDUCE),)),
    ]
    out_shape = (
        jax.ShapeDtypeStruct(query_feat.shape, BF16),
        jax.ShapeDtypeStruct(key_feat.shape, BF16),
        jax.ShapeDtypeStruct(value_feat.shape, BF16),
        jax.ShapeDtypeStruct(out_weight.shape, F32),
        jax.ShapeDtypeStruct(residues.shape, F32),
        jax.ShapeDtypeStruct(decay_rates.shape, F32),
    )
    results = pl.pallas_call(
        kernel,
        out_shape=out_shape,
        in_specs=[hbm] * 7,
        out_specs=(hbm,) * 6,
        scratch_shapes=scratch,
        compiler_params=pltpu.CompilerParams(
            collective_id=0, has_side_effects=True, vmem_limit_bytes=56 * 1024 * 1024
        ),
    )(query_feat, key_feat, value_feat, upstream, out_weight, residues, decay_rates)
    return pl.pallas_call(
        hand_on,
        out_shape=out_shape,
        in_specs=[vm] * 6,
        out_specs=(vm,) * 6,
    )(*results)


def solution(mesh):
    return jax.shard_map(
        on_device,
        mesh=mesh,
        in_specs=(
            P("cuts", None, "seq"),
            P("cuts", None, "seq"),
            P("cuts", None, "seq"),
            P("cuts", "seq", None),
            P("seq", None),
            P("seq", None),
            P("seq", None),
        ),
        out_specs=(
            P("cuts", None, "seq"),
            P("cuts", None, "seq"),
            P("cuts", None, "seq"),
            P("seq", None),
            P("seq", None),
            P("seq", None),
        ),
        check_vma=False,
    )
```

```python
import jax
import jax.numpy as jnp
from jax import lax
from jax.experimental import pallas as pl
from jax.experimental.pallas import tpu as pltpu
from jax.sharding import PartitionSpec as P

MESH = pl.DeviceIdType.MESH
F32 = jnp.float32
BF16 = jnp.bfloat16
NX, NY, NZ, NH = 4, 4, 2, 4
NSEQ = NX * NY * NZ
CH, LEN, WIDTH, HALF = 512, 128, 8192, 4096
MODES, SUB, NSUB = 16, 16, 8
GROUPS, PER = 4, 8

GATHER = (
    ("xYz", 0, 256),
    ("yXz", 256, 256),
    ("zxY", 512, 1024),
    ("zyX", 1536, 1024),
    ("xzY", 2560, 768),
    ("yzX", 3328, 768),
)
REDUCE = (
    ("zxy", 0, 512),
    ("zyx", 512, 512),
    ("zxy", 1024, 512),
    ("zyx", 1536, 512),
    ("zxy", 2048, 512),
    ("zyx", 2560, 512),
    ("Xzy", 3072, 512),
    ("Yzx", 3584, 512),
)
ORDER = (
    "G2", "G3", "m", "G0", "G5", "G4", "G1", "G2", "G3", "G5", "G0", "G1", "m", "G4", "m", "R0", "R1", "R2", "R3", "R4", "R5", "R6", "G3", "G2", "R7", "G0", "R0", "G5", "G1", "G4", "R1", "R6", "M2", "R2",
    "M3", "R7", "M4", "R3", "R0", "M5", "R4", "R1", "R6", "R7", "R5", "M0", "M1", "g", "R2", "R3", "R6", "R0", "R7", "g", "R4", "R1", "R5", "R2", "R3", "R6", "R7", "R0", "R0", "g", "g", "R3", "R4", "R1",
    "R5", "R2", "R6", "R3", "R1", "R2", "R7", "R6", "R7", "g", "g", "g", "R4", "R5", "R4", "R5",
)


def reduce_buffers():
    shapes = []
    for order, _, cols in REDUCE:
        size = {"z": NZ, "x": NX, "y": NY}
        for dim in order.lower():
            size[dim] = 1
            shapes.append((1 if dim == "z" else 3, size["z"], size["x"], size["y"], 16, cols))
    return shapes


def n_semaphores():
    steps = sum(len(o) + sum(d.isupper() for d in o) for o, _, _ in GATHER + REDUCE)
    return steps + 2 * len(REDUCE) + 9


def kernel(
    q_ref, k_ref, v_ref, up_ref, w_ref, res_ref, dec_ref,
    qg_ref, kg_ref, vg_ref, wg_ref, resg_ref, rateg_ref,
    wbuf, terms, upb, bp_own, bp_sib, bp_in, qkv, ptile, par,
    e1, e1d, re2, re3, hpad, hrev, a2a, a2b, upad, gbuf,
    ls, lds, st, std, lgs, lgds, heads, yb, conv_own, conv_sib, fgz, fgs, tail_in, fin, fin_sib, grads_out, modes_in, modes_out, *rest,
):
    n_red = len(reduce_buffers())
    red_refs = list(rest[:n_red])
    send_sem, recv_sem, round_sem, local_sem = rest[n_red:]
    cuts, seq = lax.axis_index("cuts"), lax.axis_index("seq")
    core, zh = cuts % 2, cuts // 2
    zl, x, y = seq // 16, (seq // 4) % 4, seq % 4
    z = zh * 2 + zl

    def dev(z_, x_, y_, c_):
        return {"cuts": (z_ // 2) * 2 + c_, "seq": (z_ % 2) * 16 + x_ * 4 + y_}

    xs = [(x + d) % 4 for d in range(4)]
    ys = [(y + d) % 4 for d in range(4)]
    sib = dev(z, x, y, 1 - core)
    zpair = zh * 2 + (1 - zl)
    hmates = [dev(((zh + d) % 4) * 2 + zl, x, y, core) for d in (1, 2, 3)]
    z_plus, z_minus = (z + 1) % 8, (z + 7) % 8
    mates = {
        "x": [dev(z, xs[d], y, core) for d in (1, 2, 3)],
        "y": [dev(z, x, ys[d], core) for d in (1, 2, 3)],
    }
    near_z = (dev(z_plus, x, y, core), dev(z_minus, x, y, core))
    zfar = z_minus + z_plus - zpair
    others = [{"cuts": cuts, "seq": (seq + d) % NSEQ} for d in range(1, NSEQ)]
    partners = [sib] + others + hmates + [dev(zfar, x, y, core)]

    used, used_send = [0], [0]

    def new_sem():
        used[0] += 1
        return used[0] - 1

    class Chain:
        def __init__(self):
            self.sem, self.last = used_send[0], None
            used_send[0] += 1
            chains.append(self)

        def drain(self):
            if self.last is not None:
                self.last.wait_send()
            self.last = None

    chains = []

    class Group:
        def __init__(self, moves, whole, chain=None):
            chain = chain or Chain()
            chain.drain()
            self.sem, self.whole, self.chain = new_sem(), whole, chain
            for src, dst, to in moves:
                pltpu.make_async_remote_copy(
                    src_ref=src, dst_ref=dst, send_sem=send_sem.at[chain.sem], recv_sem=recv_sem.at[self.sem],
                    device_id=to, device_id_type=MESH,
                ).start()
            chain.last = self

        def wait_recv(self):
            pltpu.make_async_copy(self.whole, self.whole, recv_sem.at[self.sem]).wait()

        def wait_send(self):
            pltpu.make_async_copy(self.whole, self.whole, send_sem.at[self.chain.sem]).wait()

    def send(src, dst, to, chain=None):
        return Group([(src, dst, to)], dst, chain)

    results = []

    def put(src, dst):
        c = pltpu.make_async_copy(src, dst, local_sem.at[7 + len(results)])
        c.start()
        results.append(c)

    mine = pl.ds(pl.multiple_of(core * HALF, HALF), HALF)
    theirs = pl.ds(pl.multiple_of((1 - core) * HALF, HALF), HALF)
    locals_ = [
        pltpu.make_async_copy(src, dst, local_sem.at[i])
        for i, (src, dst) in enumerate(
            (
                (k_ref.at[0], qkv.at[1]),
                (v_ref.at[0], qkv.at[2]),
                (w_ref.at[:, mine], wbuf.at[zl, x, y]),
                (q_ref.at[0], qkv.at[0]),
                (up_ref.at[0, :, mine], upb.at[pl.ds(0, LEN)]),
                (res_ref, modes_in.at[0]),
                (dec_ref, modes_in.at[1]),
            )
        )
    ]
    for c in locals_:
        c.start()
    barrier = pltpu.get_barrier_semaphore()
    for d in partners:
        pl.semaphore_signal(barrier, inc=1, device_id=d, device_id_type=MESH)

    locals_[0].wait()
    locals_[1].wait()
    u_out, u_in, g_out, g_in = a2a.at[0], a2a.at[1], a2a.at[2], a2a.at[3]
    s_out, s_in, p_out, p_in = a2b.at[0], a2b.at[1], a2b.at[2], a2b.at[3]
    u_out[...] = (qkv[1].astype(F32) * qkv[2].astype(F32)).reshape(NSEQ, 16, LEN)
    fgs[...] = jnp.zeros((2, 128, 128), F32)
    bp_own[...] = jnp.zeros((CH, LEN), F32)
    bp_sib[...] = jnp.zeros((CH, LEN), F32)
    pl.semaphore_wait(barrier, len(partners))

    def round_copy(src, dst, sem, n):
        return pltpu.make_async_remote_copy(
            src_ref=src.at[n], dst_ref=dst.at[seq], send_sem=round_sem.at[sem], recv_sem=recv_sem.at[sem],
            device_id={"cuts": cuts, "seq": n}, device_id_type=MESH,
        )

    def round_wait(buf, sem_ref, sem):
        part = buf.at[pl.ds(0, NSEQ - 1)]
        pltpu.make_async_copy(part, part, sem_ref.at[sem]).wait()

    def scatter(src, dst, sem):
        for d in range(1, NSEQ):
            round_copy(src, dst, sem, (seq + d) % NSEQ).start()
        dst[seq] = src[seq]

    u_sem, s_sem, g_sem, p_sem = (new_sem() for _ in range(4))
    scatter(u_out, u_in, u_sem)

    coord = {"z": zl, "x": x, "y": y}
    around = {"x": xs, "y": ys}
    full = {"z": pl.ds(0, NZ), "x": pl.ds(0, NX), "y": pl.ds(0, NY)}

    def gather(order, col, cols):
        held = {d: pl.ds(coord[d], 1) for d in "zxy"}
        chain = Chain()
        half = cols // 2

        def at(first, count, **other):
            s = {**held, **other}
            return wbuf.at[s["z"], s["x"], s["y"], :, pl.ds(first, count)]

        for name in order:
            dim = name.lower()
            r, r0, r1 = at(col, cols), at(col, half), at(col + half, half)
            if dim == "z":
                sent = Group([(r0, r0, near_z[0]), (r1, r1, near_z[1])], r, chain)
            elif name == dim:
                sent = Group([(r, r, m) for m in mates[dim]], at(col, cols, **{dim: pl.ds(0, 3)}), chain)
            else:
                plus, minus = mates[dim][0], mates[dim][2]
                sent = Group([(r, r, plus), (r, r, minus)], at(col, cols, **{dim: pl.ds(0, 2)}), chain)
                yield
                sent.wait_recv()
                r0 = at(col, half, **{dim: pl.ds(around[dim][3], 1)})
                r1 = at(col + half, half, **{dim: pl.ds(around[dim][1], 1)})
                sent = Group([(r0, r0, plus), (r1, r1, minus)], r, chain)
            yield
            sent.wait_recv()
            held[dim] = full[dim]

    def add_into(dst, srcs):
        na, nb, nc = dst.shape[:3]

        def body(i, carry):
            ia, ib, ic = i // (nb * nc), (i // nc) % nb, i % nc
            total = dst[ia, ib, ic].astype(F32)
            for s in srcs:
                total = total + s[ia, ib, ic].astype(F32)
            dst[ia, ib, ic] = total.astype(BF16)
            return carry

        lax.fori_loop(0, na * nb * nc, body, 0)

    def reduce(order, col, cols, bufs):
        left = dict(full)
        chain = Chain()
        half = cols // 2

        def at(first, count, **other):
            s = {**left, **other}
            return terms.at[s["z"], s["x"], s["y"], :, pl.ds(first, count)]

        for name, land in zip(order, bufs):
            dim = name.lower()
            arrived = [land.at[i] for i in range(land.shape[0])]
            if dim == "z":
                out = pl.ds(1 - zl, 1)
                parts = [land.at[0, :, :, :, :, pl.ds(i * half, half)] for i in (0, 1)]
                sent = Group([(at(col + i * half, half, z=out), parts[i], near_z[i]) for i in (0, 1)], land, chain)
            elif name == dim:
                sent = Group(
                    [
                        (at(col, cols, **{dim: pl.ds(around[dim][d], 1)}), land.at[d - 1], mates[dim][d - 1])
                        for d in (1, 2, 3)
                    ],
                    land,
                    chain,
                )
            else:
                plus, minus = mates[dim][0], mates[dim][2]
                to_plus, to_minus = ({dim: pl.ds(around[dim][d], 1)} for d in (1, 3))
                far = {dim: pl.ds(around[dim][2], 1)}
                in0 = land.at[2, :, :, :, :, pl.ds(0, half)]
                in1 = land.at[2, :, :, :, :, pl.ds(half, half)]
                sent = Group([(at(col, half, **far), in0, plus), (at(col + half, half, **far), in1, minus)], land.at[2], chain)
                yield
                sent.wait_recv()
                add_into(at(col, half, **to_plus), [in0])
                add_into(at(col + half, half, **to_minus), [in1])
                sent = Group(
                    [(at(col, cols, **to_plus), land.at[0], plus), (at(col, cols, **to_minus), land.at[1], minus)],
                    land.at[pl.ds(0, 2)],
                    chain,
                )
                arrived = arrived[:2]
            left[dim] = pl.ds(coord[dim], 1)
            yield
            sent.wait_recv()
            add_into(at(col, cols), arrived)
        at_cols = pl.ds(col, cols)
        own = terms.at[zl, x, y, :, at_cols]
        landed = tail_in.at[:, :, at_cols]
        sent = Group([(own, tail_in.at[i, :, at_cols], m) for i, m in enumerate(hmates)], landed, chain)
        yield
        sent.wait_recv()
        total = own[...].astype(F32)
        for i in range(NH - 1):
            total = total + tail_in[i, :, at_cols].astype(F32)
        fin[:, at_cols] = total
        c = send(fin.at[:, at_cols], fin_sib.at[:, at_cols], sib, chain)
        put(fin.at[:, at_cols], wg_ref.at[:, pl.ds(pl.multiple_of(core * HALF + col, 128), cols)])
        yield
        c.wait_recv()
        put(fin_sib.at[:, at_cols], wg_ref.at[:, pl.ds(pl.multiple_of((1 - core) * HALF + col, 128), cols)])

    def terms_of(order, col, cols, bufs):
        width = 256 if cols % 256 == 0 else 128

        def tile(i, carry):
            c = pl.ds(pl.multiple_of(col + i * width, 128), width)
            t = jnp.dot(
                jnp.concatenate([conv_own[...], conv_sib[...]], axis=1), upb[:, c], preferred_element_type=F32
            )
            terms[:, :, :, :, c] = t.astype(BF16).reshape(NZ, NX, NY, 16, width)
            return carry

        lax.fori_loop(0, cols // width, tile, 0)
        yield from reduce(order, col, cols, bufs)

    def project(col, cols):
        width = 512 if cols % 512 == 0 else 256

        def tile(i, carry):
            c = pl.ds(pl.multiple_of(col + i * width, 128), width)
            t = lax.dot_general(
                wbuf[:, :, :, :, c].reshape(CH, width), upb[:, c], (((1,), (1,)), ((), ())), preferred_element_type=F32
            )
            bp_own[...] += t[:, 0:LEN]
            bp_sib[...] += t[:, LEN:]
            return carry

        lax.fori_loop(0, cols // width, tile, 0)

    gathers = [gather(*g) for g in GATHER]
    reduces = [terms_of(*r, red_refs[3 * n : 3 * n + 3]) for n, r in enumerate(REDUCE)]

    def lanes(body):
        def run(i, carry):
            body(i, pl.ds(pl.multiple_of(i * 128, 128), 128))
            return carry

        lax.fori_loop(0, GROUPS, run, 0)

    up_sib = send(up_ref.at[0, :, theirs], upb.at[pl.ds(LEN, LEN)], sib)
    locals_[2].wait()
    for g in gathers:
        next(g)

    locals_[5].wait()
    locals_[6].wait()
    ptile[...] = jnp.zeros((128, 128), F32)
    for j in range(PER):
        ptile[16 * j : 16 * j + 16, 0:16] = modes_in[0]
        ptile[16 * j : 16 * j + 16, 16:32] = modes_in[1]
    par[...] = ptile[...].T[0:32]
    resid, rate = par[0:16], par[16:32]
    row = lax.broadcasted_iota(jnp.int32, (16, 128), 0).astype(F32)
    lane = lax.broadcasted_iota(jnp.int32, (16, 128), 1)
    zero = jnp.zeros((16, 128), F32)

    def rows16(i):
        return slice(16 * i, 16 * i + 16)

    for i in range(SUB + 1):
        e = jnp.exp(-rate * float(i))
        e1[rows16(i)] = e
        e1d[rows16(i)] = e * float(i)
    h, hr = zero, zero
    for m in range(MODES):
        rm, dm = resid[m : m + 1], rate[m : m + 1]
        fwd = rm * jnp.exp(-dm * row)
        re2[rows16(m)] = fwd
        re3[rows16(m)] = rm * jnp.exp(-dm * (16.0 - row))
        h = h + fwd
        hr = hr + rm * jnp.exp(-dm * (15.0 - row))
    hpad[0:16] = zero
    hpad[16:32] = h
    hrev[0:16] = hr
    hrev[16:32] = zero
    upad[:, 0:SUB, :] = jnp.zeros((NSUB, SUB, CH), F32)
    sub_decay = e1[rows16(SUB)]

    def hop(d):
        return jnp.exp(-rate * float(LEN * d))

    moved = (lane // 16).astype(F32) * float(LEN)
    moved_back = ((PER - 1) - lane // 16).astype(F32) * float(LEN)

    def spread(t, last):
        t = jnp.where((lane >= 112) if last else (lane < 16), t, 0.0)
        for d in (16, 32, 64):
            t = t + pltpu.roll(t, d, 1)
        return t

    own_group = seq // PER

    def give(src, dst, sem, g):
        for j in range(PER):
            n = g * PER + (j + seq) % PER

            @pl.when(n != seq)
            def _():
                round_copy(src, dst, sem, n).start()

    def convolve():
        yield
        round_wait(u_in, recv_sem, u_sem)

        def product_states(g, ln):
            upad[:, SUB : 2 * SUB, ln] = u_in[pl.ds(g * PER, PER)].reshape(128, LEN).T.reshape(NSUB, SUB, 128)
            for s0 in range(0, NSUB, 4):
                a = [zero for _ in range(4)]
                b = [zero for _ in range(4)]
                for i in range(SUB):
                    e, ed = e1[rows16(SUB - i)], e1d[rows16(SUB - i)]
                    for j in range(4):
                        u = upad[s0 + j, SUB + i : SUB + i + 1, ln]
                        a[j] = a[j] + e * u
                        b[j] = b[j] + ed * u
                for j in range(4):
                    ls[rows16(s0 + j), ln] = a[j]
                    lds[rows16(s0 + j), ln] = b[j]
            s, ds_ = zero, zero
            for i in range(NSUB):
                ds_ = sub_decay * (ds_ + float(SUB) * s) + lds[rows16(i), ln]
                s = sub_decay * s + ls[rows16(i), ln]
            heads[0:16, ln] = s
            heads[16:32, ln] = ds_

        lanes(product_states)

        cs, cds = zero, zero
        for g in range(GROUPS):
            ln = slice(128 * g, 128 * g + 128)
            s, ds_ = heads[0:16, ln], heads[16:32, ln]
            for d in (1, 2, 4):
                keep = lane >= 16 * d
                sh = jnp.where(keep, pltpu.roll(s, 16 * d, 1), 0.0)
                shd = jnp.where(keep, pltpu.roll(ds_, 16 * d, 1), 0.0)
                q = hop(d)
                ds_ = ds_ + q * (shd + float(LEN * d) * sh)
                s = s + q * sh
            first = lane >= 16
            q = jnp.exp(-rate * moved)
            heads[0:16, ln] = jnp.where(first, pltpu.roll(s, 16, 1), 0.0) + q * cs
            heads[16:32, ln] = jnp.where(first, pltpu.roll(ds_, 16, 1), 0.0) + q * (cds + moved * cs)
            q = hop(PER)
            cds = spread(ds_, True) + q * (cds + float(LEN * PER) * cs)
            cs = spread(s, True) + q * cs


        def smooth_group(i, carry):
            g = (i + own_group) % GROUPS
            ln = pl.ds(pl.multiple_of(g * 128, 128), 128)
            s, ds_ = heads[0:16, ln], heads[16:32, ln]
            for j in range(NSUB):
                st[rows16(j), ln] = s
                std[rows16(j), ln] = ds_
                ds_ = sub_decay * (ds_ + float(SUB) * s) + lds[rows16(j), ln]
                s = sub_decay * s + ls[rows16(j), ln]
            for s0 in range(0, NSUB, 4):
                acc = [zero for _ in range(4)]
                for k in range(SUB):
                    t, t2 = hpad[16 - k : 32 - k], re2[rows16(k)]
                    for j in range(4):
                        at = 16 * (s0 + j) + k
                        acc[j] = acc[j] + t * upad[s0 + j, SUB + k : SUB + k + 1, ln] + t2 * st[at : at + 1, ln]
                for j in range(4):
                    yb[rows16(s0 + j)] = acc[j]
            s_out[pl.ds(g * PER, PER)] = yb[...].T.reshape(PER, 16, LEN).astype(BF16)
            give(s_out, s_in, s_sem, g)
            return carry

        lax.fori_loop(0, GROUPS, smooth_group, 0)
        s_in[seq] = s_out[seq]
        locals_[3].wait()
        locals_[4].wait()
        up_sib.wait_recv()
        yield
        round_wait(s_in, recv_sem, s_sem)
        smooth = s_in[...].reshape(CH, LEN).astype(F32)
        conv_own[...] = (qkv[0].astype(F32) * smooth).astype(BF16)
        conv_sib_copy = send(conv_own, conv_sib, sib)
        yield
        conv_sib_copy.wait_recv()


    def gradients():
        bp_copy = send(bp_sib, bp_in, sib)
        yield
        bp_copy.wait_recv()
        back = (bp_own[...] + bp_in[...]).astype(BF16).astype(F32)
        g_out[...] = (back * qkv[0].astype(F32)).reshape(NSEQ, 16, LEN)
        scatter(g_out, g_in, g_sem)
        grads_out[0] = (back * s_in[...].reshape(CH, LEN).astype(F32)).astype(BF16)
        put(grads_out.at[0], qg_ref.at[0])
        yield
        round_wait(g_in, recv_sem, g_sem)

        def grad_states(g, ln):
            gbuf[:, ln] = g_in[pl.ds(g * PER, PER)].reshape(128, LEN).T
            for s0 in range(0, NSUB, 4):
                a = [zero for _ in range(4)]
                b = [zero for _ in range(4)]
                for i in range(SUB):
                    e, ed = e1[rows16(i)], e1d[rows16(i)]
                    for j in range(4):
                        at = 16 * (s0 + j) + i
                        v = gbuf[at : at + 1, ln]
                        a[j] = a[j] + e * v
                        b[j] = b[j] + ed * v
                for j in range(4):
                    lgs[rows16(s0 + j), ln] = a[j]
                    lgds[rows16(s0 + j), ln] = b[j]
            b = zero
            for i in reversed(range(NSUB)):
                b = sub_decay * b + lgs[rows16(i), ln]
            heads[0:16, ln] = b

        lanes(grad_states)
        cb = zero
        for g in reversed(range(GROUPS)):
            ln = slice(128 * g, 128 * g + 128)
            b = heads[0:16, ln]
            for d in (1, 2, 4):
                b = b + hop(d) * jnp.where(lane < 128 - 16 * d, pltpu.roll(b, 128 - 16 * d, 1), 0.0)
            heads[0:16, ln] = jnp.where(lane < 112, pltpu.roll(b, 112, 1), 0.0) + jnp.exp(-rate * moved_back) * cb
            cb = spread(b, False) + hop(PER) * cb


        def grad_group(i, carry):
            g = (i + own_group) % GROUPS
            ln = pl.ds(pl.multiple_of(g * 128, 128), 128)
            b = heads[0:16, ln]
            for j in reversed(range(NSUB)):
                ls[rows16(j), ln] = b
                b = sub_decay * b + lgs[rows16(j), ln]
            for s0 in range(0, NSUB, 4):
                acc = [zero for _ in range(4)]
                for k in range(SUB):
                    t, t2 = hrev[15 - k : 31 - k], re3[rows16(k)]
                    for j in range(4):
                        at = 16 * (s0 + j) + k
                        acc[j] = acc[j] + t * gbuf[at : at + 1, ln] + t2 * ls[at : at + 1, ln]
                for j in range(4):
                    yb[rows16(s0 + j)] = acc[j]
            p_out[pl.ds(g * PER, PER)] = yb[...].T.reshape(PER, 16, LEN).astype(BF16)
            give(p_out, p_in, p_sem, g)
            return carry

        lax.fori_loop(0, GROUPS, grad_group, 0)
        p_in[seq] = p_out[seq]
        yield

        def filter_grads(g, ln):
            a, b = zero, zero
            for i in range(NSUB):
                lg, s = lgs[rows16(i), ln], st[rows16(i), ln]
                a = a + lg * s
                b = b + lgds[rows16(i), ln] * s + lg * std[rows16(i), ln]
            for j in range(SUB):
                acc = zero
                for i in range(NSUB):
                    acc = acc + gbuf[rows16(i), ln] * upad[i, SUB - j : 2 * SUB - j, ln]
                f = jnp.sum(acc, axis=0, keepdims=True)
                a = a + f * e1[rows16(j)]
                b = b + f * e1d[rows16(j)]
            fgs[0, 0:16] += a
            fgs[0, 16:32] += b

        lanes(filter_grads)
        a, b = fgs[0, 0:16], fgs[0, 16:32]
        for d in (16, 32, 64):
            a = a + pltpu.roll(a, d, 1)
            b = b + pltpu.roll(b, d, 1)
        fgz[zh, 0:16] = a
        fgz[zh, 16:32] = -rate * resid * b
        fg_z = Group([(fgz.at[zh], fgz.at[zh], m) for m in hmates], fgz.at[pl.ds(0, NH - 1)])
        yield
        fg_z.wait_recv()
        fgs[0, 0:32] = (fgz[0] + fgz[1]) + (fgz[2] + fgz[3])
        fg_s = send(fgs.at[0, pl.ds(0, 32)], fgs.at[1, pl.ds(0, 32)], sib)

        yield
        round_wait(p_in, recv_sem, p_sem)
        prod_grad = p_in[...].reshape(CH, LEN).astype(F32)
        grads_out[1] = (prod_grad * qkv[2].astype(F32)).astype(BF16)
        put(grads_out.at[1], kg_ref.at[0])
        grads_out[2] = (prod_grad * qkv[1].astype(F32)).astype(BF16)
        put(grads_out.at[2], vg_ref.at[0])
        yield
        fg_s.wait_recv()
        both_fg = (fgs[0] + fgs[1]).T
        modes_out[0] = both_fg[0:16, 0:16]
        modes_out[1] = both_fg[0:16, 16:32]
        put(modes_out.at[0], resg_ref)
        put(modes_out.at[1], rateg_ref)


    tracks = {"m": convolve(), "g": gradients()}
    next(tracks["m"])
    for what in ORDER:
        if what in tracks:
            next(tracks[what], None)
        elif what[0] == "M":
            for _ in gathers[int(what[1:])]:
                pass
            project(*GATHER[int(what[1:])][1:])
        else:
            next((gathers if what[0] == "G" else reduces)[int(what[1:])], None)
    for c in results:
        c.wait()
    for c in chains:
        c.drain()
    for sem, buf in ((u_sem, u_out), (s_sem, s_out), (g_sem, g_out), (p_sem, p_out)):
        round_wait(buf, round_sem, sem)


def hand_on(*refs):
    n = len(refs) // 3
    sems = refs[-1]
    ins = [pltpu.make_async_copy(refs[i], refs[2 * n + i], sems.at[i]) for i in range(n)]
    outs = [pltpu.make_async_copy(refs[2 * n + i], refs[n + i], sems.at[n + i]) for i in range(n)]
    for c in ins:
        c.start()
    for c, d in zip(ins, outs):
        c.wait()
        d.start()
    for d in outs:
        d.wait()


def on_device(query_feat, key_feat, value_feat, upstream, out_weight, residues, decay_rates):
    hbm = pl.BlockSpec(memory_space=pl.ANY)
    slab = (NZ, NX, NY, 16)
    scratch = [
        pltpu.VMEM(slab + (HALF,), BF16),
        pltpu.VMEM(slab + (HALF,), BF16),
        pltpu.VMEM((2 * LEN, HALF), BF16),
        pltpu.VMEM((CH, LEN), F32),
        pltpu.VMEM((CH, LEN), F32),
        pltpu.VMEM((CH, LEN), F32),
        pltpu.VMEM((3, CH, LEN), BF16),
        pltpu.VMEM((128, 128), F32),
        pltpu.VMEM((32, 128), F32),
        pltpu.VMEM((272, 128), F32),
        pltpu.VMEM((272, 128), F32),
        pltpu.VMEM((256, 128), F32),
        pltpu.VMEM((256, 128), F32),
        pltpu.VMEM((32, 128), F32),
        pltpu.VMEM((32, 128), F32),
        pltpu.VMEM((4, NSEQ, 16, LEN), F32),
        pltpu.VMEM((4, NSEQ, 16, LEN), BF16),
        pltpu.VMEM((NSUB, 2 * SUB, CH), F32),
        pltpu.VMEM((LEN, CH), F32),
        pltpu.VMEM((LEN, CH), F32),
        pltpu.VMEM((LEN, CH), F32),
        pltpu.VMEM((LEN, CH), F32),
        pltpu.VMEM((LEN, CH), F32),
        pltpu.VMEM((LEN, CH), F32),
        pltpu.VMEM((LEN, CH), F32),
        pltpu.VMEM((32, CH), F32),
        pltpu.VMEM((LEN, 128), F32),
        pltpu.VMEM((CH, LEN), BF16),
        pltpu.VMEM((CH, LEN), BF16),
        pltpu.VMEM((NH, 32, 128), F32),
        pltpu.VMEM((2, 128, 128), F32),
        pltpu.VMEM((NH - 1, 16, HALF), BF16),
        pltpu.VMEM((16, HALF), F32),
        pltpu.VMEM((16, HALF), F32),
        pltpu.VMEM((3, CH, LEN), BF16),
        pltpu.VMEM((2, 16, MODES), F32),
        pltpu.VMEM((2, 16, MODES), F32),
    ]
    scratch += [pltpu.VMEM(s, BF16) for s in reduce_buffers()]
    scratch += [
        pltpu.SemaphoreType.DMA((len(GATHER) + len(REDUCE) + 5,)),
        pltpu.SemaphoreType.DMA((n_semaphores(),)),
        pltpu.SemaphoreType.DMA((4,)),
        pltpu.SemaphoreType.DMA((7 + 5 + 2 * len(REDUCE),)),
    ]
    out_shape = (
        jax.ShapeDtypeStruct(query_feat.shape, BF16),
        jax.ShapeDtypeStruct(key_feat.shape, BF16),
        jax.ShapeDtypeStruct(value_feat.shape, BF16),
        jax.ShapeDtypeStruct(out_weight.shape, F32),
        jax.ShapeDtypeStruct(residues.shape, F32),
        jax.ShapeDtypeStruct(decay_rates.shape, F32),
    )
    results = pl.pallas_call(
        kernel,
        out_shape=out_shape,
        in_specs=[hbm] * 7,
        out_specs=(hbm,) * 6,
        scratch_shapes=scratch,
        compiler_params=pltpu.CompilerParams(
            collective_id=0, has_side_effects=True, vmem_limit_bytes=56 * 1024 * 1024
        ),
    )(query_feat, key_feat, value_feat, upstream, out_weight, residues, decay_rates)
    return pl.pallas_call(
        hand_on,
        out_shape=out_shape,
        in_specs=[hbm] * 6,
        out_specs=(hbm,) * 6,
        scratch_shapes=[pltpu.VMEM(o.shape, o.dtype) for o in out_shape] + [pltpu.SemaphoreType.DMA((12,))],
    )(*results)


def solution(mesh):
    return jax.shard_map(
        on_device,
        mesh=mesh,
        in_specs=(
            P("cuts", None, "seq"),
            P("cuts", None, "seq"),
            P("cuts", None, "seq"),
            P("cuts", "seq", None),
            P("seq", None),
            P("seq", None),
            P("seq", None),
        ),
        out_specs=(
            P("cuts", None, "seq"),
            P("cuts", None, "seq"),
            P("cuts", None, "seq"),
            P("seq", None),
            P("seq", None),
            P("seq", None),
        ),
        check_vma=False,
    )
```

```python
import jax
import jax.numpy as jnp
from jax import lax
from jax.experimental import pallas as pl
from jax.experimental.pallas import tpu as pltpu
from jax.sharding import PartitionSpec as P

MESH = pl.DeviceIdType.MESH
F32 = jnp.float32
BF16 = jnp.bfloat16
NX, NY, NZ, NH = 4, 4, 2, 4
NSEQ = NX * NY * NZ
CH, LEN, WIDTH, HALF = 512, 128, 8192, 4096
MODES, SUB, NSUB = 16, 16, 8
GROUPS, PER = 4, 8

GATHER = (
    ("xYz", 0, 256),
    ("yXz", 256, 256),
    ("zxY", 512, 1024),
    ("zyX", 1536, 1024),
    ("xzY", 2560, 768),
    ("yzX", 3328, 768),
)
REDUCE = (
    ("zxy", 0, 512),
    ("zyx", 512, 512),
    ("zxy", 1024, 512),
    ("zyx", 1536, 512),
    ("zxy", 2048, 512),
    ("zyx", 2560, 512),
    ("Xzy", 3072, 512),
    ("Yzx", 3584, 512),
)
ORDER = (
    "G2", "G3", "G0", "G1", "m", "G5", "G4", "G1", "G2", "G0", "G3", "G5", "G1", "G4", "m", "m", "R0", "R1", "R2", "M1", "R3", "R4", "G2", "R5", "G0", "G3", "R6", "R7", "R0", "G5", "G4", "R1", "M3", "M2",
    "R2", "R7", "R6", "M4", "R3", "R0", "M5", "R1", "R4", "R7", "R2", "R5", "M0", "g", "R6", "R7", "R3", "g", "R1", "R0", "R2", "R6", "R4", "R5", "R7", "R3", "R6", "g", "R0", "g", "R4", "R1", "R5", "R2",
    "R0", "R7", "R1", "R2", "R3", "R7", "R6", "R3", "R6", "g", "g", "g", "R4", "R5", "R4", "R5",
)


def reduce_buffers():
    shapes = []
    for order, _, cols in REDUCE:
        size = {"z": NZ, "x": NX, "y": NY}
        for dim in order.lower():
            size[dim] = 1
            shapes.append((1 if dim == "z" else 3, size["z"], size["x"], size["y"], 16, cols))
    return shapes


def n_semaphores():
    steps = sum(len(o) + sum(d.isupper() for d in o) for o, _, _ in GATHER + REDUCE)
    return steps + len(REDUCE) + 10


def kernel(
    q_ref, k_ref, v_ref, up_ref, w_ref, res_ref, dec_ref,
    qg_ref, kg_ref, vg_ref, wg_ref, resg_ref, rateg_ref,
    wbuf, terms, upb, bp_own, bp_sib, bp_in, qkv, ptile, par,
    e1, e1d, re2, re3, hpad, hrev, a2a, a2b, upad, gbuf,
    ls, lds, st, std, lgs, lgds, heads, yb, conv_own, conv_sib, fgz, fgs, tail_in, fin, fin_sib, grads_out, modes_in, modes_out, *rest,
):
    n_red = len(reduce_buffers())
    red_refs = list(rest[:n_red])
    send_sem, recv_sem, round_sem, local_sem = rest[n_red:]
    cuts, seq = lax.axis_index("cuts"), lax.axis_index("seq")
    core, zh = cuts % 2, cuts // 2
    zl, x, y = seq // 16, (seq // 4) % 4, seq % 4
    z = zh * 2 + zl

    def dev(z_, x_, y_, c_):
        return {"cuts": (z_ // 2) * 2 + c_, "seq": (z_ % 2) * 16 + x_ * 4 + y_}

    xs = [(x + d) % 4 for d in range(4)]
    ys = [(y + d) % 4 for d in range(4)]
    sib = dev(z, x, y, 1 - core)
    zpair = zh * 2 + (1 - zl)
    hmates = [dev(((zh + d) % 4) * 2 + zl, x, y, core) for d in (1, 2, 3)]
    z_plus, z_minus = (z + 1) % 8, (z + 7) % 8
    mates = {
        "x": [dev(z, xs[d], y, core) for d in (1, 2, 3)],
        "y": [dev(z, x, ys[d], core) for d in (1, 2, 3)],
    }
    near_z = (dev(z_plus, x, y, core), dev(z_minus, x, y, core))
    zfar = z_minus + z_plus - zpair
    others = [{"cuts": cuts, "seq": (seq + d) % NSEQ} for d in range(1, NSEQ)]
    partners = [sib] + others + hmates + [dev(zfar, x, y, core)]

    used, used_send = [0], [0]

    def new_sem():
        used[0] += 1
        return used[0] - 1

    class Chain:
        def __init__(self):
            self.sem, self.last = used_send[0], None
            used_send[0] += 1
            chains.append(self)

        def drain(self):
            if self.last is not None:
                self.last.wait_send()
            self.last = None

    chains = []

    class Group:
        def __init__(self, moves, whole, chain=None):
            chain = chain or Chain()
            chain.drain()
            self.sem, self.whole, self.chain = new_sem(), whole, chain
            for src, dst, to in moves:
                pltpu.make_async_remote_copy(
                    src_ref=src, dst_ref=dst, send_sem=send_sem.at[chain.sem], recv_sem=recv_sem.at[self.sem],
                    device_id=to, device_id_type=MESH,
                ).start()
            chain.last = self

        def wait_recv(self):
            pltpu.make_async_copy(self.whole, self.whole, recv_sem.at[self.sem]).wait()

        def wait_send(self):
            pltpu.make_async_copy(self.whole, self.whole, send_sem.at[self.chain.sem]).wait()

    def send(src, dst, to, chain=None):
        return Group([(src, dst, to)], dst, chain)

    def put(src, dst, which):
        pltpu.make_async_copy(src, dst, local_sem.at[7 + which]).start()

    mine = pl.ds(pl.multiple_of(core * HALF, HALF), HALF)
    theirs = pl.ds(pl.multiple_of((1 - core) * HALF, HALF), HALF)
    locals_ = [
        pltpu.make_async_copy(src, dst, local_sem.at[i])
        for i, (src, dst) in enumerate(
            (
                (k_ref.at[0], qkv.at[1]),
                (v_ref.at[0], qkv.at[2]),
                (w_ref.at[:, mine], wbuf.at[zl, x, y]),
                (q_ref.at[0], qkv.at[0]),
                (up_ref.at[0, :, mine], upb.at[pl.ds(0, LEN)]),
                (res_ref, modes_in.at[0]),
                (dec_ref, modes_in.at[1]),
            )
        )
    ]
    for c in locals_:
        c.start()
    barrier = pltpu.get_barrier_semaphore()
    for d in partners:
        pl.semaphore_signal(barrier, inc=1, device_id=d, device_id_type=MESH)

    locals_[0].wait()
    locals_[1].wait()
    u_out, u_in, g_out, g_in = a2a.at[0], a2a.at[1], a2a.at[2], a2a.at[3]
    s_out, s_in, p_out, p_in = a2a.at[4], a2a.at[5], a2b.at[0], a2b.at[1]
    u_out[...] = (qkv[1].astype(F32) * qkv[2].astype(F32)).reshape(NSEQ, 16, LEN)
    fgs[...] = jnp.zeros((2, 128, 128), F32)
    bp_own[...] = jnp.zeros((CH, LEN), F32)
    bp_sib[...] = jnp.zeros((CH, LEN), F32)
    pl.semaphore_wait(barrier, len(partners))

    def round_copy(src, dst, sem, n):
        return pltpu.make_async_remote_copy(
            src_ref=src.at[n], dst_ref=dst.at[seq], send_sem=round_sem.at[sem], recv_sem=recv_sem.at[sem],
            device_id={"cuts": cuts, "seq": n}, device_id_type=MESH,
        )

    def round_wait(buf, sem_ref, sem):
        part = buf.at[pl.ds(0, NSEQ - 1)]
        pltpu.make_async_copy(part, part, sem_ref.at[sem]).wait()

    def scatter(src, dst, sem):
        for d in range(1, NSEQ):
            round_copy(src, dst, sem, (seq + d) % NSEQ).start()
        dst[seq] = src[seq]

    u_sem, s_sem, g_sem, p_sem, sib_sem = (new_sem() for _ in range(5))
    scatter(u_out, u_in, u_sem)

    coord = {"z": zl, "x": x, "y": y}
    around = {"x": xs, "y": ys}
    full = {"z": pl.ds(0, NZ), "x": pl.ds(0, NX), "y": pl.ds(0, NY)}

    def gather(order, col, cols):
        held = {d: pl.ds(coord[d], 1) for d in "zxy"}
        chain = Chain()
        half = cols // 2

        def at(first, count, **other):
            s = {**held, **other}
            return wbuf.at[s["z"], s["x"], s["y"], :, pl.ds(first, count)]

        for name in order:
            dim = name.lower()
            r, r0, r1 = at(col, cols), at(col, half), at(col + half, half)
            if dim == "z":
                sent = Group([(r0, r0, near_z[0]), (r1, r1, near_z[1])], r, chain)
            elif name == dim:
                sent = Group([(r, r, m) for m in mates[dim]], at(col, cols, **{dim: pl.ds(0, 3)}), chain)
            else:
                plus, minus = mates[dim][0], mates[dim][2]
                sent = Group([(r, r, plus), (r, r, minus)], at(col, cols, **{dim: pl.ds(0, 2)}), chain)
                yield
                sent.wait_recv()
                r0 = at(col, half, **{dim: pl.ds(around[dim][3], 1)})
                r1 = at(col + half, half, **{dim: pl.ds(around[dim][1], 1)})
                sent = Group([(r0, r0, plus), (r1, r1, minus)], r, chain)
            yield
            sent.wait_recv()
            held[dim] = full[dim]

    def add_into(dst, srcs):
        na, nb, nc = dst.shape[:3]

        def body(i, carry):
            ia, ib, ic = i // (nb * nc), (i // nc) % nb, i % nc
            total = dst[ia, ib, ic].astype(F32)
            for s in srcs:
                total = total + s[ia, ib, ic].astype(F32)
            dst[ia, ib, ic] = total.astype(BF16)
            return carry

        lax.fori_loop(0, na * nb * nc, body, 0)

    def reduce(order, col, cols, bufs):
        left = dict(full)
        chain = Chain()
        half = cols // 2

        def at(first, count, **other):
            s = {**left, **other}
            return terms.at[s["z"], s["x"], s["y"], :, pl.ds(first, count)]

        for name, land in zip(order, bufs):
            dim = name.lower()
            arrived = [land.at[i] for i in range(land.shape[0])]
            if dim == "z":
                out = pl.ds(1 - zl, 1)
                parts = [land.at[0, :, :, :, :, pl.ds(i * half, half)] for i in (0, 1)]
                sent = Group([(at(col + i * half, half, z=out), parts[i], near_z[i]) for i in (0, 1)], land, chain)
            elif name == dim:
                sent = Group(
                    [
                        (at(col, cols, **{dim: pl.ds(around[dim][d], 1)}), land.at[d - 1], mates[dim][d - 1])
                        for d in (1, 2, 3)
                    ],
                    land,
                    chain,
                )
            else:
                plus, minus = mates[dim][0], mates[dim][2]
                to_plus, to_minus = ({dim: pl.ds(around[dim][d], 1)} for d in (1, 3))
                far = {dim: pl.ds(around[dim][2], 1)}
                in0 = land.at[2, :, :, :, :, pl.ds(0, half)]
                in1 = land.at[2, :, :, :, :, pl.ds(half, half)]
                sent = Group([(at(col, half, **far), in0, plus), (at(col + half, half, **far), in1, minus)], land.at[2], chain)
                yield
                sent.wait_recv()
                add_into(at(col, half, **to_plus), [in0])
                add_into(at(col + half, half, **to_minus), [in1])
                sent = Group(
                    [(at(col, cols, **to_plus), land.at[0], plus), (at(col, cols, **to_minus), land.at[1], minus)],
                    land.at[pl.ds(0, 2)],
                    chain,
                )
                arrived = arrived[:2]
            left[dim] = pl.ds(coord[dim], 1)
            yield
            sent.wait_recv()
            add_into(at(col, cols), arrived)
        at_cols = pl.ds(col, cols)
        own = terms.at[zl, x, y, :, at_cols]
        landed = tail_in.at[:, :, at_cols]
        sent = Group([(own, tail_in.at[i, :, at_cols], m) for i, m in enumerate(hmates)], landed, chain)
        yield
        sent.wait_recv()
        total = own[...].astype(F32)
        for i in range(NH - 1):
            total = total + tail_in[i, :, at_cols].astype(F32)
        fin[:, at_cols] = total
        put(fin.at[:, at_cols], wg_ref.at[:, pl.ds(pl.multiple_of(core * HALF + col, 128), cols)], 2)
        chain.drain()
        pltpu.make_async_remote_copy(
            src_ref=fin.at[:, at_cols], dst_ref=fin_sib.at[:, at_cols], send_sem=round_sem.at[4],
            recv_sem=recv_sem.at[sib_sem], device_id=sib, device_id_type=MESH,
        ).start()

    def terms_of(order, col, cols, bufs):
        width = 256 if cols % 256 == 0 else 128

        def tile(i, carry):
            c = pl.ds(pl.multiple_of(col + i * width, 128), width)
            t = jnp.dot(
                jnp.concatenate([conv_own[...], conv_sib[...]], axis=1), upb[:, c], preferred_element_type=F32
            )
            terms[:, :, :, :, c] = t.astype(BF16).reshape(NZ, NX, NY, 16, width)
            return carry

        lax.fori_loop(0, cols // width, tile, 0)
        yield from reduce(order, col, cols, bufs)

    def project(col, cols):
        width = 512 if cols % 512 == 0 else 256

        def tile(i, carry):
            c = pl.ds(pl.multiple_of(col + i * width, 128), width)
            t = lax.dot_general(
                wbuf[:, :, :, :, c].reshape(CH, width), upb[:, c], (((1,), (1,)), ((), ())), preferred_element_type=F32
            )
            bp_own[...] += t[:, 0:LEN]
            bp_sib[...] += t[:, LEN:]
            return carry

        lax.fori_loop(0, cols // width, tile, 0)

    gathers = [gather(*g) for g in GATHER]
    reduces = [terms_of(*r, red_refs[3 * n : 3 * n + 3]) for n, r in enumerate(REDUCE)]

    def lanes(body):
        def run(i, carry):
            body(i, pl.ds(pl.multiple_of(i * 128, 128), 128))
            return carry

        lax.fori_loop(0, GROUPS, run, 0)

    up_sib = send(up_ref.at[0, :, theirs], upb.at[pl.ds(LEN, LEN)], sib)
    locals_[2].wait()
    for g in gathers:
        next(g)

    locals_[5].wait()
    locals_[6].wait()
    ptile[...] = jnp.zeros((128, 128), F32)
    for j in range(PER):
        ptile[16 * j : 16 * j + 16, 0:16] = modes_in[0]
        ptile[16 * j : 16 * j + 16, 16:32] = modes_in[1]
    par[...] = ptile[...].T[0:32]
    resid, rate = par[0:16], par[16:32]
    row = lax.broadcasted_iota(jnp.int32, (16, 128), 0).astype(F32)
    lane = lax.broadcasted_iota(jnp.int32, (16, 128), 1)
    zero = jnp.zeros((16, 128), F32)

    def rows16(i):
        return slice(16 * i, 16 * i + 16)

    for i in range(SUB + 1):
        e = jnp.exp(-rate * float(i))
        e1[rows16(i)] = e
        e1d[rows16(i)] = e * float(i)
    h, hr = zero, zero
    for m in range(MODES):
        rm, dm = resid[m : m + 1], rate[m : m + 1]
        fwd = rm * jnp.exp(-dm * row)
        re2[rows16(m)] = fwd
        re3[rows16(m)] = rm * jnp.exp(-dm * (16.0 - row))
        h = h + fwd
        hr = hr + rm * jnp.exp(-dm * (15.0 - row))
    hpad[0:16] = zero
    hpad[16:32] = h
    hrev[0:16] = hr
    hrev[16:32] = zero
    upad[:, 0:SUB, :] = jnp.zeros((NSUB, SUB, CH), F32)
    sub_decay = e1[rows16(SUB)]

    def hop(d):
        return jnp.exp(-rate * float(LEN * d))

    moved = (lane // 16).astype(F32) * float(LEN)
    moved_back = ((PER - 1) - lane // 16).astype(F32) * float(LEN)

    def spread(t, last):
        t = jnp.where((lane >= 112) if last else (lane < 16), t, 0.0)
        for d in (16, 32, 64):
            t = t + pltpu.roll(t, d, 1)
        return t

    own_group = seq // PER

    def give(src, dst, sem, g):
        for j in range(PER):
            n = g * PER + (j + seq) % PER

            @pl.when(n != seq)
            def _():
                round_copy(src, dst, sem, n).start()

    def convolve():
        yield
        round_wait(u_in, recv_sem, u_sem)

        def product_states(g, ln):
            upad[:, SUB : 2 * SUB, ln] = u_in[pl.ds(g * PER, PER)].reshape(128, LEN).T.reshape(NSUB, SUB, 128)
            for s0 in range(0, NSUB, 4):
                a = [zero for _ in range(4)]
                b = [zero for _ in range(4)]
                for i in range(SUB):
                    e, ed = e1[rows16(SUB - i)], e1d[rows16(SUB - i)]
                    for j in range(4):
                        u = upad[s0 + j, SUB + i : SUB + i + 1, ln]
                        a[j] = a[j] + e * u
                        b[j] = b[j] + ed * u
                for j in range(4):
                    ls[rows16(s0 + j), ln] = a[j]
                    lds[rows16(s0 + j), ln] = b[j]
            s, ds_ = zero, zero
            for i in range(NSUB):
                ds_ = sub_decay * (ds_ + float(SUB) * s) + lds[rows16(i), ln]
                s = sub_decay * s + ls[rows16(i), ln]
            heads[0:16, ln] = s
            heads[16:32, ln] = ds_

        lanes(product_states)

        cs, cds = zero, zero
        for g in range(GROUPS):
            ln = slice(128 * g, 128 * g + 128)
            s, ds_ = heads[0:16, ln], heads[16:32, ln]
            for d in (1, 2, 4):
                keep = lane >= 16 * d
                sh = jnp.where(keep, pltpu.roll(s, 16 * d, 1), 0.0)
                shd = jnp.where(keep, pltpu.roll(ds_, 16 * d, 1), 0.0)
                q = hop(d)
                ds_ = ds_ + q * (shd + float(LEN * d) * sh)
                s = s + q * sh
            first = lane >= 16
            q = jnp.exp(-rate * moved)
            heads[0:16, ln] = jnp.where(first, pltpu.roll(s, 16, 1), 0.0) + q * cs
            heads[16:32, ln] = jnp.where(first, pltpu.roll(ds_, 16, 1), 0.0) + q * (cds + moved * cs)
            q = hop(PER)
            cds = spread(ds_, True) + q * (cds + float(LEN * PER) * cs)
            cs = spread(s, True) + q * cs


        def smooth_group(i, carry):
            g = (i + own_group) % GROUPS
            ln = pl.ds(pl.multiple_of(g * 128, 128), 128)
            s, ds_ = heads[0:16, ln], heads[16:32, ln]
            for j in range(NSUB):
                st[rows16(j), ln] = s
                std[rows16(j), ln] = ds_
                ds_ = sub_decay * (ds_ + float(SUB) * s) + lds[rows16(j), ln]
                s = sub_decay * s + ls[rows16(j), ln]
            for s0 in range(0, NSUB, 4):
                acc = [zero for _ in range(4)]
                for k in range(SUB):
                    t, t2 = hpad[16 - k : 32 - k], re2[rows16(k)]
                    for j in range(4):
                        at = 16 * (s0 + j) + k
                        acc[j] = acc[j] + t * upad[s0 + j, SUB + k : SUB + k + 1, ln] + t2 * st[at : at + 1, ln]
                for j in range(4):
                    yb[rows16(s0 + j)] = acc[j]
            s_out[pl.ds(g * PER, PER)] = yb[...].T.reshape(PER, 16, LEN)
            give(s_out, s_in, s_sem, g)
            return carry

        lax.fori_loop(0, GROUPS, smooth_group, 0)
        s_in[seq] = s_out[seq]
        locals_[3].wait()
        locals_[4].wait()
        up_sib.wait_recv()
        yield
        round_wait(s_in, recv_sem, s_sem)
        smooth = s_in[...].reshape(CH, LEN)
        conv_own[...] = (qkv[0].astype(F32) * smooth).astype(BF16)
        conv_sib_copy = send(conv_own, conv_sib, sib)
        yield
        conv_sib_copy.wait_recv()


    def gradients():
        bp_copy = send(bp_sib, bp_in, sib)
        yield
        bp_copy.wait_recv()
        back = (bp_own[...] + bp_in[...]).astype(BF16).astype(F32)
        g_out[...] = (back * qkv[0].astype(F32)).reshape(NSEQ, 16, LEN)
        scatter(g_out, g_in, g_sem)
        grads_out[0] = (back * s_in[...].reshape(CH, LEN)).astype(BF16)
        put(grads_out.at[0], qg_ref.at[0], 0)
        yield
        round_wait(g_in, recv_sem, g_sem)

        def grad_states(g, ln):
            gbuf[:, ln] = g_in[pl.ds(g * PER, PER)].reshape(128, LEN).T
            for s0 in range(0, NSUB, 4):
                a = [zero for _ in range(4)]
                b = [zero for _ in range(4)]
                for i in range(SUB):
                    e, ed = e1[rows16(i)], e1d[rows16(i)]
                    for j in range(4):
                        at = 16 * (s0 + j) + i
                        v = gbuf[at : at + 1, ln]
                        a[j] = a[j] + e * v
                        b[j] = b[j] + ed * v
                for j in range(4):
                    lgs[rows16(s0 + j), ln] = a[j]
                    lgds[rows16(s0 + j), ln] = b[j]
            b = zero
            for i in reversed(range(NSUB)):
                b = sub_decay * b + lgs[rows16(i), ln]
            heads[0:16, ln] = b

        lanes(grad_states)
        cb = zero
        for g in reversed(range(GROUPS)):
            ln = slice(128 * g, 128 * g + 128)
            b = heads[0:16, ln]
            for d in (1, 2, 4):
                b = b + hop(d) * jnp.where(lane < 128 - 16 * d, pltpu.roll(b, 128 - 16 * d, 1), 0.0)
            heads[0:16, ln] = jnp.where(lane < 112, pltpu.roll(b, 112, 1), 0.0) + jnp.exp(-rate * moved_back) * cb
            cb = spread(b, False) + hop(PER) * cb


        def grad_group(i, carry):
            g = (i + own_group) % GROUPS
            ln = pl.ds(pl.multiple_of(g * 128, 128), 128)
            b = heads[0:16, ln]
            for j in reversed(range(NSUB)):
                ls[rows16(j), ln] = b
                b = sub_decay * b + lgs[rows16(j), ln]
            for s0 in range(0, NSUB, 4):
                acc = [zero for _ in range(4)]
                for k in range(SUB):
                    t, t2 = hrev[15 - k : 31 - k], re3[rows16(k)]
                    for j in range(4):
                        at = 16 * (s0 + j) + k
                        acc[j] = acc[j] + t * gbuf[at : at + 1, ln] + t2 * ls[at : at + 1, ln]
                for j in range(4):
                    yb[rows16(s0 + j)] = acc[j]
            p_out[pl.ds(g * PER, PER)] = yb[...].T.reshape(PER, 16, LEN).astype(BF16)
            give(p_out, p_in, p_sem, g)
            return carry

        lax.fori_loop(0, GROUPS, grad_group, 0)
        p_in[seq] = p_out[seq]
        yield

        def filter_grads(g, ln):
            a, b = zero, zero
            for i in range(NSUB):
                lg, s = lgs[rows16(i), ln], st[rows16(i), ln]
                a = a + lg * s
                b = b + lgds[rows16(i), ln] * s + lg * std[rows16(i), ln]
            for j in range(SUB):
                acc = zero
                for i in range(NSUB):
                    acc = acc + gbuf[rows16(i), ln] * upad[i, SUB - j : 2 * SUB - j, ln]
                f = jnp.sum(acc, axis=0, keepdims=True)
                a = a + f * e1[rows16(j)]
                b = b + f * e1d[rows16(j)]
            fgs[0, 0:16] += a
            fgs[0, 16:32] += b

        lanes(filter_grads)
        a, b = fgs[0, 0:16], fgs[0, 16:32]
        for d in (16, 32, 64):
            a = a + pltpu.roll(a, d, 1)
            b = b + pltpu.roll(b, d, 1)
        fgz[zh, 0:16] = a
        fgz[zh, 16:32] = -rate * resid * b
        fg_z = Group([(fgz.at[zh], fgz.at[zh], m) for m in hmates], fgz.at[pl.ds(0, NH - 1)])
        yield
        fg_z.wait_recv()
        fgs[0, 0:32] = (fgz[0] + fgz[1]) + (fgz[2] + fgz[3])
        fg_s = send(fgs.at[0, pl.ds(0, 32)], fgs.at[1, pl.ds(0, 32)], sib)

        yield
        round_wait(p_in, recv_sem, p_sem)
        prod_grad = p_in[...].reshape(CH, LEN).astype(F32)
        grads_out[1] = (prod_grad * qkv[2].astype(F32)).astype(BF16)
        put(grads_out.at[1], kg_ref.at[0], 0)
        grads_out[2] = (prod_grad * qkv[1].astype(F32)).astype(BF16)
        put(grads_out.at[2], vg_ref.at[0], 0)
        yield
        fg_s.wait_recv()
        both_fg = (fgs[0] + fgs[1]).T
        modes_out[0] = both_fg[0:16, 0:16]
        modes_out[1] = both_fg[0:16, 16:32]
        put(modes_out.at[0], resg_ref, 1)
        put(modes_out.at[1], rateg_ref, 1)


    tracks = {"m": convolve(), "g": gradients()}
    next(tracks["m"])
    for what in ORDER:
        if what in tracks:
            next(tracks[what], None)
        elif what[0] == "M":
            for _ in gathers[int(what[1:])]:
                pass
            project(*GATHER[int(what[1:])][1:])
        else:
            next((gathers if what[0] == "G" else reduces)[int(what[1:])], None)
    pltpu.make_async_copy(fin_sib, fin_sib, recv_sem.at[sib_sem]).wait()
    put(fin_sib, wg_ref.at[:, theirs], 2)
    pltpu.make_async_copy(fin, fin, round_sem.at[4]).wait()
    for c in chains:
        c.drain()
    for sem, buf in ((u_sem, u_out), (s_sem, s_out), (g_sem, g_out), (p_sem, p_out)):
        round_wait(buf, round_sem, sem)
    for i, done in enumerate((grads_out, modes_out, wg_ref)):
        pltpu.make_async_copy(done, done, local_sem.at[7 + i]).wait()


def hand_on(*refs):
    n = len(refs) // 3
    sems = refs[-1]
    ins = [pltpu.make_async_copy(refs[i], refs[2 * n + i], sems.at[i]) for i in range(n)]
    outs = [pltpu.make_async_copy(refs[2 * n + i], refs[n + i], sems.at[n + i]) for i in range(n)]
    for c in ins:
        c.start()
    for c, d in zip(ins, outs):
        c.wait()
        d.start()
    for d in outs:
        d.wait()


def on_device(query_feat, key_feat, value_feat, upstream, out_weight, residues, decay_rates):
    hbm = pl.BlockSpec(memory_space=pl.ANY)
    slab = (NZ, NX, NY, 16)
    scratch = [
        pltpu.VMEM(slab + (HALF,), BF16),
        pltpu.VMEM(slab + (HALF,), BF16),
        pltpu.VMEM((2 * LEN, HALF), BF16),
        pltpu.VMEM((CH, LEN), F32),
        pltpu.VMEM((CH, LEN), F32),
        pltpu.VMEM((CH, LEN), F32),
        pltpu.VMEM((3, CH, LEN), BF16),
        pltpu.VMEM((128, 128), F32),
        pltpu.VMEM((32, 128), F32),
        pltpu.VMEM((272, 128), F32),
        pltpu.VMEM((272, 128), F32),
        pltpu.VMEM((256, 128), F32),
        pltpu.VMEM((256, 128), F32),
        pltpu.VMEM((32, 128), F32),
        pltpu.VMEM((32, 128), F32),
        pltpu.VMEM((6, NSEQ, 16, LEN), F32),
        pltpu.VMEM((2, NSEQ, 16, LEN), BF16),
        pltpu.VMEM((NSUB, 2 * SUB, CH), F32),
        pltpu.VMEM((LEN, CH), F32),
        pltpu.VMEM((LEN, CH), F32),
        pltpu.VMEM((LEN, CH), F32),
        pltpu.VMEM((LEN, CH), F32),
        pltpu.VMEM((LEN, CH), F32),
        pltpu.VMEM((LEN, CH), F32),
        pltpu.VMEM((LEN, CH), F32),
        pltpu.VMEM((32, CH), F32),
        pltpu.VMEM((LEN, 128), F32),
        pltpu.VMEM((CH, LEN), BF16),
        pltpu.VMEM((CH, LEN), BF16),
        pltpu.VMEM((NH, 32, 128), F32),
        pltpu.VMEM((2, 128, 128), F32),
        pltpu.VMEM((NH - 1, 16, HALF), BF16),
        pltpu.VMEM((16, HALF), F32),
        pltpu.VMEM((16, HALF), F32),
        pltpu.VMEM((3, CH, LEN), BF16),
        pltpu.VMEM((2, 16, MODES), F32),
        pltpu.VMEM((2, 16, MODES), F32),
    ]
    scratch += [pltpu.VMEM(s, BF16) for s in reduce_buffers()]
    scratch += [
        pltpu.SemaphoreType.DMA((len(GATHER) + len(REDUCE) + 5,)),
        pltpu.SemaphoreType.DMA((n_semaphores(),)),
        pltpu.SemaphoreType.DMA((5,)),
        pltpu.SemaphoreType.DMA((10,)),
    ]
    out_shape = (
        jax.ShapeDtypeStruct(query_feat.shape, BF16),
        jax.ShapeDtypeStruct(key_feat.shape, BF16),
        jax.ShapeDtypeStruct(value_feat.shape, BF16),
        jax.ShapeDtypeStruct(out_weight.shape, F32),
        jax.ShapeDtypeStruct(residues.shape, F32),
        jax.ShapeDtypeStruct(decay_rates.shape, F32),
    )
    results = pl.pallas_call(
        kernel,
        out_shape=out_shape,
        in_specs=[hbm] * 7,
        out_specs=(hbm,) * 6,
        scratch_shapes=scratch,
        compiler_params=pltpu.CompilerParams(
            collective_id=0, has_side_effects=True, vmem_limit_bytes=56 * 1024 * 1024
        ),
    )(query_feat, key_feat, value_feat, upstream, out_weight, residues, decay_rates)
    return pl.pallas_call(
        hand_on,
        out_shape=out_shape,
        in_specs=[hbm] * 6,
        out_specs=(hbm,) * 6,
        scratch_shapes=[pltpu.VMEM(o.shape, o.dtype) for o in out_shape] + [pltpu.SemaphoreType.DMA((12,))],
    )(*results)


def solution(mesh):
    return jax.shard_map(
        on_device,
        mesh=mesh,
        in_specs=(
            P("cuts", None, "seq"),
            P("cuts", None, "seq"),
            P("cuts", None, "seq"),
            P("cuts", "seq", None),
            P("seq", None),
            P("seq", None),
            P("seq", None),
        ),
        out_specs=(
            P("cuts", None, "seq"),
            P("cuts", None, "seq"),
            P("cuts", None, "seq"),
            P("seq", None),
            P("seq", None),
            P("seq", None),
        ),
        check_vma=False,
    )
```

```python
import jax
import jax.numpy as jnp
from jax import lax
from jax.experimental import pallas as pl
from jax.experimental.pallas import tpu as pltpu
from jax.sharding import PartitionSpec as P

MESH = pl.DeviceIdType.MESH
F32 = jnp.float32
BF16 = jnp.bfloat16
NX, NY, NZ, NH = 4, 4, 2, 4
NSEQ = NX * NY * NZ
CH, LEN, WIDTH, HALF = 512, 128, 8192, 4096
MODES, SUB, NSUB = 16, 16, 8
GROUPS, PER = 4, 8

GATHER = (
    ("xYz", 0, 256),
    ("yXz", 256, 256),
    ("zxY", 512, 1024),
    ("zyX", 1536, 1024),
    ("xzY", 2560, 768),
    ("yzX", 3328, 768),
)
REDUCE = (
    ("zxy", 0, 512),
    ("zyx", 512, 512),
    ("zxy", 1024, 512),
    ("zyx", 1536, 512),
    ("zxy", 2048, 512),
    ("zyx", 2560, 512),
    ("Xzy", 3072, 512),
    ("Yzx", 3584, 512),
)
ORDER = (
    "G2", "G3", "G0", "G1", "m", "G5", "G4", "G1", "G2", "G0", "G3", "G5", "G1", "G4", "m", "m", "R0", "R1", "R2", "M1", "R3", "R4", "G2", "R5", "G0", "G3", "R6", "R7", "R0", "G5", "G4", "R1", "M3", "M2",
    "R2", "R7", "R6", "M4", "R3", "R0", "M5", "R1", "R4", "R7", "R2", "R5", "M0", "g", "R6", "R7", "R3", "g", "R1", "R0", "R2", "R6", "R4", "R5", "R7", "R3", "R6", "g", "R0", "g", "R4", "R1", "R5", "R2",
    "R0", "R7", "R1", "R2", "R3", "R7", "R6", "R3", "R6", "g", "g", "g", "R4", "R5", "R4", "R5",
)


def reduce_buffers():
    shapes = []
    for order, _, cols in REDUCE:
        size = {"z": NZ, "x": NX, "y": NY}
        for dim in order.lower():
            size[dim] = 1
            shapes.append((1 if dim == "z" else 3, size["z"], size["x"], size["y"], 16, cols))
    return shapes


def n_semaphores():
    steps = sum(len(o) + sum(d.isupper() for d in o) for o, _, _ in GATHER + REDUCE)
    return steps + len(REDUCE) + 10


def kernel(
    q_ref, k_ref, v_ref, up_ref, w_ref, res_ref, dec_ref,
    qg_ref, kg_ref, vg_ref, wg_ref, resg_ref, rateg_ref,
    wbuf, terms, upb, bp_own, bp_sib, bp_in, qkv, ptile, par,
    e1, e1d, re2, re3, hpad, hrev, a2a, a2b, upad, gbuf,
    ls, lds, st, std, lgs, lgds, heads, yb, conv_own, conv_sib, fgz, fgs, tail_in, fin, fin_sib, grads_out, modes_in, modes_out, *rest,
):
    n_red = len(reduce_buffers())
    red_refs = list(rest[:n_red])
    send_sem, recv_sem, round_sem, local_sem = rest[n_red:]
    cuts, seq = lax.axis_index("cuts"), lax.axis_index("seq")
    core, zh = cuts % 2, cuts // 2
    zl, x, y = seq // 16, (seq // 4) % 4, seq % 4
    z = zh * 2 + zl

    def dev(z_, x_, y_, c_):
        return {"cuts": (z_ // 2) * 2 + c_, "seq": (z_ % 2) * 16 + x_ * 4 + y_}

    xs = [(x + d) % 4 for d in range(4)]
    ys = [(y + d) % 4 for d in range(4)]
    sib = dev(z, x, y, 1 - core)
    zpair = zh * 2 + (1 - zl)
    hmates = [dev(((zh + d) % 4) * 2 + zl, x, y, core) for d in (1, 2, 3)]
    z_plus, z_minus = (z + 1) % 8, (z + 7) % 8
    mates = {
        "x": [dev(z, xs[d], y, core) for d in (1, 2, 3)],
        "y": [dev(z, x, ys[d], core) for d in (1, 2, 3)],
    }
    near_z = (dev(z_plus, x, y, core), dev(z_minus, x, y, core))
    zfar = z_minus + z_plus - zpair
    others = [{"cuts": cuts, "seq": (seq + d) % NSEQ} for d in range(1, NSEQ)]
    partners = [sib] + others + hmates + [dev(zfar, x, y, core)]

    used, used_send = [0], [0]

    def new_sem():
        used[0] += 1
        return used[0] - 1

    class Chain:
        def __init__(self):
            self.sem, self.last = used_send[0], None
            used_send[0] += 1
            chains.append(self)

        def drain(self):
            if self.last is not None:
                self.last.wait_send()
            self.last = None

    chains = []

    class Group:
        def __init__(self, moves, whole, chain=None):
            chain = chain or Chain()
            chain.drain()
            self.sem, self.whole, self.chain = new_sem(), whole, chain
            for src, dst, to in moves:
                pltpu.make_async_remote_copy(
                    src_ref=src, dst_ref=dst, send_sem=send_sem.at[chain.sem], recv_sem=recv_sem.at[self.sem],
                    device_id=to, device_id_type=MESH,
                ).start()
            chain.last = self

        def wait_recv(self):
            pltpu.make_async_copy(self.whole, self.whole, recv_sem.at[self.sem]).wait()

        def wait_send(self):
            pltpu.make_async_copy(self.whole, self.whole, send_sem.at[self.chain.sem]).wait()

    def send(src, dst, to, chain=None):
        return Group([(src, dst, to)], dst, chain)

    def put(src, dst, which):
        pltpu.make_async_copy(src, dst, local_sem.at[7 + which]).start()

    barrier = pltpu.get_barrier_semaphore()
    for d in partners:
        pl.semaphore_signal(barrier, inc=1, device_id=d, device_id_type=MESH)
    mine = pl.ds(pl.multiple_of(core * HALF, HALF), HALF)
    theirs = pl.ds(pl.multiple_of((1 - core) * HALF, HALF), HALF)
    locals_ = [
        pltpu.make_async_copy(src, dst, local_sem.at[i])
        for i, (src, dst) in enumerate(
            (
                (k_ref.at[0], qkv.at[1]),
                (v_ref.at[0], qkv.at[2]),
                (w_ref.at[:, mine], wbuf.at[zl, x, y]),
                (q_ref.at[0], qkv.at[0]),
                (up_ref.at[0, :, mine], upb.at[pl.ds(0, LEN)]),
                (res_ref, modes_in.at[0]),
                (dec_ref, modes_in.at[1]),
            )
        )
    ]
    for c in locals_:
        c.start()

    locals_[0].wait()
    locals_[1].wait()
    u_out, u_in, g_out, g_in = a2a.at[0], a2a.at[1], a2a.at[2], a2a.at[3]
    s_out, s_in, p_out, p_in = a2a.at[4], a2a.at[5], a2b.at[0], a2b.at[1]
    u_out[...] = (qkv[1].astype(F32) * qkv[2].astype(F32)).reshape(NSEQ, 16, LEN)
    fgs[...] = jnp.zeros((2, 128, 128), F32)
    bp_own[...] = jnp.zeros((CH, LEN), F32)
    bp_sib[...] = jnp.zeros((CH, LEN), F32)
    pl.semaphore_wait(barrier, len(partners))

    def round_copy(src, dst, sem, n):
        return pltpu.make_async_remote_copy(
            src_ref=src.at[n], dst_ref=dst.at[seq], send_sem=round_sem.at[sem], recv_sem=recv_sem.at[sem],
            device_id={"cuts": cuts, "seq": n}, device_id_type=MESH,
        )

    def round_wait(buf, sem_ref, sem):
        part = buf.at[pl.ds(0, NSEQ - 1)]
        pltpu.make_async_copy(part, part, sem_ref.at[sem]).wait()

    def scatter(src, dst, sem):
        for d in range(1, NSEQ):
            round_copy(src, dst, sem, (seq + d) % NSEQ).start()
        dst[seq] = src[seq]

    u_sem, s_sem, g_sem, p_sem, sib_sem = (new_sem() for _ in range(5))
    scatter(u_out, u_in, u_sem)

    coord = {"z": zl, "x": x, "y": y}
    around = {"x": xs, "y": ys}
    full = {"z": pl.ds(0, NZ), "x": pl.ds(0, NX), "y": pl.ds(0, NY)}

    def gather(order, col, cols):
        held = {d: pl.ds(coord[d], 1) for d in "zxy"}
        chain = Chain()
        half = cols // 2

        def at(first, count, **other):
            s = {**held, **other}
            return wbuf.at[s["z"], s["x"], s["y"], :, pl.ds(first, count)]

        for name in order:
            dim = name.lower()
            r, r0, r1 = at(col, cols), at(col, half), at(col + half, half)
            if dim == "z":
                sent = Group([(r0, r0, near_z[0]), (r1, r1, near_z[1])], r, chain)
            elif name == dim:
                sent = Group([(r, r, m) for m in mates[dim]], at(col, cols, **{dim: pl.ds(0, 3)}), chain)
            else:
                plus, minus = mates[dim][0], mates[dim][2]
                sent = Group([(r, r, plus), (r, r, minus)], at(col, cols, **{dim: pl.ds(0, 2)}), chain)
                yield
                sent.wait_recv()
                r0 = at(col, half, **{dim: pl.ds(around[dim][3], 1)})
                r1 = at(col + half, half, **{dim: pl.ds(around[dim][1], 1)})
                sent = Group([(r0, r0, plus), (r1, r1, minus)], r, chain)
            yield
            sent.wait_recv()
            held[dim] = full[dim]

    def add_into(dst, srcs):
        na, nb, nc = dst.shape[:3]

        def body(i, carry):
            ia, ib, ic = i // (nb * nc), (i // nc) % nb, i % nc
            total = dst[ia, ib, ic].astype(F32)
            for s in srcs:
                total = total + s[ia, ib, ic].astype(F32)
            dst[ia, ib, ic] = total.astype(BF16)
            return carry

        lax.fori_loop(0, na * nb * nc, body, 0)

    def reduce(order, col, cols, bufs):
        left = dict(full)
        chain = Chain()
        half = cols // 2

        def at(first, count, **other):
            s = {**left, **other}
            return terms.at[s["z"], s["x"], s["y"], :, pl.ds(first, count)]

        for name, land in zip(order, bufs):
            dim = name.lower()
            arrived = [land.at[i] for i in range(land.shape[0])]
            if dim == "z":
                out = pl.ds(1 - zl, 1)
                parts = [land.at[0, :, :, :, :, pl.ds(i * half, half)] for i in (0, 1)]
                sent = Group([(at(col + i * half, half, z=out), parts[i], near_z[i]) for i in (0, 1)], land, chain)
            elif name == dim:
                sent = Group(
                    [
                        (at(col, cols, **{dim: pl.ds(around[dim][d], 1)}), land.at[d - 1], mates[dim][d - 1])
                        for d in (1, 2, 3)
                    ],
                    land,
                    chain,
                )
            else:
                plus, minus = mates[dim][0], mates[dim][2]
                to_plus, to_minus = ({dim: pl.ds(around[dim][d], 1)} for d in (1, 3))
                far = {dim: pl.ds(around[dim][2], 1)}
                in0 = land.at[2, :, :, :, :, pl.ds(0, half)]
                in1 = land.at[2, :, :, :, :, pl.ds(half, half)]
                sent = Group([(at(col, half, **far), in0, plus), (at(col + half, half, **far), in1, minus)], land.at[2], chain)
                yield
                sent.wait_recv()
                add_into(at(col, half, **to_plus), [in0])
                add_into(at(col + half, half, **to_minus), [in1])
                sent = Group(
                    [(at(col, cols, **to_plus), land.at[0], plus), (at(col, cols, **to_minus), land.at[1], minus)],
                    land.at[pl.ds(0, 2)],
                    chain,
                )
                arrived = arrived[:2]
            left[dim] = pl.ds(coord[dim], 1)
            yield
            sent.wait_recv()
            add_into(at(col, cols), arrived)
        at_cols = pl.ds(col, cols)
        own = terms.at[zl, x, y, :, at_cols]
        landed = tail_in.at[:, :, at_cols]
        sent = Group([(own, tail_in.at[i, :, at_cols], m) for i, m in enumerate(hmates)], landed, chain)
        yield
        sent.wait_recv()
        total = own[...].astype(F32)
        for i in range(NH - 1):
            total = total + tail_in[i, :, at_cols].astype(F32)
        fin[:, at_cols] = total
        put(fin.at[:, at_cols], wg_ref.at[:, pl.ds(pl.multiple_of(core * HALF + col, 128), cols)], 2)
        chain.drain()
        pltpu.make_async_remote_copy(
            src_ref=fin.at[:, at_cols], dst_ref=fin_sib.at[:, at_cols], send_sem=round_sem.at[4],
            recv_sem=recv_sem.at[sib_sem], device_id=sib, device_id_type=MESH,
        ).start()

    def terms_of(order, col, cols, bufs):
        width = 256 if cols % 256 == 0 else 128

        def tile(i, carry):
            c = pl.ds(pl.multiple_of(col + i * width, 128), width)
            t = jnp.dot(
                jnp.concatenate([conv_own[...], conv_sib[...]], axis=1), upb[:, c], preferred_element_type=F32
            )
            terms[:, :, :, :, c] = t.astype(BF16).reshape(NZ, NX, NY, 16, width)
            return carry

        lax.fori_loop(0, cols // width, tile, 0)
        yield from reduce(order, col, cols, bufs)

    def project(col, cols):
        width = 512 if cols % 512 == 0 else 256

        def tile(i, carry):
            c = pl.ds(pl.multiple_of(col + i * width, 128), width)
            t = lax.dot_general(
                wbuf[:, :, :, :, c].reshape(CH, width), upb[:, c], (((1,), (1,)), ((), ())), preferred_element_type=F32
            )
            bp_own[...] += t[:, 0:LEN]
            bp_sib[...] += t[:, LEN:]
            return carry

        lax.fori_loop(0, cols // width, tile, 0)

    gathers = [gather(*g) for g in GATHER]
    reduces = [terms_of(*r, red_refs[3 * n : 3 * n + 3]) for n, r in enumerate(REDUCE)]

    def lanes(body):
        def run(i, carry):
            body(i, pl.ds(pl.multiple_of(i * 128, 128), 128))
            return carry

        lax.fori_loop(0, GROUPS, run, 0)

    up_sib = send(up_ref.at[0, :, theirs], upb.at[pl.ds(LEN, LEN)], sib)
    locals_[2].wait()
    for g in gathers:
        next(g)

    locals_[5].wait()
    locals_[6].wait()
    ptile[...] = jnp.zeros((128, 128), F32)
    for j in range(PER):
        ptile[16 * j : 16 * j + 16, 0:16] = modes_in[0]
        ptile[16 * j : 16 * j + 16, 16:32] = modes_in[1]
    par[...] = ptile[...].T[0:32]
    resid, rate = par[0:16], par[16:32]
    row = lax.broadcasted_iota(jnp.int32, (16, 128), 0).astype(F32)
    lane = lax.broadcasted_iota(jnp.int32, (16, 128), 1)
    zero = jnp.zeros((16, 128), F32)

    def rows16(i):
        return slice(16 * i, 16 * i + 16)

    for i in range(SUB + 1):
        e = jnp.exp(-rate * float(i))
        e1[rows16(i)] = e
        e1d[rows16(i)] = e * float(i)
    h, hr = zero, zero
    for m in range(MODES):
        rm, dm = resid[m : m + 1], rate[m : m + 1]
        fwd = rm * jnp.exp(-dm * row)
        re2[rows16(m)] = fwd
        re3[rows16(m)] = rm * jnp.exp(-dm * (16.0 - row))
        h = h + fwd
        hr = hr + rm * jnp.exp(-dm * (15.0 - row))
    hpad[0:16] = zero
    hpad[16:32] = h
    hrev[0:16] = hr
    hrev[16:32] = zero
    upad[:, 0:SUB, :] = jnp.zeros((NSUB, SUB, CH), F32)
    sub_decay = e1[rows16(SUB)]

    def hop(d):
        return jnp.exp(-rate * float(LEN * d))

    moved = (lane // 16).astype(F32) * float(LEN)
    moved_back = ((PER - 1) - lane // 16).astype(F32) * float(LEN)

    def spread(t, last):
        t = jnp.where((lane >= 112) if last else (lane < 16), t, 0.0)
        for d in (16, 32, 64):
            t = t + pltpu.roll(t, d, 1)
        return t

    own_group = seq // PER

    def give(src, dst, sem, g):
        for j in range(PER):
            n = g * PER + (j + seq) % PER

            @pl.when(n != seq)
            def _():
                round_copy(src, dst, sem, n).start()

    def convolve():
        yield
        round_wait(u_in, recv_sem, u_sem)

        def product_states(g, ln):
            upad[:, SUB : 2 * SUB, ln] = u_in[pl.ds(g * PER, PER)].reshape(128, LEN).T.reshape(NSUB, SUB, 128)
            for s0 in range(0, NSUB, 4):
                a = [zero for _ in range(4)]
                b = [zero for _ in range(4)]
                for i in range(SUB):
                    e, ed = e1[rows16(SUB - i)], e1d[rows16(SUB - i)]
                    for j in range(4):
                        u = upad[s0 + j, SUB + i : SUB + i + 1, ln]
                        a[j] = a[j] + e * u
                        b[j] = b[j] + ed * u
                for j in range(4):
                    ls[rows16(s0 + j), ln] = a[j]
                    lds[rows16(s0 + j), ln] = b[j]
            s, ds_ = zero, zero
            for i in range(NSUB):
                ds_ = sub_decay * (ds_ + float(SUB) * s) + lds[rows16(i), ln]
                s = sub_decay * s + ls[rows16(i), ln]
            heads[0:16, ln] = s
            heads[16:32, ln] = ds_

        lanes(product_states)

        cs, cds = zero, zero
        for g in range(GROUPS):
            ln = slice(128 * g, 128 * g + 128)
            s, ds_ = heads[0:16, ln], heads[16:32, ln]
            for d in (1, 2, 4):
                keep = lane >= 16 * d
                sh = jnp.where(keep, pltpu.roll(s, 16 * d, 1), 0.0)
                shd = jnp.where(keep, pltpu.roll(ds_, 16 * d, 1), 0.0)
                q = hop(d)
                ds_ = ds_ + q * (shd + float(LEN * d) * sh)
                s = s + q * sh
            first = lane >= 16
            q = jnp.exp(-rate * moved)
            heads[0:16, ln] = jnp.where(first, pltpu.roll(s, 16, 1), 0.0) + q * cs
            heads[16:32, ln] = jnp.where(first, pltpu.roll(ds_, 16, 1), 0.0) + q * (cds + moved * cs)
            q = hop(PER)
            cds = spread(ds_, True) + q * (cds + float(LEN * PER) * cs)
            cs = spread(s, True) + q * cs


        def smooth_group(i, carry):
            g = (i + own_group) % GROUPS
            ln = pl.ds(pl.multiple_of(g * 128, 128), 128)
            s, ds_ = heads[0:16, ln], heads[16:32, ln]
            for j in range(NSUB):
                st[rows16(j), ln] = s
                std[rows16(j), ln] = ds_
                ds_ = sub_decay * (ds_ + float(SUB) * s) + lds[rows16(j), ln]
                s = sub_decay * s + ls[rows16(j), ln]
            for s0 in range(0, NSUB, 4):
                acc = [zero for _ in range(4)]
                for k in range(SUB):
                    t, t2 = hpad[16 - k : 32 - k], re2[rows16(k)]
                    for j in range(4):
                        at = 16 * (s0 + j) + k
                        acc[j] = acc[j] + t * upad[s0 + j, SUB + k : SUB + k + 1, ln] + t2 * st[at : at + 1, ln]
                for j in range(4):
                    yb[rows16(s0 + j)] = acc[j]
            s_out[pl.ds(g * PER, PER)] = yb[...].T.reshape(PER, 16, LEN)
            give(s_out, s_in, s_sem, g)
            return carry

        lax.fori_loop(0, GROUPS, smooth_group, 0)
        s_in[seq] = s_out[seq]
        locals_[3].wait()
        locals_[4].wait()
        up_sib.wait_recv()
        yield
        round_wait(s_in, recv_sem, s_sem)
        smooth = s_in[...].reshape(CH, LEN)
        conv_own[...] = (qkv[0].astype(F32) * smooth).astype(BF16)
        conv_sib_copy = send(conv_own, conv_sib, sib)
        yield
        conv_sib_copy.wait_recv()


    def gradients():
        bp_copy = send(bp_sib, bp_in, sib)
        yield
        bp_copy.wait_recv()
        back = (bp_own[...] + bp_in[...]).astype(BF16).astype(F32)
        g_out[...] = (back * qkv[0].astype(F32)).reshape(NSEQ, 16, LEN)
        scatter(g_out, g_in, g_sem)
        grads_out[0] = (back * s_in[...].reshape(CH, LEN)).astype(BF16)
        put(grads_out.at[0], qg_ref.at[0], 0)
        yield
        round_wait(g_in, recv_sem, g_sem)

        def grad_states(g, ln):
            gbuf[:, ln] = g_in[pl.ds(g * PER, PER)].reshape(128, LEN).T
            for s0 in range(0, NSUB, 4):
                a = [zero for _ in range(4)]
                b = [zero for _ in range(4)]
                for i in range(SUB):
                    e, ed = e1[rows16(i)], e1d[rows16(i)]
                    for j in range(4):
                        at = 16 * (s0 + j) + i
                        v = gbuf[at : at + 1, ln]
                        a[j] = a[j] + e * v
                        b[j] = b[j] + ed * v
                for j in range(4):
                    lgs[rows16(s0 + j), ln] = a[j]
                    lgds[rows16(s0 + j), ln] = b[j]
            b = zero
            for i in reversed(range(NSUB)):
                b = sub_decay * b + lgs[rows16(i), ln]
            heads[0:16, ln] = b

        lanes(grad_states)
        cb = zero
        for g in reversed(range(GROUPS)):
            ln = slice(128 * g, 128 * g + 128)
            b = heads[0:16, ln]
            for d in (1, 2, 4):
                b = b + hop(d) * jnp.where(lane < 128 - 16 * d, pltpu.roll(b, 128 - 16 * d, 1), 0.0)
            heads[0:16, ln] = jnp.where(lane < 112, pltpu.roll(b, 112, 1), 0.0) + jnp.exp(-rate * moved_back) * cb
            cb = spread(b, False) + hop(PER) * cb


        def grad_group(i, carry):
            g = (i + own_group) % GROUPS
            ln = pl.ds(pl.multiple_of(g * 128, 128), 128)
            b = heads[0:16, ln]
            for j in reversed(range(NSUB)):
                ls[rows16(j), ln] = b
                b = sub_decay * b + lgs[rows16(j), ln]
            for s0 in range(0, NSUB, 4):
                acc = [zero for _ in range(4)]
                for k in range(SUB):
                    t, t2 = hrev[15 - k : 31 - k], re3[rows16(k)]
                    for j in range(4):
                        at = 16 * (s0 + j) + k
                        acc[j] = acc[j] + t * gbuf[at : at + 1, ln] + t2 * ls[at : at + 1, ln]
                for j in range(4):
                    yb[rows16(s0 + j)] = acc[j]
            p_out[pl.ds(g * PER, PER)] = yb[...].T.reshape(PER, 16, LEN).astype(BF16)
            give(p_out, p_in, p_sem, g)
            return carry

        lax.fori_loop(0, GROUPS, grad_group, 0)
        p_in[seq] = p_out[seq]
        yield

        def filter_grads(g, ln):
            a, b = zero, zero
            for i in range(NSUB):
                lg, s = lgs[rows16(i), ln], st[rows16(i), ln]
                a = a + lg * s
                b = b + lgds[rows16(i), ln] * s + lg * std[rows16(i), ln]
            for j in range(SUB):
                acc = zero
                for i in range(NSUB):
                    acc = acc + gbuf[rows16(i), ln] * upad[i, SUB - j : 2 * SUB - j, ln]
                f = jnp.sum(acc, axis=0, keepdims=True)
                a = a + f * e1[rows16(j)]
                b = b + f * e1d[rows16(j)]
            fgs[0, 0:16] += a
            fgs[0, 16:32] += b

        lanes(filter_grads)
        a, b = fgs[0, 0:16], fgs[0, 16:32]
        for d in (16, 32, 64):
            a = a + pltpu.roll(a, d, 1)
            b = b + pltpu.roll(b, d, 1)
        fgz[zh, 0:16] = a
        fgz[zh, 16:32] = -rate * resid * b
        fg_z = Group([(fgz.at[zh], fgz.at[zh], m) for m in hmates], fgz.at[pl.ds(0, NH - 1)])
        yield
        fg_z.wait_recv()
        fgs[0, 0:32] = (fgz[0] + fgz[1]) + (fgz[2] + fgz[3])
        fg_s = send(fgs.at[0, pl.ds(0, 32)], fgs.at[1, pl.ds(0, 32)], sib)

        yield
        round_wait(p_in, recv_sem, p_sem)
        prod_grad = p_in[...].reshape(CH, LEN).astype(F32)
        grads_out[1] = (prod_grad * qkv[2].astype(F32)).astype(BF16)
        put(grads_out.at[1], kg_ref.at[0], 0)
        grads_out[2] = (prod_grad * qkv[1].astype(F32)).astype(BF16)
        put(grads_out.at[2], vg_ref.at[0], 0)
        yield
        fg_s.wait_recv()
        both_fg = (fgs[0] + fgs[1]).T
        modes_out[0] = both_fg[0:16, 0:16]
        modes_out[1] = both_fg[0:16, 16:32]
        put(modes_out.at[0], resg_ref, 1)
        put(modes_out.at[1], rateg_ref, 1)


    tracks = {"m": convolve(), "g": gradients()}
    next(tracks["m"])
    for what in ORDER:
        if what in tracks:
            next(tracks[what], None)
        elif what[0] == "M":
            for _ in gathers[int(what[1:])]:
                pass
            project(*GATHER[int(what[1:])][1:])
        else:
            next((gathers if what[0] == "G" else reduces)[int(what[1:])], None)
    pltpu.make_async_copy(fin_sib, fin_sib, recv_sem.at[sib_sem]).wait()
    put(fin_sib, wg_ref.at[:, theirs], 2)
    pltpu.make_async_copy(fin, fin, round_sem.at[4]).wait()
    for c in chains:
        c.drain()
    for sem, buf in ((u_sem, u_out), (s_sem, s_out), (g_sem, g_out), (p_sem, p_out)):
        round_wait(buf, round_sem, sem)
    for i, done in enumerate((grads_out, modes_out, wg_ref)):
        pltpu.make_async_copy(done, done, local_sem.at[7 + i]).wait()


def hand_on(*refs):
    n = len(refs) // 3
    sems = refs[-1]
    ins = [pltpu.make_async_copy(refs[i], refs[2 * n + i], sems.at[i]) for i in range(n)]
    outs = [pltpu.make_async_copy(refs[2 * n + i], refs[n + i], sems.at[n + i]) for i in range(n)]
    for c in ins:
        c.start()
    for c, d in zip(ins, outs):
        c.wait()
        d.start()
    for d in outs:
        d.wait()


def on_device(query_feat, key_feat, value_feat, upstream, out_weight, residues, decay_rates):
    hbm = pl.BlockSpec(memory_space=pl.ANY)
    slab = (NZ, NX, NY, 16)
    scratch = [
        pltpu.VMEM(slab + (HALF,), BF16),
        pltpu.VMEM(slab + (HALF,), BF16),
        pltpu.VMEM((2 * LEN, HALF), BF16),
        pltpu.VMEM((CH, LEN), F32),
        pltpu.VMEM((CH, LEN), F32),
        pltpu.VMEM((CH, LEN), F32),
        pltpu.VMEM((3, CH, LEN), BF16),
        pltpu.VMEM((128, 128), F32),
        pltpu.VMEM((32, 128), F32),
        pltpu.VMEM((272, 128), F32),
        pltpu.VMEM((272, 128), F32),
        pltpu.VMEM((256, 128), F32),
        pltpu.VMEM((256, 128), F32),
        pltpu.VMEM((32, 128), F32),
        pltpu.VMEM((32, 128), F32),
        pltpu.VMEM((6, NSEQ, 16, LEN), F32),
        pltpu.VMEM((2, NSEQ, 16, LEN), BF16),
        pltpu.VMEM((NSUB, 2 * SUB, CH), F32),
        pltpu.VMEM((LEN, CH), F32),
        pltpu.VMEM((LEN, CH), F32),
        pltpu.VMEM((LEN, CH), F32),
        pltpu.VMEM((LEN, CH), F32),
        pltpu.VMEM((LEN, CH), F32),
        pltpu.VMEM((LEN, CH), F32),
        pltpu.VMEM((LEN, CH), F32),
        pltpu.VMEM((32, CH), F32),
        pltpu.VMEM((LEN, 128), F32),
        pltpu.VMEM((CH, LEN), BF16),
        pltpu.VMEM((CH, LEN), BF16),
        pltpu.VMEM((NH, 32, 128), F32),
        pltpu.VMEM((2, 128, 128), F32),
        pltpu.VMEM((NH - 1, 16, HALF), BF16),
        pltpu.VMEM((16, HALF), F32),
        pltpu.VMEM((16, HALF), F32),
        pltpu.VMEM((3, CH, LEN), BF16),
        pltpu.VMEM((2, 16, MODES), F32),
        pltpu.VMEM((2, 16, MODES), F32),
    ]
    scratch += [pltpu.VMEM(s, BF16) for s in reduce_buffers()]
    scratch += [
        pltpu.SemaphoreType.DMA((len(GATHER) + len(REDUCE) + 5,)),
        pltpu.SemaphoreType.DMA((n_semaphores(),)),
        pltpu.SemaphoreType.DMA((5,)),
        pltpu.SemaphoreType.DMA((10,)),
    ]
    out_shape = (
        jax.ShapeDtypeStruct(query_feat.shape, BF16),
        jax.ShapeDtypeStruct(key_feat.shape, BF16),
        jax.ShapeDtypeStruct(value_feat.shape, BF16),
        jax.ShapeDtypeStruct(out_weight.shape, F32),
        jax.ShapeDtypeStruct(residues.shape, F32),
        jax.ShapeDtypeStruct(decay_rates.shape, F32),
    )
    results = pl.pallas_call(
        kernel,
        out_shape=out_shape,
        in_specs=[hbm] * 7,
        out_specs=(hbm,) * 6,
        scratch_shapes=scratch,
        compiler_params=pltpu.CompilerParams(
            collective_id=0, has_side_effects=True, vmem_limit_bytes=56 * 1024 * 1024
        ),
    )(query_feat, key_feat, value_feat, upstream, out_weight, residues, decay_rates)
    return pl.pallas_call(
        hand_on,
        out_shape=out_shape,
        in_specs=[hbm] * 6,
        out_specs=(hbm,) * 6,
        scratch_shapes=[pltpu.VMEM(o.shape, o.dtype) for o in out_shape] + [pltpu.SemaphoreType.DMA((12,))],
    )(*results)


def solution(mesh):
    return jax.shard_map(
        on_device,
        mesh=mesh,
        in_specs=(
            P("cuts", None, "seq"),
            P("cuts", None, "seq"),
            P("cuts", None, "seq"),
            P("cuts", "seq", None),
            P("seq", None),
            P("seq", None),
            P("seq", None),
        ),
        out_specs=(
            P("cuts", None, "seq"),
            P("cuts", None, "seq"),
            P("cuts", None, "seq"),
            P("seq", None),
            P("seq", None),
            P("seq", None),
        ),
        check_vma=False,
    )
```
